256 devices in a mesh: lat: 16 (over y_hi, z), lon: 16 (over y_lo, x, core).
Axes of the slice: x: 4, y: 4 (y_hi: 2, y_lo: 2; y = y_hi * 2 + y_lo), z: 8, core: 2. Of those that a mesh axis runs over, the one named last changes fastest.
Arguments:
- tokens: bfloat16 [192, 768, 512], P('lat', 'lon'), may hold values from -6 to 6
- gain_attn: float32 [512], replicated, may hold values from 0.1 to 1.9
- w_qkv: bfloat16 [512, 1536], replicated, may hold values from -4 to 4
- w_proj: bfloat16 [512, 512], replicated, may hold values from -0.25 to 0.25
- gain_merge: float32 [2048], replicated, may hold values from 0.1 to 1.9
- w_merge: bfloat16 [2048, 1024], replicated, may hold values from -0.125 to 0.125
- g_merged: bfloat16 [96, 384, 1024], P('lat', 'lon'), may hold values from -60 to 60
Outputs:
- merged: bfloat16 [96, 384, 1024], P('lat', 'lon')
- grad_tokens: bfloat16 [192, 768, 512], P('lat', 'lon')
- grad_weights: float32 [512, 2048], P('lat', 'lon')
The draws below stay inside these ranges and needn't reach their ends.
All inputs are finite; a program needn't handle non-finite values.
Results may differ from the reference program's by a relative error of at most 0.03.
Values may be sent and summed in bfloat16 or wider, within the bound.
No kernel may reach another device: no remote copies, remote signals or barrier semaphores. Data moves between devices by JAX's collectives and lax.ppermute only.
A program may use at most 64 MiB of HBM per device.

```python
import jax
import jax.numpy as jnp
from jax import lax

D = 512
HEADS = 8
WIN_LAT = 6
WIN_LON = 12
SHIFT_LAT = 3
SHIFT_LON = 6
H_GRID = 192
W_GRID = 768


def draw_w_qkv(key, part):
    key = jax.random.fold_in(key, 11)
    keys = jax.random.split(key, 1)
    whole = jax.random.normal(keys[0], (D, 3 * D), jnp.float32) * D ** (-0.5)
    return jnp.clip(whole, -4.0, 4.0).astype(jnp.bfloat16)


def draw_g_merged(key, part):
    key = jax.random.fold_in(key, 23)
    keys = jax.random.split(key, 1)
    rows = H_GRID // 2
    cols = W_GRID // 2
    lat_rise = 3.0 ** (jnp.arange(rows, dtype=jnp.float32) / rows)
    lon_rise = 3.0 ** (jnp.arange(cols, dtype=jnp.float32) / cols)
    scale = lat_rise[:, None, None] * lon_rise[None, :, None]
    noise = jnp.clip(jax.random.normal(keys[0], (rows, cols, 2 * D), jnp.float32), -6.0, 6.0)
    return jnp.clip(noise * scale, -60.0, 60.0).astype(jnp.bfloat16)


def block_scale(rng, shape, pieces, low, top_value):
    level = 1.0
    for dim, blocks in pieces:
        draws = jax.random.uniform(jax.random.fold_in(jax.random.fold_in(rng, 6), dim), (blocks,), jnp.float32, low / len(pieces), top_value / len(pieces))
        level = level * jnp.repeat(jnp.exp(draws), shape[dim] // blocks).reshape((-1,) + (1,) * (len(shape) - 1 - dim))
    return level


def normal_values(own_key, dims, scale, most, cuts=(), held_as=jnp.bfloat16):
    result = scale * jax.random.normal(own_key, dims, jnp.float32)
    if cuts:
        result = result * block_scale(own_key, dims, cuts, -0.22, 0.18)
    return jnp.clip(result, -most, most).astype(held_as)


def setup_inputs(seed: int = 0) -> dict:
    arg_keys = jax.random.split(jax.random.key(seed), 8)
    return {
        "tokens": normal_values(arg_keys[0], (H_GRID, W_GRID, D), 1.0, 6.0, ((0, 16), (1, 16))),
        "gain_attn": jnp.clip(1.0 + 0.18 * jax.random.normal(arg_keys[1], (D,), jnp.float32), 0.1, 1.9),
        "w_qkv": draw_w_qkv(jax.random.fold_in(arg_keys[7], 71), 0),
        "w_proj": normal_values(arg_keys[3], (D, D), D ** -0.5, 0.25),
        "gain_merge": jnp.clip(1.0 + 0.18 * jax.random.normal(arg_keys[4], (4 * D,), jnp.float32), 0.1, 1.9),
        "w_merge": normal_values(arg_keys[5], (4 * D, 2 * D), (4 * D) ** -0.5, 0.125),
        "g_merged": draw_g_merged(jax.random.fold_in(arg_keys[7], 71), 0),
    }


EPS = 1e-05

def normalize(values, gain):
    center = lax.optimization_barrier(jnp.mean(values, axis=-1, keepdims=True))
    centred = values - center
    spread = lax.optimization_barrier(jnp.mean(centred * centred, axis=-1, keepdims=True))
    return centred * lax.rsqrt(spread + EPS) * gain.astype(jnp.float32)

def to_windows(field):
    rows, cols, width = field.shape
    blocks = field.reshape(rows // WIN_LAT, WIN_LAT, cols // WIN_LON, WIN_LON, width)
    return blocks.transpose(0, 2, 1, 3, 4).reshape(-1, WIN_LAT * WIN_LON, width)

def from_windows(wins, rows, cols):
    width = wins.shape[-1]
    blocks = wins.reshape(rows // WIN_LAT, cols // WIN_LON, WIN_LAT, WIN_LON, width)
    return blocks.transpose(0, 2, 1, 3, 4).reshape(rows, cols, width)

def attend(qkv, wrapped):
    count, length, three = qkv.shape
    width = three // 3
    head_size = width // HEADS
    parts = qkv.astype(jnp.float32).reshape(count, length, 3, HEADS, head_size)
    query = parts[:, :, 0]
    keys = parts[:, :, 1]
    values = parts[:, :, 2]
    scores = jnp.einsum('wqhd,wkhd->whqk', query, keys) * head_size ** (-0.5)
    lower = jnp.arange(length) // WIN_LON >= SHIFT_LAT
    apart = lower[:, None] != lower[None, :]
    blocked = wrapped[:, None, None, None] & apart[None, None, :, :]
    scores = jnp.where(blocked, jnp.float32(-1e+30), scores)
    peak = lax.optimization_barrier(jnp.max(scores, axis=-1, keepdims=True))
    weights = jnp.exp(scores - peak)
    probs = (weights / lax.optimization_barrier(jnp.sum(weights, axis=-1, keepdims=True))).astype(jnp.bfloat16)
    mixed = jnp.einsum('whqk,wkhd->wqhd', probs.astype(jnp.float32), values)
    return mixed.reshape(count, length, width).astype(jnp.bfloat16)

def pair_up(field):
    rows, cols, width = field.shape
    return field.reshape(rows // 2, 2, cols // 2, 2, width).transpose(0, 2, 3, 1, 4).reshape(rows // 2, cols // 2, 4 * width)

def split_pairs(paired, width):
    rows, cols = (paired.shape[0], paired.shape[1])
    return paired.reshape(rows, cols, 2, 2, width).transpose(0, 3, 1, 2, 4).reshape(2 * rows, 2 * cols, width)

def window_forward(shifted, wrapped, w_qkv, w_proj):
    rows, cols, width = shifted.shape
    wins = to_windows(shifted)
    flat = wins.reshape(-1, width)
    qkv = jnp.dot(flat, w_qkv, preferred_element_type=jnp.float32).astype(jnp.bfloat16)
    mixed = attend(qkv.reshape(wins.shape[0], wins.shape[1], 3 * width), wrapped)
    out = jnp.dot(mixed.reshape(-1, width), w_proj, preferred_element_type=jnp.float32).astype(jnp.bfloat16)
    return from_windows(out.reshape(wins.shape), rows, cols)

def window_backward(shifted, upstream_field, wrapped, w_qkv, w_proj):
    rows, cols, width = shifted.shape
    wins = to_windows(shifted)
    count, length = (wins.shape[0], wins.shape[1])
    flat = wins.reshape(-1, width)
    qkv = jnp.dot(flat, w_qkv, preferred_element_type=jnp.float32).astype(jnp.bfloat16)
    mixed, pullback = jax.vjp(lambda packed: attend(packed, wrapped), qkv.reshape(count, length, 3 * width))
    mixed_flat = mixed.reshape(-1, width)
    upstream = to_windows(upstream_field).reshape(-1, width)
    contract = (((0,), (0,)), ((), ()))
    grad_proj = lax.dot_general(mixed_flat, upstream, contract, preferred_element_type=jnp.float32)
    d_mixed = jnp.dot(upstream, w_proj.T, preferred_element_type=jnp.float32).astype(jnp.bfloat16)
    d_qkv, = pullback(d_mixed.reshape(count, length, width))
    d_flat = d_qkv.reshape(-1, 3 * width)
    grad_qkv = lax.dot_general(flat, d_flat, contract, preferred_element_type=jnp.float32)
    d_shift = jnp.dot(d_flat, w_qkv.T, preferred_element_type=jnp.float32).astype(jnp.bfloat16)
    return (from_windows(d_shift.reshape(count, length, width), rows, cols), grad_qkv, grad_proj)

def reference(tokens, gain_attn, w_qkv, w_proj, gain_merge, w_merge, g_merged):
    width = tokens.shape[-1]
    bands = H_GRID // WIN_LAT
    per_band = W_GRID // WIN_LON
    tokens_wide = tokens.astype(jnp.float32)
    normed = normalize(tokens_wide, gain_attn).astype(jnp.bfloat16)
    shifted = jnp.roll(normed, (-SHIFT_LAT, -SHIFT_LON), (0, 1))
    band_data = shifted.reshape(bands, WIN_LAT, W_GRID, width)
    band_ids = jnp.arange(bands).astype(jnp.int32)

    def forward_band(item):
        index, band = item
        wrapped = jnp.broadcast_to(index == bands - 1, (per_band,))
        return window_forward(band, wrapped, w_qkv, w_proj)
    attended = lax.map(forward_band, (band_ids, band_data)).reshape(H_GRID, W_GRID, width)
    added = jnp.roll(attended, (SHIFT_LAT, SHIFT_LON), (0, 1))
    summed = (tokens_wide + added.astype(jnp.float32)).astype(jnp.bfloat16)
    paired = pair_up(summed).astype(jnp.float32)
    merge_normed, merge_pull = jax.vjp(lambda values: normalize(values, gain_merge), paired)
    merged = jnp.dot(merge_normed.astype(jnp.bfloat16), w_merge, preferred_element_type=jnp.float32).astype(jnp.bfloat16)
    d_merge = jnp.dot(g_merged, w_merge.T, preferred_element_type=jnp.float32)
    d_paired, = merge_pull(d_merge)
    d_summed = split_pairs(d_paired, width).astype(jnp.bfloat16)
    d_shifted = jnp.roll(d_summed, (-SHIFT_LAT, -SHIFT_LON), (0, 1)).reshape(bands, WIN_LAT, W_GRID, width)

    def backward_band(carry, item):
        index, band, upstream = item
        wrapped = jnp.broadcast_to(index == bands - 1, (per_band,))
        d_band, grad_qkv, grad_proj = window_backward(band, upstream, wrapped, w_qkv, w_proj)
        return ((carry[0] + grad_qkv, carry[1] + grad_proj), d_band)
    start = (jnp.zeros((width, 3 * width), jnp.float32), jnp.zeros((width, width), jnp.float32))
    (grad_qkv, grad_proj), d_bands = lax.scan(backward_band, start, (band_ids, band_data, d_shifted))
    d_normed = jnp.roll(d_bands.reshape(H_GRID, W_GRID, width), (SHIFT_LAT, SHIFT_LON), (0, 1))
    _, norm_pull = jax.vjp(lambda values: normalize(values, gain_attn), tokens_wide)
    d_tokens, = norm_pull(d_normed.astype(jnp.float32))
    grad_tokens = (d_summed.astype(jnp.float32) + d_tokens).astype(jnp.bfloat16)
    grad_weights = jnp.concatenate([grad_qkv, grad_proj], axis=1)
    return (merged, grad_tokens, grad_weights)
```

```python
import jax
import jax.numpy as jnp
import numpy as np
from jax import lax
from jax.experimental import pallas as pl
from jax.experimental.pallas import tpu as pltpu
from jax.sharding import PartitionSpec as P

D = 512
HEADS = 8
HEAD = D // HEADS
WIN_LAT = 6
WIN_LON = 12
SHIFT_LAT = 3
SHIFT_LON = 6
EPS = 1e-05

ROWS, COLS = 12, 48
BORDER = 8
TOKENS = ROWS * COLS
LEN = WIN_LAT * WIN_LON
PAD = 80
PER_BAND = COLS // WIN_LON
BAND = PER_BAND * PAD
WINDOWS = 2 * PER_BAND
TOP = SHIFT_LAT * COLS
EDGE = ROWS * BORDER
CORNER = SHIFT_LAT * BORDER
SIDE = WIN_LAT * BORDER
BAND_CELLS = WIN_LAT * COLS
GROUP = HEADS // 2
GROUP_WIDTH = GROUP * HEAD
LOCAL = PER_BAND - 1
INNER = LOCAL * PAD
REST = WINDOWS - LOCAL
OUTER = REST * PAD
HELD = 8
WIDTH = WINDOWS * PAD
NEG = -1e30

f32 = jnp.float32
bf16 = jnp.bfloat16


def window_selector():
    pick = np.zeros((BAND, BAND_CELLS + SIDE), np.float32)
    for win in range(PER_BAND):
        for i in range(WIN_LAT):
            for j in range(WIN_LON):
                col = win * WIN_LON + j + SHIFT_LON
                at = i * COLS + col if col < COLS else BAND_CELLS + i * BORDER + col - COLS
                pick[win * PAD + i * WIN_LON + j, at] = 1.0
    return pick


def pair_selector():
    pick = np.zeros((4 * COLS, 4 * COLS), np.float32)
    quarter = COLS
    for a in range(2):
        for b in range(COLS // 2):
            for k, (i, j) in enumerate(((0, 0), (1, 0), (0, 1), (1, 1))):
                pick[k * quarter + a * (COLS // 2) + b, (2 * a + i) * COLS + 2 * b + j] = 1.0
    return pick


def dot(a, b):
    return lax.dot_general(a, b, (((1,), (0,)), ((), ())), preferred_element_type=f32)


def dot_nt(a, b):
    return lax.dot_general(a, b, (((1,), (1,)), ((), ())), preferred_element_type=f32)


def dot_tn(a, b):
    return lax.dot_general(a, b, (((0,), (0,)), ((), ())), preferred_element_type=f32)


def norm_parts(values):
    centred = values - jnp.mean(values, axis=-1, keepdims=True)
    scale = lax.rsqrt(jnp.mean(centred * centred, axis=-1, keepdims=True) + EPS)
    return centred * scale, scale


def outer_windows(pick_ref, cells, lat, lon, diag):
    first = jnp.concatenate([cells[:BAND_CELLS], lon[CORNER : CORNER + SIDE].astype(bf16)], axis=0)
    beside = jnp.concatenate([lon[CORNER + SIDE :], diag[:CORNER]], axis=0).astype(bf16)
    second = jnp.concatenate([cells[BAND_CELLS:], lat, beside], axis=0)
    return dot(pick_ref[INNER:], first).astype(bf16), dot(pick_ref[...], second).astype(bf16)


def head_masks(dtype):
    lane = lax.broadcasted_iota(jnp.int32, (1, GROUP_WIDTH), 1) // HEAD
    return [(lane == h).astype(f32).astype(dtype) for h in range(GROUP)]


def spread_heads(block, masks):
    return jnp.concatenate([block * m for m in masks], axis=0)


def collect_heads(stacked, masks):
    total = stacked[:PAD] * masks[0]
    for h in range(1, GROUP):
        total = total + stacked[h * PAD : (h + 1) * PAD] * masks[h]
    return total


def last_band():
    at_end = lax.axis_index("lat") == lax.axis_size("lat") - 1
    return jnp.where(at_end, f32(1), f32(0))


def score_masks():
    shape = (PAD, GROUP * PAD)
    key = lax.broadcasted_iota(jnp.int32, shape, 0)
    query = lax.rem(lax.broadcasted_iota(jnp.int32, shape, 1), PAD)
    base = jnp.where(key >= LEN, f32(NEG), f32(0))
    apart = jnp.where((key < LEN // 2) != (query < LEN // 2), f32(NEG), f32(0))
    return base, jnp.minimum(base, apart * last_band())


def attend(windows, qkv_ref, mixed_ref, probs_ref):
    low, wide = head_masks(bf16), head_masks(f32)
    masks = score_masks()
    for win, wraps in enumerate(windows):
        rows = pl.ds(win * PAD, PAD)
        mask = masks[1] if wraps else masks[0]
        for g in range(2):
            at = g * GROUP_WIDTH
            queries = spread_heads(qkv_ref[rows, at : at + GROUP_WIDTH], low)
            keys = qkv_ref[rows, D + at : D + at + GROUP_WIDTH]
            values = qkv_ref[rows, 2 * D + at : 2 * D + at + GROUP_WIDTH]
            scores = dot_nt(keys, queries) * HEAD ** (-0.5) + mask
            weights = jnp.exp(scores - jnp.max(scores, axis=0, keepdims=True))
            probs = weights * (1.0 / jnp.sum(weights, axis=0, keepdims=True))
            probs_ref[win, g] = probs
            mixed = collect_heads(dot_tn(probs.astype(bf16), values), wide)
            mixed_ref[rows, at : at + GROUP_WIDTH] = mixed.astype(bf16)


def attend_back(count, offset, qkv_ref, probs_ref, dmix_ref, dqkv_ref):
    low, wide = head_masks(bf16), head_masks(f32)
    for win in range(count):
        rows = pl.ds(win * PAD, PAD)
        out = pl.ds(offset + win * PAD, PAD)
        for g in range(2):
            at = g * GROUP_WIDTH
            queries = spread_heads(qkv_ref[rows, at : at + GROUP_WIDTH], low)
            keys = qkv_ref[rows, D + at : D + at + GROUP_WIDTH]
            values = qkv_ref[rows, 2 * D + at : 2 * D + at + GROUP_WIDTH]
            above = spread_heads(dmix_ref[rows, at : at + GROUP_WIDTH], low)
            probs = probs_ref[win, g]
            d_probs = dot_nt(values, above).astype(bf16).astype(f32)
            along = probs * d_probs
            d_scores = along - probs * jnp.sum(along, axis=0, keepdims=True)
            d_scores = (d_scores * HEAD ** (-0.5)).astype(bf16)
            d_queries = collect_heads(dot_tn(d_scores, keys), wide)
            d_keys = dot(d_scores, queries)
            d_values = dot(probs.astype(bf16), above)
            dqkv_ref[out, at : at + GROUP_WIDTH] = d_queries.astype(bf16)
            dqkv_ref[out, D + at : D + at + GROUP_WIDTH] = d_keys.astype(bf16)
            dqkv_ref[out, 2 * D + at : 2 * D + at + GROUP_WIDTH] = d_values.astype(bf16)


def put_back(result, back_ref, main_ref, lat_ref, lon_ref):
    for band in range(2):
        cells = dot(back_ref[...], result(band)).astype(bf16)
        if band == 0:
            main_ref[:BAND_CELLS] = cells[:BAND_CELLS]
        else:
            main_ref[BAND_CELLS:] = cells[: BAND_CELLS - TOP]
            lat_ref[...] = cells[BAND_CELLS - TOP : BAND_CELLS]
        lon_ref[band * SIDE : (band + 1) * SIDE] = cells[BAND_CELLS:]


def assemble(main_ref, lat_ref, lon_ref, diag_ref, out_ref):
    out_ref[:SHIFT_LAT] = lat_ref[...].astype(f32).reshape(SHIFT_LAT, COLS, D)
    out_ref[SHIFT_LAT:] = main_ref[...].astype(f32).reshape(ROWS - SHIFT_LAT, COLS, D)
    corner = diag_ref[...].astype(f32)[SIDE - CORNER :].reshape(SHIFT_LAT, BORDER, D)
    beside = lon_ref[...].astype(f32)[: EDGE - CORNER].reshape(ROWS - SHIFT_LAT, BORDER, D)
    out_ref[:SHIFT_LAT, :BORDER] += corner
    out_ref[SHIFT_LAT:, :BORDER] += beside


def border_kernel(tok_ref, own_ref, top_ref, edge_ref, corner_ref, sem):
    copy = pltpu.make_async_copy(tok_ref, own_ref, sem)
    copy.start()
    copy.wait()
    top_ref[...] = own_ref[:TOP]
    edge = [own_ref[row * COLS : row * COLS + 16].astype(f32)[:BORDER] for row in range(ROWS)]
    edge_ref[...] = jnp.concatenate(edge, axis=0).astype(bf16)
    corner_ref[...] = jnp.concatenate(edge[:WIN_LAT], axis=0).astype(bf16)


def inner_kernel(tok_ref, *refs):
    held, got = refs[:HELD], refs[HELD : 2 * HELD]
    cells_ref, xs_ref, qkv_ref, mixed_ref, probs_ref, att_ref, sem = refs[2 * HELD :]
    copies = [pltpu.make_async_copy(a, b, sem.at[i]) for i, (a, b) in enumerate(zip(held, got))]
    for copy in copies:
        copy.start()
    gain_ref, pick_ref, wqkv_ref, wproj_ref = got[:4]
    normed = norm_parts(tok_ref[TOP:].astype(f32))[0]
    for copy in copies:
        copy.wait()
    cells_ref[...] = (normed * gain_ref[...]).astype(bf16)
    xs_ref[...] = dot(pick_ref[:INNER, :BAND_CELLS], cells_ref[:BAND_CELLS]).astype(bf16)
    qkv_ref[...] = dot(xs_ref[...], wqkv_ref[...]).astype(bf16)
    attend([False] * LOCAL, qkv_ref, mixed_ref, probs_ref)
    att_ref[...] = dot(mixed_ref[...], wproj_ref[...]).astype(bf16)


def outer_kernel(
    cells_ref, lat_ref, lon_ref, diag_ref, gain_ref, wqkv_ref, wproj_ref, pick_ref, back_ref, att0_ref,
    xs_ref, qkv_ref, mixed_ref, probs_ref, main_ref, out_lat_ref, out_lon_ref,
    att_ref,
):
    def normed(ref):
        return norm_parts(ref[...].astype(f32))[0] * gain_ref[...]

    first, second = outer_windows(
        pick_ref, cells_ref[...], normed(lat_ref).astype(bf16), normed(lon_ref), normed(diag_ref)
    )
    xs_ref[:PAD] = first
    xs_ref[PAD:] = second
    qkv_ref[...] = dot(xs_ref[...], wqkv_ref[...]).astype(bf16)
    attend([False] + [True] * PER_BAND, qkv_ref, mixed_ref, probs_ref)
    att_ref[:INNER] = att0_ref[...]
    att_ref[INNER:] = dot(mixed_ref[...], wproj_ref[...]).astype(bf16)
    put_back(lambda band: att_ref[pl.ds(band * BAND, BAND)], back_ref, main_ref, out_lat_ref, out_lon_ref)


def cotangent_kernel(g_ref, gain_ref, wmerge_ref, out_ref, weights_ref, held_ref, sem):
    copies = [
        pltpu.make_async_copy(g_ref, held_ref, sem.at[0]),
        pltpu.make_async_copy(wmerge_ref, weights_ref, sem.at[1]),
    ]
    for copy in copies:
        copy.start()
    for copy in copies:
        copy.wait()
    for k in range(4):
        out_ref[k] = dot_nt(held_ref[...], weights_ref[k * D : (k + 1) * D]) * gain_ref[k]


def pair_kernel(
    tok_ref, main_ref, lat_ref, lon_ref, diag_ref, gain_ref, cot_ref, pair_ref, unpair_ref,
    dsum_ref, edge_ref, normed_ref,
    added_ref, members_ref,
):
    assemble(main_ref, lat_ref, lon_ref, diag_ref, added_ref)
    quarter = COLS
    for part in range(3):
        rows = pl.ds(part * 4 * COLS, 4 * COLS)
        added = added_ref[pl.ds(part * 4, 4)].reshape(4 * COLS, D)
        summed = (tok_ref[rows].astype(f32) + added).astype(bf16)
        paired = dot(pair_ref[...], summed)
        for k in range(4):
            members_ref[k, pl.ds(part * quarter, quarter)] = paired[k * quarter : (k + 1) * quarter]
    width = 4 * D
    total = sum(jnp.sum(members_ref[k], axis=-1, keepdims=True) for k in range(4))
    center = total / width
    for k in range(4):
        members_ref[k] = members_ref[k] - center
    spread = sum(jnp.sum(members_ref[k] * members_ref[k], axis=-1, keepdims=True) for k in range(4)) / width
    scale = lax.rsqrt(spread + EPS)
    for k in range(4):
        members_ref[k] = members_ref[k] * scale
        normed_ref[k] = (members_ref[k] * gain_ref[k]).astype(bf16)
    flat = sum(jnp.sum(cot_ref[k], axis=-1, keepdims=True) for k in range(4)) / width
    along = sum(jnp.sum(cot_ref[k] * members_ref[k], axis=-1, keepdims=True) for k in range(4)) / width
    for k in range(4):
        members_ref[k] = (cot_ref[k] - flat - members_ref[k] * along) * scale
    for part in range(3):
        rows = pl.ds(part * quarter, quarter)
        block = jnp.concatenate([members_ref[k, rows].astype(bf16) for k in range(4)], axis=0)
        cells = dot(unpair_ref[...], block)
        dsum_ref[pl.ds(part * 4 * COLS, 4 * COLS)] = cells.astype(bf16)
        added_ref[pl.ds(part * 4, 4)] = cells.reshape(4, COLS, D)
    edge_ref[...] = added_ref[:, :BORDER].reshape(EDGE, D).astype(bf16)


def merge_kernel(normed_ref, wmerge_ref, out_ref):
    total = dot(normed_ref[0], wmerge_ref[:D])
    for k in range(1, 4):
        total = total + dot(normed_ref[k], wmerge_ref[k * D : (k + 1) * D])
    out_ref[...] = total.astype(bf16)


def inner_back_kernel(
    dsum_ref, qkv_ref, probs_ref, wproj_ref, pick_ref, xs0_ref, xs_ref, mixed0_ref, mixed_ref,
    up_ref, dqkv_ref, xst_ref, mixt_ref,
    dmix_ref,
):
    xst_ref[...] = jnp.concatenate([xs0_ref[...], xs_ref[...]], axis=0).T
    mixt_ref[...] = jnp.concatenate([mixed0_ref[...], mixed_ref[...]], axis=0).T
    up_ref[...] = dot(pick_ref[:INNER, :BAND_CELLS], dsum_ref[TOP : TOP + BAND_CELLS]).astype(bf16)
    dmix_ref[...] = dot_nt(up_ref[...], wproj_ref[...]).astype(bf16)
    attend_back(LOCAL, 0, qkv_ref, probs_ref, dmix_ref, dqkv_ref)


def outer_back_kernel(
    dsum_ref, lat_ref, lon_ref, diag_ref, xst_ref, mixt_ref, up0_ref, dqkv0_ref,
    qkv_ref, probs_ref, wproj_ref, pick_ref,
    dqkv_ref, keep_ref, send_ref,
    up_ref, dmix_ref,
):
    first, second = outer_windows(
        pick_ref, dsum_ref[TOP:], lat_ref[...], lon_ref[...].astype(f32), diag_ref[...].astype(f32)
    )
    up_ref[:INNER] = up0_ref[...]
    up_ref[INNER:BAND] = first
    up_ref[BAND:] = second
    dqkv_ref[:INNER] = dqkv0_ref[...]
    dmix_ref[...] = dot_nt(up_ref[INNER:], wproj_ref[...]).astype(bf16)
    attend_back(REST, INNER, qkv_ref, probs_ref, dmix_ref, dqkv_ref)
    lat_at, lon_at = lax.axis_index("lat"), lax.axis_index("lon")
    even_core = lax.rem(lon_at, 2) == 0
    my_x = lax.rem(lax.div(lon_at, 2), 4)
    my_y = lax.div(lat_at, 8) * 2 + lax.div(lon_at, 8)
    x_steps = [lax.bitwise_xor(my_x, jnp.int32(i)) for i in range(4)]
    y_steps = [lax.bitwise_xor(my_y, jnp.int32(i)) for i in range(4)]
    for col in range(8):
        if col < 6:
            grad = dot(xst_ref[...], dqkv_ref[:, col * 256 : (col + 1) * 256])
        else:
            grad = dot(mixt_ref[...], up_ref[:, (col - 6) * 256 : (col - 5) * 256])
        even, odd = grad[:, :128], grad[:, 128:]
        kept = jnp.where(even_core, even, odd).astype(bf16)
        sent = jnp.where(even_core, odd, even).astype(bf16)
        low, x = divmod(col, 4)
        for lat in range(16):
            high, z = divmod(lat, 8)
            y = high * 2 + low
            rows = slice(lat * 32, (lat + 1) * 32)
            on_even = x_steps[x], lat * 2 + low
            on_odd = y_steps[y], z * 4 + x
            mine = [jnp.where(even_core, a, b) for a, b in zip(on_even, on_odd)]
            other = [jnp.where(even_core, b, a) for a, b in zip(on_even, on_odd)]
            keep_ref[mine[0], mine[1]] = kept[rows]
            send_ref[other[0], other[1]] = sent[rows]


def cells_back_kernel(dqkv_ref, wqkv_ref, back_ref, main_ref, out_lat_ref, out_lon_ref, dx_ref):
    dx_ref[...] = dot_nt(dqkv_ref[...], wqkv_ref[...]).astype(bf16)
    put_back(lambda band: dx_ref[pl.ds(band * BAND, BAND)], back_ref, main_ref, out_lat_ref, out_lon_ref)


def add_kernel(a_ref, b_ref, *out_refs):
    for k, out_ref in enumerate(out_refs):
        out_ref[...] = (a_ref[k].astype(f32) + b_ref[k].astype(f32)).astype(bf16)


def join_kernel(a_ref, b_ref, c_ref, d_ref, out_ref):
    total = a_ref[...].astype(f32) + b_ref[...].astype(f32) + c_ref[...].astype(f32) + d_ref[...].astype(f32)
    out_ref[...] = total.astype(bf16)


def sum_kernel(parts_ref, out_ref):
    total = parts_ref[0].astype(f32)
    for i in range(1, parts_ref.shape[0]):
        total = total + parts_ref[i].astype(f32)
    out_ref[...] = total.astype(out_ref.dtype)


def tokens_kernel(tok_ref, dsum_ref, main_ref, lat_ref, lon_ref, diag_ref, gain_ref, out_ref, field_ref):
    assemble(main_ref, lat_ref, lon_ref, diag_ref, field_ref)
    for part in range(3):
        rows = pl.ds(part * 4 * COLS, 4 * COLS)
        cot = field_ref[pl.ds(part * 4, 4)].reshape(4 * COLS, D) * gain_ref[...]
        normed, scale = norm_parts(tok_ref[rows].astype(f32))
        flat = jnp.mean(cot, axis=-1, keepdims=True)
        along = jnp.mean(cot * normed, axis=-1, keepdims=True)
        d_tokens = (cot - flat - normed * along) * scale
        out_ref[rows] = (dsum_ref[rows].astype(f32) + d_tokens).astype(bf16)


def call(kernel, outs, scratch=(), places=None, limit=20):
    spaces = {} if places is None else {
        "in_specs": [pl.BlockSpec(memory_space=pl.ANY if p else pltpu.VMEM) for p in places]
    }
    return pl.pallas_call(
        kernel,
        out_shape=[jax.ShapeDtypeStruct(s, t) for s, t in outs],
        scratch_shapes=[pltpu.VMEM(*s) if isinstance(s, tuple) else s for s in scratch],
        cost_estimate=pl.CostEstimate(flops=10**9, bytes_accessed=2 * 10**6, transcendentals=0),
        compiler_params=pltpu.CompilerParams(vmem_limit_bytes=limit * 1024 * 1024),
        **spaces,
    )


SCATTERED = [((TOKENS - TOP, D), bf16), ((TOP, D), bf16), ((EDGE, D), bf16)]


def saved(count):
    rows = count * PAD
    return [((rows, D), bf16), ((rows, 3 * D), bf16), ((rows, D), bf16), ((count, 2, PAD, GROUP * PAD), f32)]


def after(value, *others):
    return lax.optimization_barrier((value, *others))[0]


def chain(tok, gain, w_qkv, w_proj, gain_merge, w_merge, g_merged, fetch, hand_on):
    tok, top, edge, corner = call(
        border_kernel,
        [((TOKENS, D), bf16), ((TOP, D), bf16), ((EDGE, D), bf16), ((SIDE, D), bf16)],
        [pltpu.SemaphoreType.DMA],
        [1],
    )(tok)
    beside = fetch(top, edge, corner)
    pick, pair = window_selector(), pair_selector()
    selectors = [jnp.asarray(c, bf16) for c in (pick.T, pair, pair.T)]
    held = [gain, jnp.asarray(pick, bf16), w_qkv, w_proj, gain_merge] + selectors
    got = call(
        inner_kernel,
        [(h.shape, h.dtype) for h in held] + [((TOKENS - TOP, D), bf16)] + saved(LOCAL) + [((INNER, D), bf16)],
        [pltpu.SemaphoreType.DMA((HELD,))],
        [0] + [1] * HELD,
    )(tok, *held)
    gain, pick, w_qkv, w_proj, gain_merge, back, pair, unpair = got[:HELD]
    cells, xs0, qkv0, mixed0, probs0, att0 = got[HELD:]
    xs1, qkv1, mixed1, probs1, main, to_lat, to_lon = call(
        outer_kernel, saved(REST) + SCATTERED, [((WIDTH, D), bf16)]
    )(cells, *beside, gain, w_qkv, w_proj, pick, back, att0)
    beside = hand_on(to_lat, to_lon)
    cots, w_merge = call(
        cotangent_kernel,
        [((4, TOKENS // 4, D), f32), ((4 * D, 2 * D), bf16)],
        [((TOKENS // 4, 2 * D), bf16), pltpu.SemaphoreType.DMA((2,))],
        [1, 0, 1],
    )(after(g_merged, to_lat), gain_merge, w_merge)
    d_summed, edge, merge_normed = call(
        pair_kernel,
        [((TOKENS, D), bf16), ((EDGE, D), bf16), ((4, TOKENS // 4, D), bf16)],
        [((ROWS, COLS, D), f32), ((4, TOKENS // 4, D), f32)],
    )(tok, main, *beside, gain_merge, cots, pair, unpair)
    beside = fetch(d_summed[:TOP], edge, edge[:SIDE])
    (merged,) = call(merge_kernel, [((TOKENS // 4, 2 * D), bf16)])(merge_normed, w_merge)
    up0, dqkv0, xst, mixt = call(
        inner_back_kernel,
        [((INNER, D), bf16), ((INNER, 3 * D), bf16), ((D, WIDTH), bf16), ((D, WIDTH), bf16)],
        [((INNER, D), bf16)],
    )(d_summed, qkv0, probs0, w_proj, pick, xs0, xs1, mixed0, mixed1)
    dqkv, keep, sent = call(
        outer_back_kernel,
        [((WIDTH, 3 * D), bf16), ((4, 32, 32, 128), bf16), ((4, 32, 32, 128), bf16)],
        [((WIDTH, D), bf16), ((OUTER, D), bf16)],
    )(d_summed, *beside, xst, mixt, after(up0, merged), dqkv0, qkv1, probs1, w_proj, pick)
    main, to_lat, to_lon = call(cells_back_kernel, SCATTERED, [((WIDTH, D), bf16)])(dqkv, w_qkv, back)

    def finish(ready):
        beside = hand_on(after(to_lat, ready), after(to_lon, ready))
        (grad_tokens,) = call(tokens_kernel, [((TOKENS, D), bf16)], [((ROWS, COLS, D), f32)])(
            tok, d_summed, main, *beside, gain
        )
        return merged, grad_tokens

    return finish, keep, sent, to_lat


def solution(mesh):
    lats, lons = mesh.shape["lat"], mesh.shape["lon"]
    count = lats * lons

    def send(block, down, right):
        route = [
            (i, (i // lons + down) % lats * lons + (i % lons + right) % lons) for i in range(count)
        ]
        return lax.ppermute(block, ("lat", "lon"), route)

    def fetch(top, edge, corner):
        return send(top, -1, 0), send(edge, 0, -1), send(corner, -1, -1)

    def hand_on(lat, lon):
        return send(lat, 1, 0), send(lon, 0, 1), send(lon[SIDE:], 1, 1)

    def place(i):
        lat, lon = divmod(i, lons)
        return lat // 8, lat % 8, lon // 8, lon // 2 % 4, lon % 2

    def across(i, step):
        high, z, low, x, core = place(i)
        if core:
            high, low = divmod((high * 2 + low) ^ step, 2)
        else:
            x = x ^ step
        return (high * 8 + z) * lons + low * 8 + x * 2 + core

    rest = {}
    for i in range(count):
        high, z, low, x, core = place(i)
        rest.setdefault((core, high * 2 + low if core else x), []).append(i)
    rest = list(rest.values())

    def reduce_across(keep, sent, ready):
        other = lax.ppermute(sent, ("lat", "lon"), [(i, i ^ 1) for i in range(count)])
        own, *others = call(add_kernel, [((32, 32, 128), bf16)] * 4)(keep, after(other, ready))
        got = [
            lax.ppermute(block, ("lat", "lon"), [(i, across(i, step)) for i in range(count)])
            for step, block in enumerate(others, 1)
        ]
        return call(join_kernel, [((32, 32, 128), bf16)])(own, *got)[0]

    def reduce_rest(sums):
        parts = lax.all_to_all(sums, ("lat", "lon"), 0, 0, axis_index_groups=rest, tiled=True)
        return call(sum_kernel, [((32, 128), f32)])(parts)[0]

    def body(tokens, gain_attn, w_qkv, w_proj, gain_merge, w_merge, g_merged):
        finish, keep, sent, ready = chain(
            tokens.reshape(TOKENS, D), gain_attn.reshape(1, D), w_qkv, w_proj, gain_merge.reshape(4, 1, D),
            w_merge, g_merged.reshape(TOKENS // 4, 2 * D), fetch, hand_on,
        )
        sums = reduce_across(keep, sent, ready)
        grad_weights = reduce_rest(sums)
        merged, grad_tokens = finish(sums)
        return (
            merged.reshape(ROWS // 2, COLS // 2, 2 * D),
            grad_tokens.reshape(ROWS, COLS, D),
            grad_weights,
        )

    return jax.shard_map(
        body,
        mesh=mesh,
        in_specs=(P("lat", "lon", None), P(), P(), P(), P(), P(), P("lat", "lon", None)),
        out_specs=(P("lat", "lon", None), P("lat", "lon", None), P("lat", "lon")),
        check_vma=False,
    )
```

```python
import jax
import jax.numpy as jnp
import numpy as np
from jax import lax
from jax.experimental import pallas as pl
from jax.experimental.pallas import tpu as pltpu
from jax.sharding import PartitionSpec as P

D = 512
HEADS = 8
HEAD = D // HEADS
WIN_LAT = 6
WIN_LON = 12
SHIFT_LAT = 3
SHIFT_LON = 6
EPS = 1e-05

ROWS, COLS = 12, 48
BORDER = 8
TOKENS = ROWS * COLS
LEN = WIN_LAT * WIN_LON
PAD = 80
PER_BAND = COLS // WIN_LON
BAND = PER_BAND * PAD
WINDOWS = 2 * PER_BAND
TOP = SHIFT_LAT * COLS
EDGE = ROWS * BORDER
CORNER = SHIFT_LAT * BORDER
SIDE = WIN_LAT * BORDER
BAND_CELLS = WIN_LAT * COLS
GROUP = HEADS // 2
GROUP_WIDTH = GROUP * HEAD
LOCAL = PER_BAND - 1
INNER = LOCAL * PAD
REST = WINDOWS - LOCAL
OUTER = REST * PAD
HELD = 8
WIDTH = WINDOWS * PAD
NEG = -1e30

f32 = jnp.float32
bf16 = jnp.bfloat16


def window_selector():
    pick = np.zeros((BAND, BAND_CELLS + SIDE), np.float32)
    for win in range(PER_BAND):
        for i in range(WIN_LAT):
            for j in range(WIN_LON):
                col = win * WIN_LON + j + SHIFT_LON
                at = i * COLS + col if col < COLS else BAND_CELLS + i * BORDER + col - COLS
                pick[win * PAD + i * WIN_LON + j, at] = 1.0
    return pick


def pair_selector():
    pick = np.zeros((4 * COLS, 4 * COLS), np.float32)
    quarter = COLS
    for a in range(2):
        for b in range(COLS // 2):
            for k, (i, j) in enumerate(((0, 0), (1, 0), (0, 1), (1, 1))):
                pick[k * quarter + a * (COLS // 2) + b, (2 * a + i) * COLS + 2 * b + j] = 1.0
    return pick


def dot(a, b):
    return lax.dot_general(a, b, (((1,), (0,)), ((), ())), preferred_element_type=f32)


def dot_nt(a, b):
    return lax.dot_general(a, b, (((1,), (1,)), ((), ())), preferred_element_type=f32)


def dot_tn(a, b):
    return lax.dot_general(a, b, (((0,), (0,)), ((), ())), preferred_element_type=f32)


def norm_parts(values):
    centred = values - jnp.mean(values, axis=-1, keepdims=True)
    scale = lax.rsqrt(jnp.mean(centred * centred, axis=-1, keepdims=True) + EPS)
    return centred * scale, scale


def outer_windows(pick_ref, cells, lat, lon, diag):
    first = jnp.concatenate([cells[:BAND_CELLS], lon[CORNER : CORNER + SIDE].astype(bf16)], axis=0)
    beside = jnp.concatenate([lon[CORNER + SIDE :], diag[:CORNER]], axis=0).astype(bf16)
    second = jnp.concatenate([cells[BAND_CELLS:], lat, beside], axis=0)
    return dot(pick_ref[INNER:], first).astype(bf16), dot(pick_ref[...], second).astype(bf16)


def head_masks(dtype):
    lane = lax.broadcasted_iota(jnp.int32, (1, GROUP_WIDTH), 1) // HEAD
    return [(lane == h).astype(f32).astype(dtype) for h in range(GROUP)]


def spread_heads(block, masks):
    return jnp.concatenate([block * m for m in masks], axis=0)


def collect_heads(stacked, masks):
    total = stacked[:PAD] * masks[0]
    for h in range(1, GROUP):
        total = total + stacked[h * PAD : (h + 1) * PAD] * masks[h]
    return total


def last_band():
    at_end = lax.axis_index("lat") == lax.axis_size("lat") - 1
    return jnp.where(at_end, f32(1), f32(0))


def score_masks():
    shape = (PAD, GROUP * PAD)
    key = lax.broadcasted_iota(jnp.int32, shape, 0)
    query = lax.rem(lax.broadcasted_iota(jnp.int32, shape, 1), PAD)
    base = jnp.where(key >= LEN, f32(NEG), f32(0))
    apart = jnp.where((key < LEN // 2) != (query < LEN // 2), f32(NEG), f32(0))
    return base, jnp.minimum(base, apart * last_band())


def attend(windows, qkv_ref, mixed_ref, probs_ref):
    low, wide = head_masks(bf16), head_masks(f32)
    masks = score_masks()
    for win, wraps in enumerate(windows):
        rows = pl.ds(win * PAD, PAD)
        mask = masks[1] if wraps else masks[0]
        for g in range(2):
            at = g * GROUP_WIDTH
            queries = spread_heads(qkv_ref[rows, at : at + GROUP_WIDTH], low)
            keys = qkv_ref[rows, D + at : D + at + GROUP_WIDTH]
            values = qkv_ref[rows, 2 * D + at : 2 * D + at + GROUP_WIDTH]
            scores = dot_nt(keys, queries) * HEAD ** (-0.5) + mask
            weights = jnp.exp(scores - jnp.max(scores, axis=0, keepdims=True))
            probs = weights * (1.0 / jnp.sum(weights, axis=0, keepdims=True))
            probs_ref[win, g] = probs
            mixed = collect_heads(dot_tn(probs.astype(bf16), values), wide)
            mixed_ref[rows, at : at + GROUP_WIDTH] = mixed.astype(bf16)


def attend_back(count, offset, qkv_ref, probs_ref, dmix_ref, dqkv_ref):
    low, wide = head_masks(bf16), head_masks(f32)
    for win in range(count):
        rows = pl.ds(win * PAD, PAD)
        out = pl.ds(offset + win * PAD, PAD)
        for g in range(2):
            at = g * GROUP_WIDTH
            queries = spread_heads(qkv_ref[rows, at : at + GROUP_WIDTH], low)
            keys = qkv_ref[rows, D + at : D + at + GROUP_WIDTH]
            values = qkv_ref[rows, 2 * D + at : 2 * D + at + GROUP_WIDTH]
            above = spread_heads(dmix_ref[rows, at : at + GROUP_WIDTH], low)
            probs = probs_ref[win, g]
            d_probs = dot_nt(values, above).astype(bf16).astype(f32)
            along = probs * d_probs
            d_scores = along - probs * jnp.sum(along, axis=0, keepdims=True)
            d_scores = (d_scores * HEAD ** (-0.5)).astype(bf16)
            d_queries = collect_heads(dot_tn(d_scores, keys), wide)
            d_keys = dot(d_scores, queries)
            d_values = dot(probs.astype(bf16), above)
            dqkv_ref[out, at : at + GROUP_WIDTH] = d_queries.astype(bf16)
            dqkv_ref[out, D + at : D + at + GROUP_WIDTH] = d_keys.astype(bf16)
            dqkv_ref[out, 2 * D + at : 2 * D + at + GROUP_WIDTH] = d_values.astype(bf16)


def put_back(result, back_ref, main_ref, lat_ref, lon_ref):
    for band in range(2):
        cells = dot(back_ref[...], result(band)).astype(bf16)
        if band == 0:
            main_ref[:BAND_CELLS] = cells[:BAND_CELLS]
        else:
            main_ref[BAND_CELLS:] = cells[: BAND_CELLS - TOP]
            lat_ref[...] = cells[BAND_CELLS - TOP : BAND_CELLS]
        lon_ref[band * SIDE : (band + 1) * SIDE] = cells[BAND_CELLS:]


def assemble(main_ref, lat_ref, lon_ref, diag_ref, out_ref):
    out_ref[:SHIFT_LAT] = lat_ref[...].astype(f32).reshape(SHIFT_LAT, COLS, D)
    out_ref[SHIFT_LAT:] = main_ref[...].astype(f32).reshape(ROWS - SHIFT_LAT, COLS, D)
    corner = diag_ref[...].astype(f32)[SIDE - CORNER :].reshape(SHIFT_LAT, BORDER, D)
    beside = lon_ref[...].astype(f32)[: EDGE - CORNER].reshape(ROWS - SHIFT_LAT, BORDER, D)
    out_ref[:SHIFT_LAT, :BORDER] += corner
    out_ref[SHIFT_LAT:, :BORDER] += beside


def border_kernel(tok_ref, own_ref, top_ref, edge_ref, corner_ref, sem):
    copy = pltpu.make_async_copy(tok_ref, own_ref, sem)
    copy.start()
    copy.wait()
    top_ref[...] = own_ref[:TOP]
    edge = [own_ref[row * COLS : row * COLS + 16].astype(f32)[:BORDER] for row in range(ROWS)]
    edge_ref[...] = jnp.concatenate(edge, axis=0).astype(bf16)
    corner_ref[...] = jnp.concatenate(edge[:WIN_LAT], axis=0).astype(bf16)


def inner_kernel(tok_ref, *refs):
    held, got = refs[:HELD], refs[HELD : 2 * HELD]
    cells_ref, xs_ref, qkv_ref, mixed_ref, probs_ref, att_ref, sem = refs[2 * HELD :]
    copies = [pltpu.make_async_copy(a, b, sem.at[i]) for i, (a, b) in enumerate(zip(held, got))]
    for copy in copies:
        copy.start()
    gain_ref, pick_ref, wqkv_ref, wproj_ref = got[:4]
    normed = norm_parts(tok_ref[TOP:].astype(f32))[0]
    for copy in copies:
        copy.wait()
    cells_ref[...] = (normed * gain_ref[...]).astype(bf16)
    xs_ref[...] = dot(pick_ref[:INNER, :BAND_CELLS], cells_ref[:BAND_CELLS]).astype(bf16)
    qkv_ref[...] = dot(xs_ref[...], wqkv_ref[...]).astype(bf16)
    attend([False] * LOCAL, qkv_ref, mixed_ref, probs_ref)
    att_ref[...] = dot(mixed_ref[...], wproj_ref[...]).astype(bf16)


def outer_kernel(
    cells_ref, lat_ref, lon_ref, diag_ref, gain_ref, wqkv_ref, wproj_ref, pick_ref, back_ref, att0_ref,
    xs_ref, qkv_ref, mixed_ref, probs_ref, main_ref, out_lat_ref, out_lon_ref,
    att_ref,
):
    def normed(ref):
        return norm_parts(ref[...].astype(f32))[0] * gain_ref[...]

    first, second = outer_windows(
        pick_ref, cells_ref[...], normed(lat_ref).astype(bf16), normed(lon_ref), normed(diag_ref)
    )
    xs_ref[:PAD] = first
    xs_ref[PAD:] = second
    qkv_ref[...] = dot(xs_ref[...], wqkv_ref[...]).astype(bf16)
    attend([False] + [True] * PER_BAND, qkv_ref, mixed_ref, probs_ref)
    att_ref[:INNER] = att0_ref[...]
    att_ref[INNER:] = dot(mixed_ref[...], wproj_ref[...]).astype(bf16)
    put_back(lambda band: att_ref[pl.ds(band * BAND, BAND)], back_ref, main_ref, out_lat_ref, out_lon_ref)


def cotangent_kernel(g_ref, gain_ref, wmerge_ref, out_ref, weights_ref, held_ref, sem):
    copies = [
        pltpu.make_async_copy(g_ref, held_ref, sem.at[0]),
        pltpu.make_async_copy(wmerge_ref, weights_ref, sem.at[1]),
    ]
    for copy in copies:
        copy.start()
    for copy in copies:
        copy.wait()
    for k in range(4):
        out_ref[k] = dot_nt(held_ref[...], weights_ref[k * D : (k + 1) * D]) * gain_ref[k]


def pair_kernel(
    tok_ref, main_ref, lat_ref, lon_ref, diag_ref, gain_ref, cot_ref, pair_ref, unpair_ref,
    dsum_ref, edge_ref, normed_ref,
    added_ref, members_ref,
):
    assemble(main_ref, lat_ref, lon_ref, diag_ref, added_ref)
    quarter = COLS
    for part in range(3):
        rows = pl.ds(part * 4 * COLS, 4 * COLS)
        added = added_ref[pl.ds(part * 4, 4)].reshape(4 * COLS, D)
        summed = (tok_ref[rows].astype(f32) + added).astype(bf16)
        paired = dot(pair_ref[...], summed)
        for k in range(4):
            members_ref[k, pl.ds(part * quarter, quarter)] = paired[k * quarter : (k + 1) * quarter]
    width = 4 * D
    total = sum(jnp.sum(members_ref[k], axis=-1, keepdims=True) for k in range(4))
    center = total / width
    for k in range(4):
        members_ref[k] = members_ref[k] - center
    spread = sum(jnp.sum(members_ref[k] * members_ref[k], axis=-1, keepdims=True) for k in range(4)) / width
    scale = lax.rsqrt(spread + EPS)
    for k in range(4):
        members_ref[k] = members_ref[k] * scale
        normed_ref[k] = (members_ref[k] * gain_ref[k]).astype(bf16)
    flat = sum(jnp.sum(cot_ref[k], axis=-1, keepdims=True) for k in range(4)) / width
    along = sum(jnp.sum(cot_ref[k] * members_ref[k], axis=-1, keepdims=True) for k in range(4)) / width
    for k in range(4):
        members_ref[k] = (cot_ref[k] - flat - members_ref[k] * along) * scale
    for part in range(3):
        rows = pl.ds(part * quarter, quarter)
        block = jnp.concatenate([members_ref[k, rows].astype(bf16) for k in range(4)], axis=0)
        cells = dot(unpair_ref[...], block)
        dsum_ref[pl.ds(part * 4 * COLS, 4 * COLS)] = cells.astype(bf16)
        added_ref[pl.ds(part * 4, 4)] = cells.reshape(4, COLS, D)
    edge_ref[...] = added_ref[:, :BORDER].reshape(EDGE, D).astype(bf16)


def merge_kernel(normed_ref, wmerge_ref, out_ref):
    total = dot(normed_ref[0], wmerge_ref[:D])
    for k in range(1, 4):
        total = total + dot(normed_ref[k], wmerge_ref[k * D : (k + 1) * D])
    out_ref[...] = total.astype(bf16)


def inner_back_kernel(
    dsum_ref, qkv_ref, probs_ref, wproj_ref, pick_ref, xs0_ref, xs_ref, mixed0_ref, mixed_ref,
    up_ref, dqkv_ref, xst_ref, mixt_ref,
    dmix_ref,
):
    xst_ref[...] = jnp.concatenate([xs0_ref[...], xs_ref[...]], axis=0).T
    mixt_ref[...] = jnp.concatenate([mixed0_ref[...], mixed_ref[...]], axis=0).T
    up_ref[...] = dot(pick_ref[:INNER, :BAND_CELLS], dsum_ref[TOP : TOP + BAND_CELLS]).astype(bf16)
    dmix_ref[...] = dot_nt(up_ref[...], wproj_ref[...]).astype(bf16)
    attend_back(LOCAL, 0, qkv_ref, probs_ref, dmix_ref, dqkv_ref)


def outer_back_kernel(
    dsum_ref, lat_ref, lon_ref, diag_ref, xst_ref, mixt_ref, up0_ref, dqkv0_ref,
    qkv_ref, probs_ref, wproj_ref, pick_ref,
    dqkv_ref, keep_ref, send_ref,
    up_ref, dmix_ref,
):
    first, second = outer_windows(
        pick_ref, dsum_ref[TOP:], lat_ref[...], lon_ref[...].astype(f32), diag_ref[...].astype(f32)
    )
    up_ref[:INNER] = up0_ref[...]
    up_ref[INNER:BAND] = first
    up_ref[BAND:] = second
    dqkv_ref[:INNER] = dqkv0_ref[...]
    dmix_ref[...] = dot_nt(up_ref[INNER:], wproj_ref[...]).astype(bf16)
    attend_back(REST, INNER, qkv_ref, probs_ref, dmix_ref, dqkv_ref)
    lat_at, lon_at = lax.axis_index("lat"), lax.axis_index("lon")
    even_core = lax.rem(lon_at, 2) == 0
    my_x = lax.rem(lax.div(lon_at, 2), 4)
    my_y = lax.div(lat_at, 8) * 2 + lax.div(lon_at, 8)
    x_steps = [lax.bitwise_xor(my_x, jnp.int32(i)) for i in range(4)]
    y_steps = [lax.bitwise_xor(my_y, jnp.int32(i)) for i in range(4)]
    for col in range(8):
        if col < 6:
            grad = dot(xst_ref[...], dqkv_ref[:, col * 256 : (col + 1) * 256])
        else:
            grad = dot(mixt_ref[...], up_ref[:, (col - 6) * 256 : (col - 5) * 256])
        even, odd = grad[:, :128], grad[:, 128:]
        kept = jnp.where(even_core, even, odd).astype(bf16)
        sent = jnp.where(even_core, odd, even).astype(bf16)
        low, x = divmod(col, 4)
        for lat in range(16):
            high, z = divmod(lat, 8)
            y = high * 2 + low
            rows = slice(lat * 32, (lat + 1) * 32)
            on_even = x_steps[x], lat * 2 + low
            on_odd = y_steps[y], z * 4 + x
            mine = [jnp.where(even_core, a, b) for a, b in zip(on_even, on_odd)]
            other = [jnp.where(even_core, b, a) for a, b in zip(on_even, on_odd)]
            keep_ref[mine[0], mine[1]] = kept[rows]
            send_ref[other[0], other[1]] = sent[rows]


def cells_back_kernel(dqkv_ref, wqkv_ref, back_ref, main_ref, out_lat_ref, out_lon_ref, dx_ref):
    dx_ref[...] = dot_nt(dqkv_ref[...], wqkv_ref[...]).astype(bf16)
    put_back(lambda band: dx_ref[pl.ds(band * BAND, BAND)], back_ref, main_ref, out_lat_ref, out_lon_ref)


def add_kernel(a_ref, b_ref, own_ref, later_ref, first_ref, second_ref):
    half = own_ref.shape[0] // 2

    def both(k, rows):
        return (a_ref[k, rows].astype(f32) + b_ref[k, rows].astype(f32)).astype(bf16)

    upper, lower = pl.ds(0, half), pl.ds(half, half)
    own_ref[...] = both(0, pl.ds(0, 2 * half))
    first_ref[0], first_ref[1] = both(1, upper), both(2, upper)
    second_ref[0], second_ref[1] = both(3, lower), both(2, lower)
    later_ref[0], later_ref[1] = both(3, upper), both(1, lower)


def relay_kernel(own_ref, later_ref, first_ref, second_ref, out_ref, to_third_ref, to_first_ref):
    half = own_ref.shape[0] // 2

    def both(a, b):
        return (a.astype(f32) + b.astype(f32)).astype(bf16)

    out_ref[:half] = both(own_ref[:half], first_ref[0])
    out_ref[half:] = both(own_ref[half:], second_ref[0])
    to_third_ref[...] = both(later_ref[0], first_ref[1])
    to_first_ref[...] = both(later_ref[1], second_ref[1])


def join_kernel(own_ref, upper_ref, lower_ref, out_ref):
    half = own_ref.shape[0] // 2
    out_ref[:half] = (own_ref[:half].astype(f32) + upper_ref[...].astype(f32)).astype(bf16)
    out_ref[half:] = (own_ref[half:].astype(f32) + lower_ref[...].astype(f32)).astype(bf16)


def sum_kernel(parts_ref, out_ref):
    total = parts_ref[0].astype(f32)
    for i in range(1, parts_ref.shape[0]):
        total = total + parts_ref[i].astype(f32)
    out_ref[...] = total.astype(out_ref.dtype)


def tokens_kernel(tok_ref, dsum_ref, main_ref, lat_ref, lon_ref, diag_ref, gain_ref, out_ref, field_ref):
    assemble(main_ref, lat_ref, lon_ref, diag_ref, field_ref)
    for part in range(3):
        rows = pl.ds(part * 4 * COLS, 4 * COLS)
        cot = field_ref[pl.ds(part * 4, 4)].reshape(4 * COLS, D) * gain_ref[...]
        normed, scale = norm_parts(tok_ref[rows].astype(f32))
        flat = jnp.mean(cot, axis=-1, keepdims=True)
        along = jnp.mean(cot * normed, axis=-1, keepdims=True)
        d_tokens = (cot - flat - normed * along) * scale
        out_ref[rows] = (dsum_ref[rows].astype(f32) + d_tokens).astype(bf16)


def call(kernel, outs, scratch=(), places=None, limit=20):
    spaces = {} if places is None else {
        "in_specs": [pl.BlockSpec(memory_space=pl.ANY if p else pltpu.VMEM) for p in places]
    }
    return pl.pallas_call(
        kernel,
        out_shape=[jax.ShapeDtypeStruct(s, t) for s, t in outs],
        scratch_shapes=[pltpu.VMEM(*s) if isinstance(s, tuple) else s for s in scratch],
        cost_estimate=pl.CostEstimate(flops=10**9, bytes_accessed=2 * 10**6, transcendentals=0),
        compiler_params=pltpu.CompilerParams(vmem_limit_bytes=limit * 1024 * 1024),
        **spaces,
    )


SCATTERED = [((TOKENS - TOP, D), bf16), ((TOP, D), bf16), ((EDGE, D), bf16)]


def saved(count):
    rows = count * PAD
    return [((rows, D), bf16), ((rows, 3 * D), bf16), ((rows, D), bf16), ((count, 2, PAD, GROUP * PAD), f32)]


def after(value, *others):
    return lax.optimization_barrier((value, *others))[0]


def chain(tok, gain, w_qkv, w_proj, gain_merge, w_merge, g_merged, fetch, hand_on):
    tok, top, edge, corner = call(
        border_kernel,
        [((TOKENS, D), bf16), ((TOP, D), bf16), ((EDGE, D), bf16), ((SIDE, D), bf16)],
        [pltpu.SemaphoreType.DMA],
        [1],
    )(tok)
    beside = fetch(top, edge, corner)
    pick, pair = window_selector(), pair_selector()
    selectors = [jnp.asarray(c, bf16) for c in (pick.T, pair, pair.T)]
    held = [gain, jnp.asarray(pick, bf16), w_qkv, w_proj, gain_merge] + selectors
    got = call(
        inner_kernel,
        [(h.shape, h.dtype) for h in held] + [((TOKENS - TOP, D), bf16)] + saved(LOCAL) + [((INNER, D), bf16)],
        [pltpu.SemaphoreType.DMA((HELD,))],
        [0] + [1] * HELD,
    )(tok, *held)
    gain, pick, w_qkv, w_proj, gain_merge, back, pair, unpair = got[:HELD]
    cells, xs0, qkv0, mixed0, probs0, att0 = got[HELD:]
    xs1, qkv1, mixed1, probs1, main, to_lat, to_lon = call(
        outer_kernel, saved(REST) + SCATTERED, [((WIDTH, D), bf16)]
    )(cells, *beside, gain, w_qkv, w_proj, pick, back, att0)
    beside = hand_on(to_lat, to_lon)
    cots, w_merge = call(
        cotangent_kernel,
        [((4, TOKENS // 4, D), f32), ((4 * D, 2 * D), bf16)],
        [((TOKENS // 4, 2 * D), bf16), pltpu.SemaphoreType.DMA((2,))],
        [1, 0, 1],
    )(after(g_merged, to_lat), gain_merge, w_merge)
    d_summed, edge, merge_normed = call(
        pair_kernel,
        [((TOKENS, D), bf16), ((EDGE, D), bf16), ((4, TOKENS // 4, D), bf16)],
        [((ROWS, COLS, D), f32), ((4, TOKENS // 4, D), f32)],
    )(tok, main, *beside, gain_merge, cots, pair, unpair)
    beside = fetch(d_summed[:TOP], edge, edge[:SIDE])
    (merged,) = call(merge_kernel, [((TOKENS // 4, 2 * D), bf16)])(merge_normed, w_merge)
    up0, dqkv0, xst, mixt = call(
        inner_back_kernel,
        [((INNER, D), bf16), ((INNER, 3 * D), bf16), ((D, WIDTH), bf16), ((D, WIDTH), bf16)],
        [((INNER, D), bf16)],
    )(d_summed, qkv0, probs0, w_proj, pick, xs0, xs1, mixed0, mixed1)
    dqkv, keep, sent = call(
        outer_back_kernel,
        [((WIDTH, 3 * D), bf16), ((4, 32, 32, 128), bf16), ((4, 32, 32, 128), bf16)],
        [((WIDTH, D), bf16), ((OUTER, D), bf16)],
    )(d_summed, *beside, xst, mixt, after(up0, merged), dqkv0, qkv1, probs1, w_proj, pick)
    main, to_lat, to_lon = call(cells_back_kernel, SCATTERED, [((WIDTH, D), bf16)])(dqkv, w_qkv, back)

    def finish(ready):
        beside = hand_on(after(to_lat, ready), after(to_lon, ready))
        (grad_tokens,) = call(tokens_kernel, [((TOKENS, D), bf16)], [((ROWS, COLS, D), f32)])(
            tok, d_summed, main, *beside, gain
        )
        return merged, grad_tokens, beside

    return finish, keep, sent, to_lat


def solution(mesh):
    lats, lons = mesh.shape["lat"], mesh.shape["lon"]
    count = lats * lons

    def send(block, down, right):
        route = [
            (i, (i // lons + down) % lats * lons + (i % lons + right) % lons) for i in range(count)
        ]
        return lax.ppermute(block, ("lat", "lon"), route)

    def fetch(top, edge, corner):
        return send(top, -1, 0), send(edge, 0, -1), send(corner, -1, -1)

    def hand_on(lat, lon):
        return send(lat, 1, 0), send(lon, 0, 1), send(lon[SIDE:], 1, 1)

    def place(i):
        lat, lon = divmod(i, lons)
        return lat // 8, lat % 8, lon // 8, lon // 2 % 4, lon % 2

    def across(i, step):
        high, z, low, x, core = place(i)
        if core:
            high, low = divmod((high * 2 + low) ^ step, 2)
        else:
            x = x ^ step
        return (high * 8 + z) * lons + low * 8 + x * 2 + core

    rest = {}
    for i in range(count):
        high, z, low, x, core = place(i)
        rest.setdefault((core, high * 2 + low if core else x), []).append(i)
    rest = list(rest.values())

    def swap(block, step):
        return lax.ppermute(block, ("lat", "lon"), [(i, across(i, step)) for i in range(count)])

    def reduce_across(keep, sent, ready):
        other = lax.ppermute(sent, ("lat", "lon"), [(i, i ^ 1) for i in range(count)])
        whole, pair, half = ((32, 32, 128), bf16), ((2, 16, 32, 128), bf16), ((16, 32, 128), bf16)
        own, later, first, second = call(add_kernel, [whole, pair, pair, pair])(keep, after(other, ready))
        own, to_third, to_first = call(relay_kernel, [whole, half, half])(
            own, later, swap(first, 1), swap(second, 3)
        )
        return call(join_kernel, [whole])(own, swap(to_third, 3), swap(to_first, 1))[0], later

    def reduce_rest(sums):
        parts = lax.all_to_all(sums, ("lat", "lon"), 0, 0, axis_index_groups=rest, tiled=True)
        return call(sum_kernel, [((32, 128), f32)])(parts)[0]

    def body(tokens, gain_attn, w_qkv, w_proj, gain_merge, w_merge, g_merged):
        finish, keep, sent, ready = chain(
            tokens.reshape(TOKENS, D), gain_attn.reshape(1, D), w_qkv, w_proj, gain_merge.reshape(4, 1, D),
            w_merge, g_merged.reshape(TOKENS // 4, 2 * D), fetch, hand_on,
        )
        sums, sending = reduce_across(keep, sent, ready)
        merged, grad_tokens, beside = finish(sending)
        grad_weights = reduce_rest(after(sums, *beside))
        return (
            merged.reshape(ROWS // 2, COLS // 2, 2 * D),
            grad_tokens.reshape(ROWS, COLS, D),
            grad_weights,
        )

    return jax.shard_map(
        body,
        mesh=mesh,
        in_specs=(P("lat", "lon", None), P(), P(), P(), P(), P(), P("lat", "lon", None)),
        out_specs=(P("lat", "lon", None), P("lat", "lon", None), P("lat", "lon")),
        check_vma=False,
    )
```

```python
import jax
import jax.numpy as jnp
import numpy as np
from jax import lax
from jax.experimental import pallas as pl
from jax.experimental.pallas import tpu as pltpu
from jax.sharding import PartitionSpec as P

D = 512
HEADS = 8
HEAD = D // HEADS
WIN_LAT = 6
WIN_LON = 12
SHIFT_LAT = 3
SHIFT_LON = 6
EPS = 1e-05

ROWS, COLS = 12, 48
BORDER = 8
TOKENS = ROWS * COLS
LEN = WIN_LAT * WIN_LON
PAD = 80
PER_BAND = COLS // WIN_LON
BAND = PER_BAND * PAD
WINDOWS = 2 * PER_BAND
TOP = SHIFT_LAT * COLS
EDGE = ROWS * BORDER
CORNER = SHIFT_LAT * BORDER
SIDE = WIN_LAT * BORDER
BAND_CELLS = WIN_LAT * COLS
GROUP = HEADS // 2
GROUP_WIDTH = GROUP * HEAD
LOCAL = PER_BAND - 1
INNER = LOCAL * PAD
REST = WINDOWS - LOCAL
OUTER = REST * PAD
PAIR_ROWS, PAIR_COLS = ROWS // 2, COLS // 2
PAIRS = PAIR_ROWS * PAIR_COLS
PAIR_TOP = 2 * PAIR_COLS
PAIR_SIDE = PAIR_ROWS * BORDER
PAIR_CORNER = 2 * BORDER
HELD = 10
WIDTH = WINDOWS * PAD
NEG = -1e30

f32 = jnp.float32
bf16 = jnp.bfloat16


def band_selector():
    pick = np.zeros((BAND, BAND_CELLS), np.float32)
    for win in range(PER_BAND):
        for i in range(WIN_LAT):
            for j in range(WIN_LON):
                pick[win * PAD + i * WIN_LON + j, i * COLS + win * WIN_LON + j] = 1.0
    return pick


def shift_selector(rows, cols, shift):
    pick = np.zeros((rows * cols, rows * (cols + BORDER)), np.float32)
    for i in range(rows):
        for j in range(cols):
            col = j + shift
            pick[i * cols + j, i * cols + col if col < cols else rows * cols + i * BORDER + col - cols] = 1.0
    return pick


def pair_selector():
    pick = np.zeros((4 * COLS, 4 * COLS), np.float32)
    quarter = COLS
    for a in range(2):
        for b in range(COLS // 2):
            for k, (i, j) in enumerate(((0, 0), (1, 0), (0, 1), (1, 1))):
                pick[k * quarter + a * (COLS // 2) + b, (2 * a + i) * COLS + 2 * b + j] = 1.0
    return pick


def dot(a, b):
    return lax.dot_general(a, b, (((1,), (0,)), ((), ())), preferred_element_type=f32)


def dot_nt(a, b):
    return lax.dot_general(a, b, (((1,), (1,)), ((), ())), preferred_element_type=f32)


def dot_tn(a, b):
    return lax.dot_general(a, b, (((0,), (0,)), ((), ())), preferred_element_type=f32)


def norm_parts(values):
    centred = values - jnp.mean(values, axis=-1, keepdims=True)
    scale = lax.rsqrt(jnp.mean(centred * centred, axis=-1, keepdims=True) + EPS)
    return centred * scale, scale


def band_sources(cells, lat, lon, diag):
    first = jnp.concatenate([cells[:BAND_CELLS], lon[CORNER : CORNER + SIDE].astype(bf16)], axis=0)
    beside = jnp.concatenate([lon[CORNER + SIDE : EDGE], diag[:CORNER]], axis=0).astype(bf16)
    second = jnp.concatenate([cells[BAND_CELLS:], lat, beside], axis=0)
    return first, second


def halves(block):
    return jnp.concatenate([block[:, :D], block[:, D:]], axis=0)


def head_masks():
    lane = lax.broadcasted_iota(jnp.int32, (1, GROUP_WIDTH), 1) // HEAD
    return [(lane == h).astype(f32).astype(bf16) for h in range(GROUP)]


def spread_heads(block, masks):
    return jnp.concatenate([block * m for m in masks], axis=0)


def per_head(stacked, block):
    first = lax.broadcasted_iota(jnp.int32, (1, 2 * HEAD), 1) < HEAD
    all_heads = dot_tn(stacked, block)
    out = []
    for pair in range(GROUP // 2):
        part = all_heads[:, pair * 2 * HEAD : (pair + 1) * 2 * HEAD]
        at = pair * 2 * PAD
        out.append(jnp.where(first, part[at : at + PAD], part[at + PAD : at + 2 * PAD]))
    return jnp.concatenate(out, axis=1)


def last_band():
    at_end = lax.axis_index("lat") == lax.axis_size("lat") - 1
    return jnp.where(at_end, f32(1), f32(0))


def halves_apart():
    shape = (LEN, GROUP * PAD)
    key = lax.broadcasted_iota(jnp.int32, shape, 0)
    query = lax.rem(lax.broadcasted_iota(jnp.int32, shape, 1), PAD)
    return jnp.where((key < LEN // 2) != (query < LEN // 2), f32(NEG), f32(0)) * last_band()


def attend(windows, qkv_ref, mixed_ref, probs_ref):
    masks = [m * HEAD ** (-0.5) for m in head_masks()]
    apart = halves_apart() if any(windows) else None
    for win, wraps in enumerate(windows):
        rows = pl.ds(win * PAD, PAD)
        for g in range(2):
            at = g * GROUP_WIDTH
            queries = spread_heads(qkv_ref[rows, at : at + GROUP_WIDTH], masks)
            keys = qkv_ref[rows, D + at : D + at + GROUP_WIDTH]
            values = qkv_ref[rows, 2 * D + at : 2 * D + at + GROUP_WIDTH]
            scores = dot_nt(keys, queries)[:LEN]
            if wraps:
                scores = scores + apart
            weights = jnp.exp(scores - jnp.max(scores, axis=0, keepdims=True))
            probs = weights * (1.0 / jnp.sum(weights, axis=0, keepdims=True))
            probs = jnp.concatenate([probs, jnp.zeros((PAD - LEN, GROUP * PAD), f32)], axis=0)
            probs_ref[win, g] = probs
            mixed_ref[rows, at : at + GROUP_WIDTH] = per_head(probs.astype(bf16), values).astype(bf16)


def attend_back(windows, dmix_ref, dqkv_ref, offset):
    masks = head_masks()
    scaled = [m * HEAD ** (-0.5) for m in masks]
    for win, (qkv_ref, probs_ref, place) in enumerate(windows):
        rows = pl.ds(place * PAD, PAD)
        out = pl.ds(offset + win * PAD, PAD)
        for g in range(2):
            at = g * GROUP_WIDTH
            queries = spread_heads(qkv_ref[rows, at : at + GROUP_WIDTH], scaled)
            keys = qkv_ref[rows, D + at : D + at + GROUP_WIDTH]
            values = qkv_ref[rows, 2 * D + at : 2 * D + at + GROUP_WIDTH]
            above = spread_heads(dmix_ref[pl.ds(win * PAD, PAD), at : at + GROUP_WIDTH], masks)
            probs = probs_ref[place, g]
            d_probs = dot_nt(values, above)
            along = jnp.sum(probs * d_probs, axis=0, keepdims=True)
            d_scores = (probs * (d_probs - along)).astype(bf16)
            d_queries = per_head(d_scores, keys) * HEAD ** (-0.5)
            d_keys = dot(d_scores, queries)
            d_values = dot(probs.astype(bf16), above)
            dqkv_ref[out, at : at + GROUP_WIDTH] = d_queries.astype(bf16)
            dqkv_ref[out, D + at : D + at + GROUP_WIDTH] = d_keys.astype(bf16)
            dqkv_ref[out, 2 * D + at : 2 * D + at + GROUP_WIDTH] = d_values.astype(bf16)


def border_kernel(tok_ref, g_ref, own_ref, own_g_ref, top_ref, edge_ref, corner_ref, sem):
    copies = [
        pltpu.make_async_copy(tok_ref, own_ref, sem.at[0]),
        pltpu.make_async_copy(g_ref, own_g_ref, sem.at[1]),
    ]
    for copy in copies:
        copy.start()
    for copy in copies:
        copy.wait()
    edge = [own_ref[row * COLS : row * COLS + 16].astype(f32)[:BORDER] for row in range(ROWS)]
    cots = own_g_ref[...].astype(f32)
    side = [cots[row * PAIR_COLS : row * PAIR_COLS + BORDER] for row in range(PAIR_ROWS)]
    top_ref[:TOP] = own_ref[:TOP]
    top_ref[TOP:] = halves(own_g_ref[:PAIR_TOP])
    edge_ref[:EDGE] = jnp.concatenate(edge, axis=0).astype(bf16)
    edge_ref[EDGE:] = halves(jnp.concatenate(side, axis=0).astype(bf16))
    corner_ref[:SIDE] = jnp.concatenate(edge[:WIN_LAT], axis=0).astype(bf16)
    corner_ref[SIDE:] = halves(jnp.concatenate(side[:2], axis=0).astype(bf16))


def inner_kernel(tok_ref, *refs):
    held, got = refs[:HELD], refs[HELD : 2 * HELD]
    cells_ref, xs_ref, qkv_ref, mixed_ref, probs_ref, att_ref, sem = refs[2 * HELD :]
    copies = [pltpu.make_async_copy(a, b, sem.at[i]) for i, (a, b) in enumerate(zip(held, got))]
    for copy in copies:
        copy.start()
    gain_ref, pick_ref, wqkv_ref, wproj_ref = got[:4]
    normed = norm_parts(tok_ref[TOP:].astype(f32))[0]
    for copy in copies:
        copy.wait()
    cells_ref[...] = (normed * gain_ref[...]).astype(bf16)
    xs_ref[...] = dot(pick_ref[:INNER, :BAND_CELLS], cells_ref[:BAND_CELLS]).astype(bf16)
    qkv_ref[...] = dot(xs_ref[...], wqkv_ref[...]).astype(bf16)
    attend([False] * LOCAL, qkv_ref, mixed_ref, probs_ref)
    att_ref[...] = dot(mixed_ref[...], wproj_ref[...]).astype(bf16)


def outer_kernel(
    tok_ref, cells_ref, lat_ref, lon_ref, diag_ref, gain_ref, wqkv_ref, wproj_ref, pick_ref, shift_ref, cells_pick_ref,
    att0_ref,
    xs_ref, qkv_ref, mixed_ref, probs_ref, tok_out_ref, summed_ref, row_ref,
    att_ref,
):
    def normed(values):
        return norm_parts(values)[0] * gain_ref[...]

    lat, lon, diag = lat_ref[:TOP], lon_ref[:EDGE].astype(f32), diag_ref[:SIDE].astype(f32)
    first, second = band_sources(cells_ref[...], normed(lat.astype(f32)).astype(bf16), normed(lon), normed(diag))
    xs_ref[:PAD] = dot(pick_ref[INNER:], first).astype(bf16)
    xs_ref[PAD:] = dot(pick_ref[...], second).astype(bf16)
    qkv_ref[...] = dot(xs_ref[...], wqkv_ref[...]).astype(bf16)
    attend([False] + [True] * PER_BAND, qkv_ref, mixed_ref, probs_ref)
    att_ref[:INNER] = att0_ref[...]
    att_ref[INNER:] = dot(mixed_ref[...], wproj_ref[...]).astype(bf16)
    for band, source in enumerate(band_sources(tok_ref[TOP:], lat, lon, diag)):
        rows = pl.ds(band * BAND_CELLS, BAND_CELLS)
        tokens = dot(shift_ref[...], source)
        added = dot(cells_pick_ref[...], att_ref[pl.ds(band * BAND, BAND)])
        tok_out_ref[rows] = tokens.astype(bf16)
        summed_ref[rows] = (tokens + added).astype(bf16)
    row_ref[...] = summed_ref[:COLS]


def cotangent_kernel(
    g_ref, lat_ref, lon_ref, diag_ref, gain_ref, shift_ref, wmerge_ref, out_ref, weights_ref, sem
):
    copy = pltpu.make_async_copy(wmerge_ref, weights_ref, sem)
    copy.start()
    parts = []
    for half in range(2):
        lat = lat_ref[TOP + half * PAIR_TOP : TOP + (half + 1) * PAIR_TOP]
        at = EDGE + half * PAIR_SIDE
        lon = lon_ref[at + PAIR_CORNER : at + PAIR_SIDE]
        diag = diag_ref[SIDE + half * PAIR_CORNER : SIDE + (half + 1) * PAIR_CORNER]
        own = g_ref[PAIR_TOP:, half * D : (half + 1) * D]
        parts.append(dot(shift_ref[...], jnp.concatenate([own, lat, lon, diag], axis=0)).astype(bf16))
    cots = jnp.concatenate(parts, axis=1)
    copy.wait()
    for k in range(4):
        out_ref[k] = dot_nt(cots, weights_ref[k * D : (k + 1) * D]) * gain_ref[k]


def pair_kernel(
    summed_ref, row_ref, gain_ref, cot_ref, pair_ref, unpair_ref,
    dsum_ref, out_row_ref, normed_ref,
    members_ref,
):
    quarter = COLS
    for part in range(3):
        first = COLS + part * 4 * COLS
        if part < 2:
            summed = summed_ref[first : first + 4 * COLS]
        else:
            summed = jnp.concatenate([summed_ref[first:], row_ref[...]], axis=0)
        paired = dot(pair_ref[...], summed)
        for k in range(4):
            members_ref[k, pl.ds(part * quarter, quarter)] = paired[k * quarter : (k + 1) * quarter]
    width = 4 * D
    total = sum(jnp.sum(members_ref[k], axis=-1, keepdims=True) for k in range(4))
    center = total / width
    for k in range(4):
        members_ref[k] = members_ref[k] - center
    spread = sum(jnp.sum(members_ref[k] * members_ref[k], axis=-1, keepdims=True) for k in range(4)) / width
    scale = lax.rsqrt(spread + EPS)
    for k in range(4):
        members_ref[k] = members_ref[k] * scale
        normed_ref[k] = (members_ref[k] * gain_ref[k]).astype(bf16)
    flat = sum(jnp.sum(cot_ref[k], axis=-1, keepdims=True) for k in range(4)) / width
    along = sum(jnp.sum(cot_ref[k] * members_ref[k], axis=-1, keepdims=True) for k in range(4)) / width
    for k in range(4):
        members_ref[k] = (cot_ref[k] - flat - members_ref[k] * along) * scale
    for part in range(3):
        rows = pl.ds(part * quarter, quarter)
        block = jnp.concatenate([members_ref[k, rows].astype(bf16) for k in range(4)], axis=0)
        dsum_ref[pl.ds(part * 4 * COLS, 4 * COLS)] = dot(unpair_ref[...], block).astype(bf16)
    out_row_ref[...] = dsum_ref[TOKENS - COLS :]


def merge_kernel(normed_ref, wmerge_ref, unshift_ref, main_ref, lat_ref, lon_ref, diag_ref):
    total = dot(normed_ref[0], wmerge_ref[:D])
    for k in range(1, 4):
        total = total + dot(normed_ref[k], wmerge_ref[k * D : (k + 1) * D])
    pairs = dot(unshift_ref[...], total.astype(bf16)).astype(bf16)
    main_ref[...] = pairs[: PAIRS - PAIR_TOP]
    lat_ref[...] = halves(pairs[PAIRS - PAIR_TOP : PAIRS])
    lon_ref[...] = halves(pairs[PAIRS : PAIRS + PAIR_SIDE - PAIR_CORNER])
    diag_ref[...] = halves(pairs[PAIRS + PAIR_SIDE - PAIR_CORNER :])


def inner_back_kernel(
    dsum_ref, qkv_ref, probs_ref, wproj_ref, pick_ref, xs0_ref, xs_ref, mixed0_ref, mixed_ref,
    up_ref, dqkv_ref, xst_ref, mixt_ref,
    dmix_ref,
):
    xst_ref[...] = jnp.concatenate([xs0_ref[...], xs_ref[...]], axis=0).T
    mixt_ref[...] = jnp.concatenate([mixed0_ref[...], mixed_ref[...]], axis=0).T
    up_ref[...] = dot(pick_ref[...], dsum_ref[BAND_CELLS - COLS : TOKENS - COLS]).astype(bf16)
    dmix_ref[...] = dot_nt(up_ref[...], wproj_ref[...]).astype(bf16)
    attend_back([(qkv_ref, probs_ref, win) for win in range(1, REST)], dmix_ref, dqkv_ref, 0)


def outer_back_kernel(
    dsum_ref, row_ref, xst_ref, mixt_ref, up1_ref, dqkv1_ref, qkv0_ref, probs0_ref, qkv_ref, probs_ref,
    wproj_ref, pick_ref,
    dqkv_ref, keep_ref, send_ref,
    up_ref, dmix_ref,
):
    cells = jnp.concatenate([row_ref[...], dsum_ref[: BAND_CELLS - COLS]], axis=0)
    up_ref[:BAND] = dot(pick_ref[...], cells).astype(bf16)
    up_ref[BAND:] = up1_ref[...]
    dqkv_ref[BAND:] = dqkv1_ref[...]
    dmix_ref[...] = dot_nt(up_ref[:BAND], wproj_ref[...]).astype(bf16)
    windows = [(qkv0_ref, probs0_ref, win) for win in range(LOCAL)] + [(qkv_ref, probs_ref, 0)]
    attend_back(windows, dmix_ref, dqkv_ref, 0)
    lat_at, lon_at = lax.axis_index("lat"), lax.axis_index("lon")
    even_core = lax.rem(lon_at, 2) == 0
    my_x = lax.rem(lax.div(lon_at, 2), 4)
    my_y = lax.div(lat_at, 8) * 2 + lax.div(lon_at, 8)
    x_steps = [lax.bitwise_xor(my_x, jnp.int32(i)) for i in range(4)]
    y_steps = [lax.bitwise_xor(my_y, jnp.int32(i)) for i in range(4)]
    for col in range(8):
        if col < 6:
            grad = dot(xst_ref[...], dqkv_ref[:, col * 256 : (col + 1) * 256])
        else:
            grad = dot(mixt_ref[...], up_ref[:, (col - 6) * 256 : (col - 5) * 256])
        even, odd = grad[:, :128], grad[:, 128:]
        kept = jnp.where(even_core, even, odd).astype(bf16)
        sent = jnp.where(even_core, odd, even).astype(bf16)
        low, x = divmod(col, 4)
        for lat in range(16):
            high, z = divmod(lat, 8)
            y = high * 2 + low
            rows = slice(lat * 32, (lat + 1) * 32)
            on_even = x_steps[x], lat * 2 + low
            on_odd = y_steps[y], z * 4 + x
            mine = [jnp.where(even_core, a, b) for a, b in zip(on_even, on_odd)]
            other = [jnp.where(even_core, b, a) for a, b in zip(on_even, on_odd)]
            keep_ref[mine[0], mine[1]] = kept[rows]
            send_ref[other[0], other[1]] = sent[rows]


def cells_back_kernel(
    dqkv_ref, wqkv_ref, cells_pick_ref, unshift_ref, tok_ref, dsum_ref, row_ref, gain_ref, m_lat_ref, m_lon_ref, m_diag_ref,
    main_ref, lat_ref, lon_ref, diag_ref,
    dx_ref,
):
    dx_ref[...] = dot_nt(dqkv_ref[...], wqkv_ref[...]).astype(bf16)
    for band in range(2):
        if band == 0:
            above = jnp.concatenate([row_ref[...], dsum_ref[: BAND_CELLS - COLS]], axis=0)
        else:
            above = dsum_ref[BAND_CELLS - COLS : TOKENS - COLS]
        cot = dot(cells_pick_ref[...], dx_ref[pl.ds(band * BAND, BAND)]) * gain_ref[...]
        normed, scale = norm_parts(tok_ref[pl.ds(band * BAND_CELLS, BAND_CELLS)].astype(f32))
        flat = jnp.mean(cot, axis=-1, keepdims=True)
        along = jnp.mean(cot * normed, axis=-1, keepdims=True)
        grads = (above.astype(f32) + (cot - flat - normed * along) * scale).astype(bf16)
        cells = dot(unshift_ref[...], grads).astype(bf16)
        if band == 0:
            main_ref[:BAND_CELLS] = cells[:BAND_CELLS]
        else:
            main_ref[BAND_CELLS:] = cells[: BAND_CELLS - TOP]
            lat_ref[:TOP] = cells[BAND_CELLS - TOP : BAND_CELLS]
            diag_ref[:SIDE] = cells[BAND_CELLS:]
        lon_ref[band * SIDE : (band + 1) * SIDE] = cells[BAND_CELLS:]
    lat_ref[TOP:] = m_lat_ref[...]
    lon_ref[EDGE:] = m_lon_ref[...]
    diag_ref[SIDE:] = m_diag_ref[...]


def fill_edge(field, side, rows, cols):
    width = field.shape[-1]
    field, side = field.astype(f32).reshape(rows, cols, width), side.astype(f32).reshape(rows, BORDER, width)
    first = field[:, :BORDER] + side
    return jnp.concatenate([first, field[:, BORDER:]], axis=1).reshape(rows * cols, width).astype(bf16)


def own_cells_kernel(main_ref, lat_ref, lon_ref, diag_ref, m_main_ref, tokens_ref, merged_ref):
    corner = diag_ref[:SIDE].astype(f32)[SIDE - CORNER :]
    beside = lon_ref[:EDGE].astype(f32)[: EDGE - CORNER]
    tokens_ref[:TOP] = fill_edge(lat_ref[:TOP], corner, SHIFT_LAT, COLS)
    tokens_ref[TOP:] = fill_edge(main_ref[...], beside, ROWS - SHIFT_LAT, COLS)
    side_rows = PAIR_SIDE - PAIR_CORNER
    for half in range(2):
        cols = pl.ds(half * D, D)
        lat = lat_ref[TOP + half * PAIR_TOP : TOP + (half + 1) * PAIR_TOP]
        lon = lon_ref[EDGE + half * side_rows : EDGE + (half + 1) * side_rows]
        diag = diag_ref[SIDE + half * PAIR_CORNER : SIDE + (half + 1) * PAIR_CORNER]
        merged_ref[:PAIR_TOP, cols] = fill_edge(lat, diag, 2, PAIR_COLS)
        merged_ref[PAIR_TOP:, cols] = fill_edge(m_main_ref[:, cols], lon, PAIR_ROWS - 2, PAIR_COLS)


def add_kernel(a_ref, b_ref, own_ref, later_ref, first_ref, second_ref):
    half = own_ref.shape[0] // 2

    def both(k, rows):
        return (a_ref[k, rows].astype(f32) + b_ref[k, rows].astype(f32)).astype(bf16)

    upper, lower = pl.ds(0, half), pl.ds(half, half)
    own_ref[...] = both(0, pl.ds(0, 2 * half))
    first_ref[0], first_ref[1] = both(1, upper), both(2, upper)
    second_ref[0], second_ref[1] = both(3, lower), both(2, lower)
    later_ref[0], later_ref[1] = both(3, upper), both(1, lower)


def relay_kernel(own_ref, later_ref, first_ref, second_ref, out_ref, to_third_ref, to_first_ref):
    half = own_ref.shape[0] // 2

    def both(a, b):
        return (a.astype(f32) + b.astype(f32)).astype(bf16)

    out_ref[:half] = both(own_ref[:half], first_ref[0])
    out_ref[half:] = both(own_ref[half:], second_ref[0])
    to_third_ref[...] = both(later_ref[0], first_ref[1])
    to_first_ref[...] = both(later_ref[1], second_ref[1])


def join_kernel(own_ref, upper_ref, lower_ref, out_ref):
    half = own_ref.shape[0] // 2
    out_ref[:half] = (own_ref[:half].astype(f32) + upper_ref[...].astype(f32)).astype(bf16)
    out_ref[half:] = (own_ref[half:].astype(f32) + lower_ref[...].astype(f32)).astype(bf16)


def sum_kernel(parts_ref, out_ref):
    total = parts_ref[0].astype(f32)
    for i in range(1, parts_ref.shape[0]):
        total = total + parts_ref[i].astype(f32)
    out_ref[...] = total.astype(out_ref.dtype)


def call(kernel, outs, scratch=(), places=None, limit=20):
    spaces = {} if places is None else {
        "in_specs": [pl.BlockSpec(memory_space=(pltpu.VMEM, pl.ANY, pltpu.HBM)[p]) for p in places]
    }
    return pl.pallas_call(
        kernel,
        out_shape=[jax.ShapeDtypeStruct(s, t) for s, t in outs],
        scratch_shapes=[pltpu.VMEM(*s) if isinstance(s, tuple) else s for s in scratch],
        cost_estimate=pl.CostEstimate(flops=10**9, bytes_accessed=2 * 10**6, transcendentals=0),
        compiler_params=pltpu.CompilerParams(vmem_limit_bytes=limit * 1024 * 1024),
        **spaces,
    )


def saved(count):
    rows = count * PAD
    return [((rows, D), bf16), ((rows, 3 * D), bf16), ((rows, D), bf16), ((count, 2, PAD, GROUP * PAD), f32)]


def after(value, *others):
    return lax.optimization_barrier((value, *others))[0]


def chain(tok, gain, w_qkv, w_proj, gain_merge, w_merge, g_merged, fetch, hand_on, up, down):
    tok, g_merged, top, edge, corner = call(
        border_kernel,
        [
            ((TOKENS, D), bf16), ((PAIRS, 2 * D), bf16),
            ((TOP + 2 * PAIR_TOP, D), bf16), ((EDGE + 2 * PAIR_SIDE, D), bf16), ((SIDE + 2 * PAIR_CORNER, D), bf16),
        ],
        [pltpu.SemaphoreType.DMA((2,))],
        [2, 2],
    )(tok, g_merged)
    beside = fetch(top, edge, corner)
    pair, band = pair_selector(), band_selector()
    shift = shift_selector(WIN_LAT, COLS, SHIFT_LON)
    pair_shift = shift_selector(PAIR_ROWS, PAIR_COLS, SHIFT_LON // 2)
    held = [gain, jnp.asarray(band @ shift, bf16), w_qkv, w_proj, gain_merge]
    held += [jnp.asarray(c, bf16) for c in (shift, band.T, pair, pair.T, pair_shift)]
    got = call(
        inner_kernel,
        [(h.shape, h.dtype) for h in held] + [((TOKENS - TOP, D), bf16)] + saved(LOCAL) + [((INNER, D), bf16)],
        [pltpu.SemaphoreType.DMA((HELD,))],
        [0] + [1] * HELD,
    )(tok, *held)
    gain, pick, w_qkv, w_proj, gain_merge, shift, cells_pick, pair, unpair, pair_shift = got[:HELD]
    cells, xs0, qkv0, mixed0, probs0, att0 = got[HELD:]
    xs1, qkv1, mixed1, probs1, tok, summed, row = call(
        outer_kernel,
        saved(REST) + [((TOKENS, D), bf16), ((TOKENS, D), bf16), ((COLS, D), bf16)],
        [((WIDTH, D), bf16)],
    )(tok, cells, *beside, gain, w_qkv, w_proj, pick, shift, cells_pick, att0)
    last = up(row)
    cots, w_merge = call(
        cotangent_kernel,
        [((4, PAIRS, D), f32), ((4 * D, 2 * D), bf16)],
        [pltpu.SemaphoreType.DMA],
        [0] * 6 + [1],
    )(after(g_merged, row), *beside, gain_merge, pair_shift, w_merge)
    d_summed, row, merge_normed = call(
        pair_kernel,
        [((TOKENS, D), bf16), ((COLS, D), bf16), ((4, PAIRS, D), bf16)],
        [((4, PAIRS, D), f32)],
    )(summed, last, gain_merge, cots, pair, unpair)
    first = down(row)
    band = jnp.asarray(band_selector(), bf16)
    unshift = jnp.asarray(shift_selector(WIN_LAT, COLS, SHIFT_LON).T, bf16)
    pair_unshift = jnp.asarray(shift_selector(PAIR_ROWS, PAIR_COLS, SHIFT_LON // 2).T, bf16)
    up1, dqkv1, xst, mixt = call(
        inner_back_kernel,
        [((BAND, D), bf16), ((BAND, 3 * D), bf16), ((D, WIDTH), bf16), ((D, WIDTH), bf16)],
        [((BAND, D), bf16)],
    )(d_summed, qkv1, probs1, w_proj, band, xs0, xs1, mixed0, mixed1)
    m_main, m_lat, m_lon, m_diag = call(
        merge_kernel,
        [
            ((PAIRS - PAIR_TOP, 2 * D), bf16), ((2 * PAIR_TOP, D), bf16),
            ((2 * (PAIR_SIDE - PAIR_CORNER), D), bf16), ((2 * PAIR_CORNER, D), bf16),
        ],
    )(merge_normed, w_merge, pair_unshift)
    dqkv, keep, sent = call(
        outer_back_kernel,
        [((WIDTH, 3 * D), bf16), ((4, 32, 32, 128), bf16), ((4, 32, 32, 128), bf16)],
        [((WIDTH, D), bf16), ((BAND, D), bf16)],
    )(d_summed, first, xst, mixt, up1, dqkv1, qkv0, probs0, qkv1, probs1, w_proj, band)

    def cells_back(ready):
        return call(
            cells_back_kernel,
            [
                ((TOKENS - TOP, D), bf16), ((TOP + 2 * PAIR_TOP, D), bf16),
                ((EDGE + 2 * (PAIR_SIDE - PAIR_CORNER), D), bf16), ((SIDE + 2 * PAIR_CORNER, D), bf16),
            ],
            [((WIDTH, D), bf16)],
        )(after(dqkv, ready), w_qkv, cells_pick, unshift, tok, d_summed, first, gain, m_lat, m_lon, m_diag)

    def finish(main, *pieces):
        grad_tokens, merged = call(own_cells_kernel, [((TOKENS, D), bf16), ((PAIRS, 2 * D), bf16)])(
            main, *hand_on(*pieces), m_main
        )
        return merged, grad_tokens

    return cells_back, finish, keep, sent, m_lat


def solution(mesh):
    lats, lons = mesh.shape["lat"], mesh.shape["lon"]
    count = lats * lons

    def send(block, down, right):
        route = [
            (i, (i // lons + down) % lats * lons + (i % lons + right) % lons) for i in range(count)
        ]
        return lax.ppermute(block, ("lat", "lon"), route)

    def fetch(top, edge, corner):
        return send(top, -1, 0), send(edge, 0, -1), send(corner, -1, -1)

    def hand_on(lat, lon, diag):
        return send(lat, 1, 0), send(lon, 0, 1), send(diag, 1, 1)

    def place(i):
        lat, lon = divmod(i, lons)
        return lat // 8, lat % 8, lon // 8, lon // 2 % 4, lon % 2

    def across(i, step):
        high, z, low, x, core = place(i)
        if core:
            high, low = divmod((high * 2 + low) ^ step, 2)
        else:
            x = x ^ step
        return (high * 8 + z) * lons + low * 8 + x * 2 + core

    rest = {}
    for i in range(count):
        high, z, low, x, core = place(i)
        rest.setdefault((core, high * 2 + low if core else x), []).append(i)
    rest = list(rest.values())

    def swap(block, step):
        return lax.ppermute(block, ("lat", "lon"), [(i, across(i, step)) for i in range(count)])

    def reduce_across(keep, sent, ready, cells_back):
        other = lax.ppermute(sent, ("lat", "lon"), [(i, i ^ 1) for i in range(count)])
        whole, pair, half = ((32, 32, 128), bf16), ((2, 16, 32, 128), bf16), ((16, 32, 128), bf16)
        own, later, first, second = call(add_kernel, [whole, pair, pair, pair])(keep, after(other, ready))
        first, second = swap(first, 1), swap(second, 3)
        pieces = cells_back(later)
        own, to_third, to_first = call(relay_kernel, [whole, half, half])(own, after(later, *pieces), first, second)
        sums = call(join_kernel, [whole])(own, swap(to_third, 3), swap(to_first, 1))[0]
        return sums, [after(piece, sums) for piece in pieces]

    def reduce_rest(sums):
        parts = lax.all_to_all(sums, ("lat", "lon"), 0, 0, axis_index_groups=rest, tiled=True)
        return call(sum_kernel, [((32, 128), f32)])(parts)[0]

    def body(tokens, gain_attn, w_qkv, w_proj, gain_merge, w_merge, g_merged):
        cells_back, finish, keep, sent, ready = chain(
            tokens.reshape(TOKENS, D), gain_attn.reshape(1, D), w_qkv, w_proj, gain_merge.reshape(4, 1, D),
            w_merge, g_merged.reshape(PAIRS, 2 * D), fetch, hand_on,
            lambda row: send(row, -1, 0), lambda row: send(row, 1, 0),
        )
        sums, pieces = reduce_across(keep, sent, ready, cells_back)
        grad_weights = reduce_rest(sums)
        merged, grad_tokens = finish(*pieces)
        return (
            merged.reshape(ROWS // 2, COLS // 2, 2 * D),
            grad_tokens.reshape(ROWS, COLS, D),
            grad_weights,
        )

    return jax.shard_map(
        body,
        mesh=mesh,
        in_specs=(P("lat", "lon", None), P(), P(), P(), P(), P(), P("lat", "lon", None)),
        out_specs=(P("lat", "lon", None), P("lat", "lon", None), P("lat", "lon")),
        check_vma=False,
    )
```

```python
import jax
import jax.numpy as jnp
import numpy as np
from jax import lax
from jax.experimental import pallas as pl
from jax.experimental.pallas import tpu as pltpu
from jax.sharding import PartitionSpec as P

D = 512
HEADS = 8
HEAD = D // HEADS
WIN_LAT = 6
WIN_LON = 12
SHIFT_LAT = 3
SHIFT_LON = 6
EPS = 1e-05

ROWS, COLS = 12, 48
BORDER = 8
TOKENS = ROWS * COLS
LEN = WIN_LAT * WIN_LON
PAD = 80
PER_BAND = COLS // WIN_LON
BAND = PER_BAND * PAD
WINDOWS = 2 * PER_BAND
TOP = SHIFT_LAT * COLS
EDGE = ROWS * BORDER
CORNER = SHIFT_LAT * BORDER
SIDE = WIN_LAT * BORDER
BAND_CELLS = WIN_LAT * COLS
GROUP = HEADS // 2
GROUP_WIDTH = GROUP * HEAD
LOCAL = PER_BAND - 1
INNER = LOCAL * PAD
REST = WINDOWS - LOCAL
OUTER = REST * PAD
PAIR_ROWS, PAIR_COLS = ROWS // 2, COLS // 2
PAIRS = PAIR_ROWS * PAIR_COLS
PAIR_TOP = 2 * PAIR_COLS
PAIR_SIDE = PAIR_ROWS * BORDER
PAIR_CORNER = 2 * BORDER
HELD = 10
WIDTH = WINDOWS * PAD
NEG = -1e30

f32 = jnp.float32
bf16 = jnp.bfloat16


def band_selector():
    pick = np.zeros((BAND, BAND_CELLS), np.float32)
    for win in range(PER_BAND):
        for i in range(WIN_LAT):
            for j in range(WIN_LON):
                pick[win * PAD + i * WIN_LON + j, i * COLS + win * WIN_LON + j] = 1.0
    return pick


def shift_selector(rows, cols, shift):
    pick = np.zeros((rows * cols, rows * (cols + BORDER)), np.float32)
    for i in range(rows):
        for j in range(cols):
            col = j + shift
            pick[i * cols + j, i * cols + col if col < cols else rows * cols + i * BORDER + col - cols] = 1.0
    return pick


def pair_selector():
    pick = np.zeros((4 * COLS, 4 * COLS), np.float32)
    quarter = COLS
    for a in range(2):
        for b in range(COLS // 2):
            for k, (i, j) in enumerate(((0, 0), (1, 0), (0, 1), (1, 1))):
                pick[k * quarter + a * (COLS // 2) + b, (2 * a + i) * COLS + 2 * b + j] = 1.0
    return pick


def dot(a, b):
    return lax.dot_general(a, b, (((1,), (0,)), ((), ())), preferred_element_type=f32)


def dot_nt(a, b):
    return lax.dot_general(a, b, (((1,), (1,)), ((), ())), preferred_element_type=f32)


def dot_tn(a, b):
    return lax.dot_general(a, b, (((0,), (0,)), ((), ())), preferred_element_type=f32)


def norm_parts(values):
    centred = values - jnp.mean(values, axis=-1, keepdims=True)
    scale = lax.rsqrt(jnp.mean(centred * centred, axis=-1, keepdims=True) + EPS)
    return centred * scale, scale


def band_sources(cells, lat, lon, diag):
    first = jnp.concatenate([cells[:BAND_CELLS], lon[CORNER : CORNER + SIDE].astype(bf16)], axis=0)
    beside = jnp.concatenate([lon[CORNER + SIDE : EDGE], diag[:CORNER]], axis=0).astype(bf16)
    second = jnp.concatenate([cells[BAND_CELLS:], lat, beside], axis=0)
    return first, second


def halves(block):
    return jnp.concatenate([block[:, :D], block[:, D:]], axis=0)


def head_masks():
    lane = lax.broadcasted_iota(jnp.int32, (1, GROUP_WIDTH), 1) // HEAD
    return [(lane == h).astype(f32).astype(bf16) for h in range(GROUP)]


def spread_heads(block, masks):
    return jnp.concatenate([block * m for m in masks], axis=0)


def per_head(stacked, block):
    first = lax.broadcasted_iota(jnp.int32, (1, 2 * HEAD), 1) < HEAD
    all_heads = dot_tn(stacked, block)
    out = []
    for pair in range(GROUP // 2):
        part = all_heads[:, pair * 2 * HEAD : (pair + 1) * 2 * HEAD]
        at = pair * 2 * PAD
        out.append(jnp.where(first, part[at : at + PAD], part[at + PAD : at + 2 * PAD]))
    return jnp.concatenate(out, axis=1)


def last_band():
    at_end = lax.axis_index("lat") == lax.axis_size("lat") - 1
    return jnp.where(at_end, f32(1), f32(0))


def halves_apart():
    shape = (LEN, GROUP * PAD)
    key = lax.broadcasted_iota(jnp.int32, shape, 0)
    query = lax.rem(lax.broadcasted_iota(jnp.int32, shape, 1), PAD)
    return jnp.where((key < LEN // 2) != (query < LEN // 2), f32(NEG), f32(0)) * last_band()


def attend(windows, qkv_ref, mixed_ref, probs_ref):
    masks = [m * HEAD ** (-0.5) for m in head_masks()]
    apart = halves_apart() if any(windows) else None
    for win, wraps in enumerate(windows):
        rows = pl.ds(win * PAD, PAD)
        for g in range(2):
            at = g * GROUP_WIDTH
            queries = spread_heads(qkv_ref[rows, at : at + GROUP_WIDTH], masks)
            keys = qkv_ref[rows, D + at : D + at + GROUP_WIDTH]
            values = qkv_ref[rows, 2 * D + at : 2 * D + at + GROUP_WIDTH]
            scores = dot_nt(keys, queries)[:LEN]
            if wraps:
                scores = scores + apart
            weights = jnp.exp(scores - jnp.max(scores, axis=0, keepdims=True))
            probs = weights * (1.0 / jnp.sum(weights, axis=0, keepdims=True))
            probs = jnp.concatenate([probs, jnp.zeros((PAD - LEN, GROUP * PAD), f32)], axis=0)
            probs_ref[win, g] = probs
            mixed_ref[rows, at : at + GROUP_WIDTH] = per_head(probs.astype(bf16), values).astype(bf16)


def attend_back(windows, dmix_ref, dqkv_ref, offset):
    masks = head_masks()
    scaled = [m * HEAD ** (-0.5) for m in masks]
    for win, (qkv_ref, probs_ref, place) in enumerate(windows):
        rows = pl.ds(place * PAD, PAD)
        out = pl.ds(offset + win * PAD, PAD)
        for g in range(2):
            at = g * GROUP_WIDTH
            queries = spread_heads(qkv_ref[rows, at : at + GROUP_WIDTH], scaled)
            keys = qkv_ref[rows, D + at : D + at + GROUP_WIDTH]
            values = qkv_ref[rows, 2 * D + at : 2 * D + at + GROUP_WIDTH]
            above = spread_heads(dmix_ref[pl.ds(win * PAD, PAD), at : at + GROUP_WIDTH], masks)
            probs = probs_ref[place, g]
            d_probs = dot_nt(values, above)
            along = jnp.sum(probs * d_probs, axis=0, keepdims=True)
            d_scores = (probs * (d_probs - along)).astype(bf16)
            d_queries = per_head(d_scores, keys) * HEAD ** (-0.5)
            d_keys = dot(d_scores, queries)
            d_values = dot(probs.astype(bf16), above)
            dqkv_ref[out, at : at + GROUP_WIDTH] = d_queries.astype(bf16)
            dqkv_ref[out, D + at : D + at + GROUP_WIDTH] = d_keys.astype(bf16)
            dqkv_ref[out, 2 * D + at : 2 * D + at + GROUP_WIDTH] = d_values.astype(bf16)


def border_kernel(tok_ref, g_ref, own_ref, own_g_ref, top_ref, edge_ref, corner_ref, sem):
    copies = [
        pltpu.make_async_copy(tok_ref, own_ref, sem.at[0]),
        pltpu.make_async_copy(g_ref, own_g_ref, sem.at[1]),
    ]
    for copy in copies:
        copy.start()
    for copy in copies:
        copy.wait()
    edge = [own_ref[row * COLS : row * COLS + 16].astype(f32)[:BORDER] for row in range(ROWS)]
    cots = own_g_ref[...].astype(f32)
    side = [cots[row * PAIR_COLS : row * PAIR_COLS + BORDER] for row in range(PAIR_ROWS)]
    top_ref[:TOP] = own_ref[:TOP]
    top_ref[TOP:] = halves(own_g_ref[:PAIR_TOP])
    edge_ref[:EDGE] = jnp.concatenate(edge, axis=0).astype(bf16)
    edge_ref[EDGE:] = halves(jnp.concatenate(side, axis=0).astype(bf16))
    corner_ref[:SIDE] = jnp.concatenate(edge[:WIN_LAT], axis=0).astype(bf16)
    corner_ref[SIDE:] = halves(jnp.concatenate(side[:2], axis=0).astype(bf16))


def inner_kernel(tok_ref, *refs):
    held, got = refs[:HELD], refs[HELD : 2 * HELD]
    cells_ref, xs_ref, qkv_ref, mixed_ref, probs_ref, att_ref, sem = refs[2 * HELD :]
    copies = [pltpu.make_async_copy(a, b, sem.at[i]) for i, (a, b) in enumerate(zip(held, got))]
    for copy in copies:
        copy.start()
    gain_ref, pick_ref, wqkv_ref, wproj_ref = got[:4]
    normed = norm_parts(tok_ref[TOP:].astype(f32))[0]
    for copy in copies:
        copy.wait()
    cells_ref[...] = (normed * gain_ref[...]).astype(bf16)
    xs_ref[...] = dot(pick_ref[:INNER, :BAND_CELLS], cells_ref[:BAND_CELLS]).astype(bf16)
    qkv_ref[...] = dot(xs_ref[...], wqkv_ref[...]).astype(bf16)
    attend([False] * LOCAL, qkv_ref, mixed_ref, probs_ref)
    att_ref[...] = dot(mixed_ref[...], wproj_ref[...]).astype(bf16)


def outer_kernel(
    tok_ref, cells_ref, lat_ref, lon_ref, diag_ref, gain_ref, wqkv_ref, wproj_ref, pick_ref, shift_ref, cells_pick_ref,
    att0_ref,
    xs_ref, qkv_ref, mixed_ref, probs_ref, tok_out_ref, summed_ref, row_ref,
    att_ref,
):
    def normed(values):
        return norm_parts(values)[0] * gain_ref[...]

    lat, lon, diag = lat_ref[:TOP], lon_ref[:EDGE].astype(f32), diag_ref[:SIDE].astype(f32)
    first, second = band_sources(cells_ref[...], normed(lat.astype(f32)).astype(bf16), normed(lon), normed(diag))
    xs_ref[:PAD] = dot(pick_ref[INNER:], first).astype(bf16)
    xs_ref[PAD:] = dot(pick_ref[...], second).astype(bf16)
    qkv_ref[...] = dot(xs_ref[...], wqkv_ref[...]).astype(bf16)
    attend([False] + [True] * PER_BAND, qkv_ref, mixed_ref, probs_ref)
    att_ref[:INNER] = att0_ref[...]
    att_ref[INNER:] = dot(mixed_ref[...], wproj_ref[...]).astype(bf16)
    for band, source in enumerate(band_sources(tok_ref[TOP:], lat, lon, diag)):
        rows = pl.ds(band * BAND_CELLS, BAND_CELLS)
        tokens = dot(shift_ref[...], source)
        added = dot(cells_pick_ref[...], att_ref[pl.ds(band * BAND, BAND)])
        tok_out_ref[rows] = tokens.astype(bf16)
        summed_ref[rows] = (tokens + added).astype(bf16)
    row_ref[...] = summed_ref[:COLS]


def cotangent_kernel(
    g_ref, lat_ref, lon_ref, diag_ref, gain_ref, shift_ref, wmerge_ref, out_ref, weights_ref, sem
):
    copy = pltpu.make_async_copy(wmerge_ref, weights_ref, sem)
    copy.start()
    parts = []
    for half in range(2):
        lat = lat_ref[TOP + half * PAIR_TOP : TOP + (half + 1) * PAIR_TOP]
        at = EDGE + half * PAIR_SIDE
        lon = lon_ref[at + PAIR_CORNER : at + PAIR_SIDE]
        diag = diag_ref[SIDE + half * PAIR_CORNER : SIDE + (half + 1) * PAIR_CORNER]
        own = g_ref[PAIR_TOP:, half * D : (half + 1) * D]
        parts.append(dot(shift_ref[...], jnp.concatenate([own, lat, lon, diag], axis=0)).astype(bf16))
    cots = jnp.concatenate(parts, axis=1)
    copy.wait()
    for k in range(4):
        out_ref[k] = dot_nt(cots, weights_ref[k * D : (k + 1) * D]) * gain_ref[k]


def pair_kernel(
    summed_ref, row_ref, gain_ref, cot_ref, pair_ref, unpair_ref,
    dsum_ref, out_row_ref, normed_ref,
    members_ref,
):
    quarter = COLS
    for part in range(3):
        first = COLS + part * 4 * COLS
        if part < 2:
            summed = summed_ref[first : first + 4 * COLS]
        else:
            summed = jnp.concatenate([summed_ref[first:], row_ref[...]], axis=0)
        paired = dot(pair_ref[...], summed)
        for k in range(4):
            members_ref[k, pl.ds(part * quarter, quarter)] = paired[k * quarter : (k + 1) * quarter]
    width = 4 * D
    total = sum(jnp.sum(members_ref[k], axis=-1, keepdims=True) for k in range(4))
    center = total / width
    for k in range(4):
        members_ref[k] = members_ref[k] - center
    spread = sum(jnp.sum(members_ref[k] * members_ref[k], axis=-1, keepdims=True) for k in range(4)) / width
    scale = lax.rsqrt(spread + EPS)
    for k in range(4):
        members_ref[k] = members_ref[k] * scale
        normed_ref[k] = (members_ref[k] * gain_ref[k]).astype(bf16)
    flat = sum(jnp.sum(cot_ref[k], axis=-1, keepdims=True) for k in range(4)) / width
    along = sum(jnp.sum(cot_ref[k] * members_ref[k], axis=-1, keepdims=True) for k in range(4)) / width
    for k in range(4):
        members_ref[k] = (cot_ref[k] - flat - members_ref[k] * along) * scale
    for part in range(3):
        rows = pl.ds(part * quarter, quarter)
        block = jnp.concatenate([members_ref[k, rows].astype(bf16) for k in range(4)], axis=0)
        dsum_ref[pl.ds(part * 4 * COLS, 4 * COLS)] = dot(unpair_ref[...], block).astype(bf16)
    out_row_ref[...] = dsum_ref[TOKENS - COLS :]


def merge_kernel(normed_ref, wmerge_ref, unshift_ref, main_ref, lat_ref, lon_ref, diag_ref):
    total = dot(normed_ref[0], wmerge_ref[:D])
    for k in range(1, 4):
        total = total + dot(normed_ref[k], wmerge_ref[k * D : (k + 1) * D])
    pairs = dot(unshift_ref[...], total.astype(bf16)).astype(bf16)
    main_ref[...] = pairs[: PAIRS - PAIR_TOP]
    lat_ref[...] = halves(pairs[PAIRS - PAIR_TOP : PAIRS])
    lon_ref[...] = halves(pairs[PAIRS : PAIRS + PAIR_SIDE - PAIR_CORNER])
    diag_ref[...] = halves(pairs[PAIRS + PAIR_SIDE - PAIR_CORNER :])


def inner_back_kernel(
    dsum_ref, qkv_ref, probs_ref, wproj_ref, pick_ref, xs0_ref, xs_ref, mixed0_ref, mixed_ref,
    up_ref, dqkv_ref, xst_ref, mixt_ref,
    dmix_ref,
):
    xst_ref[...] = jnp.concatenate([xs0_ref[...], xs_ref[...]], axis=0).T
    mixt_ref[...] = jnp.concatenate([mixed0_ref[...], mixed_ref[...]], axis=0).T
    up_ref[...] = dot(pick_ref[...], dsum_ref[BAND_CELLS - COLS : TOKENS - COLS]).astype(bf16)
    dmix_ref[...] = dot_nt(up_ref[...], wproj_ref[...]).astype(bf16)
    attend_back([(qkv_ref, probs_ref, win) for win in range(1, REST)], dmix_ref, dqkv_ref, 0)


def outer_back_kernel(
    dsum_ref, row_ref, xst_ref, mixt_ref, up1_ref, dqkv1_ref, qkv0_ref, probs0_ref, qkv_ref, probs_ref,
    wproj_ref, pick_ref,
    dqkv_ref, keep_ref, send_ref,
    up_ref, dmix_ref,
):
    cells = jnp.concatenate([row_ref[...], dsum_ref[: BAND_CELLS - COLS]], axis=0)
    up_ref[:BAND] = dot(pick_ref[...], cells).astype(bf16)
    up_ref[BAND:] = up1_ref[...]
    dqkv_ref[BAND:] = dqkv1_ref[...]
    dmix_ref[...] = dot_nt(up_ref[:BAND], wproj_ref[...]).astype(bf16)
    windows = [(qkv0_ref, probs0_ref, win) for win in range(LOCAL)] + [(qkv_ref, probs_ref, 0)]
    attend_back(windows, dmix_ref, dqkv_ref, 0)
    lat_at, lon_at = lax.axis_index("lat"), lax.axis_index("lon")
    even_core = lax.rem(lon_at, 2) == 0
    my_x = lax.rem(lax.div(lon_at, 2), 4)
    my_y = lax.div(lat_at, 8) * 2 + lax.div(lon_at, 8)
    x_steps = [lax.bitwise_xor(my_x, jnp.int32(i)) for i in range(4)]
    y_steps = [lax.bitwise_xor(my_y, jnp.int32(i)) for i in range(4)]
    for col in range(8):
        if col < 6:
            grad = dot(xst_ref[...], dqkv_ref[:, col * 256 : (col + 1) * 256])
        else:
            grad = dot(mixt_ref[...], up_ref[:, (col - 6) * 256 : (col - 5) * 256])
        even, odd = grad[:, :128], grad[:, 128:]
        kept = jnp.where(even_core, even, odd).astype(bf16)
        sent = jnp.where(even_core, odd, even).astype(bf16)
        low, x = divmod(col, 4)
        for lat in range(16):
            high, z = divmod(lat, 8)
            y = high * 2 + low
            rows = slice(lat * 32, (lat + 1) * 32)
            on_even = x_steps[x], lat * 2 + low
            on_odd = y_steps[y], z * 4 + x
            mine = [jnp.where(even_core, a, b) for a, b in zip(on_even, on_odd)]
            other = [jnp.where(even_core, b, a) for a, b in zip(on_even, on_odd)]
            keep_ref[mine[0], mine[1]] = kept[rows]
            send_ref[other[0], other[1]] = sent[rows]


def cells_back_kernel(
    dqkv_ref, wqkv_ref, cells_pick_ref, unshift_ref, tok_ref, dsum_ref, row_ref, gain_ref, m_lat_ref, m_lon_ref, m_diag_ref,
    main_ref, lat_ref, lon_ref, diag_ref,
    dx_ref,
):
    dx_ref[...] = dot_nt(dqkv_ref[...], wqkv_ref[...]).astype(bf16)
    for band in range(2):
        if band == 0:
            above = jnp.concatenate([row_ref[...], dsum_ref[: BAND_CELLS - COLS]], axis=0)
        else:
            above = dsum_ref[BAND_CELLS - COLS : TOKENS - COLS]
        cot = dot(cells_pick_ref[...], dx_ref[pl.ds(band * BAND, BAND)]) * gain_ref[...]
        normed, scale = norm_parts(tok_ref[pl.ds(band * BAND_CELLS, BAND_CELLS)].astype(f32))
        flat = jnp.mean(cot, axis=-1, keepdims=True)
        along = jnp.mean(cot * normed, axis=-1, keepdims=True)
        grads = (above.astype(f32) + (cot - flat - normed * along) * scale).astype(bf16)
        cells = dot(unshift_ref[...], grads).astype(bf16)
        if band == 0:
            main_ref[:BAND_CELLS] = cells[:BAND_CELLS]
        else:
            main_ref[BAND_CELLS:] = cells[: BAND_CELLS - TOP]
            lat_ref[:TOP] = cells[BAND_CELLS - TOP : BAND_CELLS]
            diag_ref[:SIDE] = cells[BAND_CELLS:]
        lon_ref[band * SIDE : (band + 1) * SIDE] = cells[BAND_CELLS:]
    lat_ref[TOP:] = m_lat_ref[...]
    lon_ref[EDGE:] = m_lon_ref[...]
    diag_ref[SIDE:] = m_diag_ref[...]


def fill_edge(field, side, rows, cols):
    width = field.shape[-1]
    field, side = field.astype(f32).reshape(rows, cols, width), side.astype(f32).reshape(rows, BORDER, width)
    first = field[:, :BORDER] + side
    return jnp.concatenate([first, field[:, BORDER:]], axis=1).reshape(rows * cols, width).astype(bf16)


def own_cells_kernel(main_ref, lat_ref, lon_ref, diag_ref, m_main_ref, tokens_ref, merged_ref):
    corner = diag_ref[:SIDE].astype(f32)[SIDE - CORNER :]
    beside = lon_ref[:EDGE].astype(f32)[: EDGE - CORNER]
    tokens_ref[:TOP] = fill_edge(lat_ref[:TOP], corner, SHIFT_LAT, COLS)
    tokens_ref[TOP:] = fill_edge(main_ref[...], beside, ROWS - SHIFT_LAT, COLS)
    side_rows = PAIR_SIDE - PAIR_CORNER
    for half in range(2):
        cols = pl.ds(half * D, D)
        lat = lat_ref[TOP + half * PAIR_TOP : TOP + (half + 1) * PAIR_TOP]
        lon = lon_ref[EDGE + half * side_rows : EDGE + (half + 1) * side_rows]
        diag = diag_ref[SIDE + half * PAIR_CORNER : SIDE + (half + 1) * PAIR_CORNER]
        merged_ref[:PAIR_TOP, cols] = fill_edge(lat, diag, 2, PAIR_COLS)
        merged_ref[PAIR_TOP:, cols] = fill_edge(m_main_ref[:, cols], lon, PAIR_ROWS - 2, PAIR_COLS)


def add_kernel(a_ref, b_ref, *out_refs):
    for k, out_ref in enumerate(out_refs):
        out_ref[...] = (a_ref[k].astype(f32) + b_ref[k].astype(f32)).astype(bf16)


def join_kernel(a_ref, b_ref, c_ref, d_ref, out_ref):
    total = a_ref[...].astype(f32) + b_ref[...].astype(f32) + c_ref[...].astype(f32) + d_ref[...].astype(f32)
    out_ref[...] = total.astype(bf16)


def sum_kernel(parts_ref, out_ref):
    total = parts_ref[0].astype(f32)
    for i in range(1, parts_ref.shape[0]):
        total = total + parts_ref[i].astype(f32)
    out_ref[...] = total.astype(out_ref.dtype)


def call(kernel, outs, scratch=(), places=None, limit=20):
    spaces = {} if places is None else {
        "in_specs": [pl.BlockSpec(memory_space=(pltpu.VMEM, pl.ANY, pltpu.HBM)[p]) for p in places]
    }
    return pl.pallas_call(
        kernel,
        out_shape=[jax.ShapeDtypeStruct(s, t) for s, t in outs],
        scratch_shapes=[pltpu.VMEM(*s) if isinstance(s, tuple) else s for s in scratch],
        cost_estimate=pl.CostEstimate(flops=10**9, bytes_accessed=2 * 10**6, transcendentals=0),
        compiler_params=pltpu.CompilerParams(vmem_limit_bytes=limit * 1024 * 1024),
        **spaces,
    )


def saved(count):
    rows = count * PAD
    return [((rows, D), bf16), ((rows, 3 * D), bf16), ((rows, D), bf16), ((count, 2, PAD, GROUP * PAD), f32)]


def after(value, *others):
    return lax.optimization_barrier((value, *others))[0]


def chain(tok, gain, w_qkv, w_proj, gain_merge, w_merge, g_merged, fetch, up, down):
    tok, g_merged, top, edge, corner = call(
        border_kernel,
        [
            ((TOKENS, D), bf16), ((PAIRS, 2 * D), bf16),
            ((TOP + 2 * PAIR_TOP, D), bf16), ((EDGE + 2 * PAIR_SIDE, D), bf16), ((SIDE + 2 * PAIR_CORNER, D), bf16),
        ],
        [pltpu.SemaphoreType.DMA((2,))],
        [2, 2],
    )(tok, g_merged)
    beside = fetch(top, edge, corner)
    pair, band = pair_selector(), band_selector()
    shift = shift_selector(WIN_LAT, COLS, SHIFT_LON)
    pair_shift = shift_selector(PAIR_ROWS, PAIR_COLS, SHIFT_LON // 2)
    held = [gain, jnp.asarray(band @ shift, bf16), w_qkv, w_proj, gain_merge]
    held += [jnp.asarray(c, bf16) for c in (shift, band.T, pair, pair.T, pair_shift)]
    got = call(
        inner_kernel,
        [(h.shape, h.dtype) for h in held] + [((TOKENS - TOP, D), bf16)] + saved(LOCAL) + [((INNER, D), bf16)],
        [pltpu.SemaphoreType.DMA((HELD,))],
        [0] + [1] * HELD,
    )(tok, *held)
    gain, pick, w_qkv, w_proj, gain_merge, shift, cells_pick, pair, unpair, pair_shift = got[:HELD]
    cells, xs0, qkv0, mixed0, probs0, att0 = got[HELD:]
    xs1, qkv1, mixed1, probs1, tok, summed, row = call(
        outer_kernel,
        saved(REST) + [((TOKENS, D), bf16), ((TOKENS, D), bf16), ((COLS, D), bf16)],
        [((WIDTH, D), bf16)],
    )(tok, cells, *beside, gain, w_qkv, w_proj, pick, shift, cells_pick, att0)
    last = up(row)
    cots, w_merge = call(
        cotangent_kernel,
        [((4, PAIRS, D), f32), ((4 * D, 2 * D), bf16)],
        [pltpu.SemaphoreType.DMA],
        [0] * 6 + [1],
    )(after(g_merged, row), *beside, gain_merge, pair_shift, w_merge)
    d_summed, row, merge_normed = call(
        pair_kernel,
        [((TOKENS, D), bf16), ((COLS, D), bf16), ((4, PAIRS, D), bf16)],
        [((4, PAIRS, D), f32)],
    )(summed, last, gain_merge, cots, pair, unpair)
    first = down(row)
    band = jnp.asarray(band_selector(), bf16)
    unshift = jnp.asarray(shift_selector(WIN_LAT, COLS, SHIFT_LON).T, bf16)
    pair_unshift = jnp.asarray(shift_selector(PAIR_ROWS, PAIR_COLS, SHIFT_LON // 2).T, bf16)
    up1, dqkv1, xst, mixt = call(
        inner_back_kernel,
        [((BAND, D), bf16), ((BAND, 3 * D), bf16), ((D, WIDTH), bf16), ((D, WIDTH), bf16)],
        [((BAND, D), bf16)],
    )(d_summed, qkv1, probs1, w_proj, band, xs0, xs1, mixed0, mixed1)
    m_main, m_lat, m_lon, m_diag = call(
        merge_kernel,
        [
            ((PAIRS - PAIR_TOP, 2 * D), bf16), ((2 * PAIR_TOP, D), bf16),
            ((2 * (PAIR_SIDE - PAIR_CORNER), D), bf16), ((2 * PAIR_CORNER, D), bf16),
        ],
    )(merge_normed, w_merge, pair_unshift)
    dqkv, keep, sent = call(
        outer_back_kernel,
        [((WIDTH, 3 * D), bf16), ((4, 32, 32, 128), bf16), ((4, 32, 32, 128), bf16)],
        [((WIDTH, D), bf16), ((BAND, D), bf16)],
    )(d_summed, first, xst, mixt, after(up1, m_lat), dqkv1, qkv0, probs0, qkv1, probs1, w_proj, band)
    main, to_lat, to_lon, to_diag = call(
        cells_back_kernel,
        [
            ((TOKENS - TOP, D), bf16), ((TOP + 2 * PAIR_TOP, D), bf16),
            ((EDGE + 2 * (PAIR_SIDE - PAIR_CORNER), D), bf16), ((SIDE + 2 * PAIR_CORNER, D), bf16),
        ],
        [((WIDTH, D), bf16)],
    )(dqkv, w_qkv, cells_pick, unshift, tok, d_summed, first, gain, m_lat, m_lon, m_diag)

    def finish(lat, lon, diag):
        grad_tokens, merged = call(own_cells_kernel, [((TOKENS, D), bf16), ((PAIRS, 2 * D), bf16)])(
            main, lat, lon, diag, m_main
        )
        return merged, grad_tokens

    return finish, keep, sent, (to_lat, to_lon, to_diag)


def solution(mesh):
    lats, lons = mesh.shape["lat"], mesh.shape["lon"]
    count = lats * lons

    def send(block, down, right):
        route = [
            (i, (i // lons + down) % lats * lons + (i % lons + right) % lons) for i in range(count)
        ]
        return lax.ppermute(block, ("lat", "lon"), route)

    def fetch(top, edge, corner):
        return send(top, -1, 0), send(edge, 0, -1), send(corner, -1, -1)

    def place(i):
        lat, lon = divmod(i, lons)
        return lat // 8, lat % 8, lon // 8, lon // 2 % 4, lon % 2

    def across(i, step):
        high, z, low, x, core = place(i)
        if core:
            high, low = divmod((high * 2 + low) ^ step, 2)
        else:
            x = x ^ step
        return (high * 8 + z) * lons + low * 8 + x * 2 + core

    rest = {}
    for i in range(count):
        high, z, low, x, core = place(i)
        rest.setdefault((core, high * 2 + low if core else x), []).append(i)
    rest = list(rest.values())

    def swap(block, step):
        return lax.ppermute(block, ("lat", "lon"), [(i, across(i, step)) for i in range(count)])

    def reduce_across(keep, sent, to_lat):
        other = lax.ppermute(sent, ("lat", "lon"), [(i, i ^ 1) for i in range(count)])
        own, *others = call(add_kernel, [((32, 32, 128), bf16)] * 4)(keep, after(other, to_lat))
        got = [swap(block, step) for step, block in enumerate(others, 1)]
        lat = send(to_lat, 1, 0)
        return call(join_kernel, [((32, 32, 128), bf16)])(after(own, lat), *got)[0], lat

    def reduce_rest(sums):
        parts = lax.all_to_all(sums, ("lat", "lon"), 0, 0, axis_index_groups=rest, tiled=True)
        return call(sum_kernel, [((32, 128), f32)])(parts)[0]

    def body(tokens, gain_attn, w_qkv, w_proj, gain_merge, w_merge, g_merged):
        finish, keep, sent, (to_lat, to_lon, to_diag) = chain(
            tokens.reshape(TOKENS, D), gain_attn.reshape(1, D), w_qkv, w_proj, gain_merge.reshape(4, 1, D),
            w_merge, g_merged.reshape(PAIRS, 2 * D), fetch,
            lambda row: send(row, -1, 0), lambda row: send(row, 1, 0),
        )
        sums, lat = reduce_across(keep, sent, to_lat)
        grad_weights = reduce_rest(sums)
        lon, diag = send(after(to_lon, sums), 0, 1), send(after(to_diag, sums), 1, 1)
        merged, grad_tokens = finish(lat, lon, diag)
        return (
            merged.reshape(ROWS // 2, COLS // 2, 2 * D),
            grad_tokens.reshape(ROWS, COLS, D),
            grad_weights,
        )

    return jax.shard_map(
        body,
        mesh=mesh,
        in_specs=(P("lat", "lon", None), P(), P(), P(), P(), P(), P("lat", "lon", None)),
        out_specs=(P("lat", "lon", None), P("lat", "lon", None), P("lat", "lon")),
        check_vma=False,
    )
```

```python
import jax
import jax.numpy as jnp
import numpy as np
from jax import lax
from jax.experimental import pallas as pl
from jax.experimental.pallas import tpu as pltpu
from jax.sharding import PartitionSpec as P

D = 512
HEADS = 8
HEAD = D // HEADS
WIN_LAT = 6
WIN_LON = 12
SHIFT_LAT = 3
SHIFT_LON = 6
EPS = 1e-05

ROWS, COLS = 12, 48
BORDER = 8
TOKENS = ROWS * COLS
LEN = WIN_LAT * WIN_LON
PAD = 80
PER_BAND = COLS // WIN_LON
BAND = PER_BAND * PAD
WINDOWS = 2 * PER_BAND
TOP = SHIFT_LAT * COLS
EDGE = ROWS * BORDER
CORNER = SHIFT_LAT * BORDER
SIDE = WIN_LAT * BORDER
BAND_CELLS = WIN_LAT * COLS
GROUP = HEADS // 2
GROUP_WIDTH = GROUP * HEAD
LOCAL = PER_BAND - 1
INNER = LOCAL * PAD
REST = WINDOWS - LOCAL
OUTER = REST * PAD
PAIR_ROWS, PAIR_COLS = ROWS // 2, COLS // 2
PAIRS = PAIR_ROWS * PAIR_COLS
PAIR_TOP = 2 * PAIR_COLS
PAIR_SIDE = PAIR_ROWS * BORDER
PAIR_CORNER = 2 * BORDER
HELD = 10
WIDTH = WINDOWS * PAD
NEG = -1e30

f32 = jnp.float32
bf16 = jnp.bfloat16


def band_selector():
    pick = np.zeros((BAND, BAND_CELLS), np.float32)
    for win in range(PER_BAND):
        for i in range(WIN_LAT):
            for j in range(WIN_LON):
                pick[win * PAD + i * WIN_LON + j, i * COLS + win * WIN_LON + j] = 1.0
    return pick


def shift_selector(rows, cols, shift):
    pick = np.zeros((rows * cols, rows * (cols + BORDER)), np.float32)
    for i in range(rows):
        for j in range(cols):
            col = j + shift
            pick[i * cols + j, i * cols + col if col < cols else rows * cols + i * BORDER + col - cols] = 1.0
    return pick


def pair_selector():
    pick = np.zeros((4 * COLS, 4 * COLS), np.float32)
    quarter = COLS
    for a in range(2):
        for b in range(COLS // 2):
            for k, (i, j) in enumerate(((0, 0), (1, 0), (0, 1), (1, 1))):
                pick[k * quarter + a * (COLS // 2) + b, (2 * a + i) * COLS + 2 * b + j] = 1.0
    return pick


def dot(a, b):
    return lax.dot_general(a, b, (((1,), (0,)), ((), ())), preferred_element_type=f32)


def dot_nt(a, b):
    return lax.dot_general(a, b, (((1,), (1,)), ((), ())), preferred_element_type=f32)


def dot_tn(a, b):
    return lax.dot_general(a, b, (((0,), (0,)), ((), ())), preferred_element_type=f32)


def norm_parts(values):
    centred = values - jnp.mean(values, axis=-1, keepdims=True)
    scale = lax.rsqrt(jnp.mean(centred * centred, axis=-1, keepdims=True) + EPS)
    return centred * scale, scale


def band_sources(cells, lat, lon, diag):
    first = jnp.concatenate([cells[:BAND_CELLS], lon[CORNER : CORNER + SIDE].astype(bf16)], axis=0)
    beside = jnp.concatenate([lon[CORNER + SIDE : EDGE], diag[:CORNER]], axis=0).astype(bf16)
    second = jnp.concatenate([cells[BAND_CELLS:], lat, beside], axis=0)
    return first, second


def halves(block):
    return jnp.concatenate([block[:, :D], block[:, D:]], axis=0)


def head_masks():
    lane = lax.broadcasted_iota(jnp.int32, (1, GROUP_WIDTH), 1) // HEAD
    return [(lane == h).astype(f32).astype(bf16) for h in range(GROUP)]


def spread_heads(block, masks):
    return jnp.concatenate([block * m for m in masks], axis=0)


def per_head(stacked, block):
    first = lax.broadcasted_iota(jnp.int32, (1, 2 * HEAD), 1) < HEAD
    all_heads = dot_tn(stacked, block)
    out = []
    for pair in range(GROUP // 2):
        part = all_heads[:, pair * 2 * HEAD : (pair + 1) * 2 * HEAD]
        at = pair * 2 * PAD
        out.append(jnp.where(first, part[at : at + PAD], part[at + PAD : at + 2 * PAD]))
    return jnp.concatenate(out, axis=1)


def last_band():
    at_end = lax.axis_index("lat") == lax.axis_size("lat") - 1
    return jnp.where(at_end, f32(1), f32(0))


def halves_apart():
    shape = (LEN, GROUP * PAD)
    key = lax.broadcasted_iota(jnp.int32, shape, 0)
    query = lax.rem(lax.broadcasted_iota(jnp.int32, shape, 1), PAD)
    return jnp.where((key < LEN // 2) != (query < LEN // 2), f32(NEG), f32(0)) * last_band()


def attend(windows, qkv_ref, mixed_ref, probs_ref):
    masks = [m * HEAD ** (-0.5) for m in head_masks()]
    apart = halves_apart() if any(windows) else None
    for win, wraps in enumerate(windows):
        rows = pl.ds(win * PAD, PAD)
        for g in range(2):
            at = g * GROUP_WIDTH
            queries = spread_heads(qkv_ref[rows, at : at + GROUP_WIDTH], masks)
            keys = qkv_ref[rows, D + at : D + at + GROUP_WIDTH]
            values = qkv_ref[rows, 2 * D + at : 2 * D + at + GROUP_WIDTH]
            scores = dot_nt(keys, queries)[:LEN]
            if wraps:
                scores = scores + apart
            weights = jnp.exp(scores - jnp.max(scores, axis=0, keepdims=True))
            probs = weights * (1.0 / jnp.sum(weights, axis=0, keepdims=True))
            probs = jnp.concatenate([probs, jnp.zeros((PAD - LEN, GROUP * PAD), f32)], axis=0)
            probs_ref[win, g] = probs
            mixed_ref[rows, at : at + GROUP_WIDTH] = per_head(probs.astype(bf16), values).astype(bf16)


def attend_back(windows, dmix_ref, dqkv_ref, offset):
    masks = head_masks()
    scaled = [m * HEAD ** (-0.5) for m in masks]
    for win, (qkv_ref, probs_ref, place) in enumerate(windows):
        rows = pl.ds(place * PAD, PAD)
        out = pl.ds(offset + win * PAD, PAD)
        for g in range(2):
            at = g * GROUP_WIDTH
            queries = spread_heads(qkv_ref[rows, at : at + GROUP_WIDTH], scaled)
            keys = qkv_ref[rows, D + at : D + at + GROUP_WIDTH]
            values = qkv_ref[rows, 2 * D + at : 2 * D + at + GROUP_WIDTH]
            above = spread_heads(dmix_ref[pl.ds(win * PAD, PAD), at : at + GROUP_WIDTH], masks)
            probs = probs_ref[place, g]
            d_probs = dot_nt(values, above)
            along = jnp.sum(probs * d_probs, axis=0, keepdims=True)
            d_scores = (probs * (d_probs - along)).astype(bf16)
            d_queries = per_head(d_scores, keys) * HEAD ** (-0.5)
            d_keys = dot(d_scores, queries)
            d_values = dot(probs.astype(bf16), above)
            dqkv_ref[out, at : at + GROUP_WIDTH] = d_queries.astype(bf16)
            dqkv_ref[out, D + at : D + at + GROUP_WIDTH] = d_keys.astype(bf16)
            dqkv_ref[out, 2 * D + at : 2 * D + at + GROUP_WIDTH] = d_values.astype(bf16)


def border_kernel(tok_ref, g_ref, own_ref, own_g_ref, top_ref, g_top_ref, edge_ref, corner_ref, sem):
    copies = [
        pltpu.make_async_copy(tok_ref, own_ref, sem.at[0]),
        pltpu.make_async_copy(g_ref, own_g_ref, sem.at[1]),
    ]
    for copy in copies:
        copy.start()
    for copy in copies:
        copy.wait()
    edge = [own_ref[row * COLS : row * COLS + 16].astype(f32)[:BORDER] for row in range(ROWS)]
    cots = own_g_ref[...].astype(f32)
    side = [cots[row * PAIR_COLS : row * PAIR_COLS + BORDER] for row in range(PAIR_ROWS)]
    top_ref[...] = own_ref[:TOP]
    g_top_ref[...] = halves(own_g_ref[:PAIR_TOP])
    edge_ref[:EDGE] = jnp.concatenate(edge, axis=0).astype(bf16)
    edge_ref[EDGE:] = halves(jnp.concatenate(side, axis=0).astype(bf16))
    corner_ref[:SIDE] = jnp.concatenate(edge[:WIN_LAT], axis=0).astype(bf16)
    corner_ref[SIDE:] = halves(jnp.concatenate(side[:2], axis=0).astype(bf16))


def inner_kernel(tok_ref, *refs):
    held, got = refs[:HELD], refs[HELD : 2 * HELD]
    cells_ref, xs_ref, qkv_ref, mixed_ref, probs_ref, att_ref, sem = refs[2 * HELD :]
    copies = [pltpu.make_async_copy(a, b, sem.at[i]) for i, (a, b) in enumerate(zip(held, got))]
    for copy in copies:
        copy.start()
    gain_ref, pick_ref, wqkv_ref, wproj_ref = got[:4]
    normed = norm_parts(tok_ref[TOP:].astype(f32))[0]
    for copy in copies:
        copy.wait()
    cells_ref[...] = (normed * gain_ref[...]).astype(bf16)
    xs_ref[...] = dot(pick_ref[:INNER, :BAND_CELLS], cells_ref[:BAND_CELLS]).astype(bf16)
    qkv_ref[...] = dot(xs_ref[...], wqkv_ref[...]).astype(bf16)
    attend([False] * LOCAL, qkv_ref, mixed_ref, probs_ref)
    att_ref[...] = dot(mixed_ref[...], wproj_ref[...]).astype(bf16)


def outer_kernel(
    tok_ref, cells_ref, lat_ref, lon_ref, diag_ref, gain_ref, wqkv_ref, wproj_ref, pick_ref, shift_ref, cells_pick_ref,
    att0_ref,
    xs_ref, qkv_ref, mixed_ref, probs_ref, tok_out_ref, summed_ref, row_ref,
    att_ref,
):
    def normed(values):
        return norm_parts(values)[0] * gain_ref[...]

    lat, lon, diag = lat_ref[...], lon_ref[:EDGE].astype(f32), diag_ref[:SIDE].astype(f32)
    first, second = band_sources(cells_ref[...], normed(lat.astype(f32)).astype(bf16), normed(lon), normed(diag))
    xs_ref[:PAD] = dot(pick_ref[INNER:], first).astype(bf16)
    xs_ref[PAD:] = dot(pick_ref[...], second).astype(bf16)
    qkv_ref[...] = dot(xs_ref[...], wqkv_ref[...]).astype(bf16)
    attend([False] + [True] * PER_BAND, qkv_ref, mixed_ref, probs_ref)
    att_ref[:INNER] = att0_ref[...]
    att_ref[INNER:] = dot(mixed_ref[...], wproj_ref[...]).astype(bf16)
    for band, source in enumerate(band_sources(tok_ref[TOP:], lat, lon, diag)):
        rows = pl.ds(band * BAND_CELLS, BAND_CELLS)
        tokens = dot(shift_ref[...], source)
        added = dot(cells_pick_ref[...], att_ref[pl.ds(band * BAND, BAND)])
        tok_out_ref[rows] = tokens.astype(bf16)
        summed_ref[rows] = (tokens + added).astype(bf16)
    row_ref[...] = summed_ref[:COLS]


def cotangent_kernel(
    g_ref, lat_ref, lon_ref, diag_ref, gain_ref, shift_ref, wmerge_ref, out_ref, weights_ref, sem
):
    copy = pltpu.make_async_copy(wmerge_ref, weights_ref, sem)
    copy.start()
    parts = []
    for half in range(2):
        lat = lat_ref[half * PAIR_TOP : (half + 1) * PAIR_TOP]
        at = EDGE + half * PAIR_SIDE
        lon = lon_ref[at + PAIR_CORNER : at + PAIR_SIDE]
        diag = diag_ref[SIDE + half * PAIR_CORNER : SIDE + (half + 1) * PAIR_CORNER]
        own = g_ref[PAIR_TOP:, half * D : (half + 1) * D]
        parts.append(dot(shift_ref[...], jnp.concatenate([own, lat, lon, diag], axis=0)).astype(bf16))
    cots = jnp.concatenate(parts, axis=1)
    copy.wait()
    for k in range(4):
        out_ref[k] = dot_nt(cots, weights_ref[k * D : (k + 1) * D]) * gain_ref[k]


def pair_kernel(
    summed_ref, row_ref, gain_ref, cot_ref, pair_ref, unpair_ref,
    dsum_ref, out_row_ref, normed_ref,
    members_ref,
):
    quarter = COLS
    for part in range(3):
        first = COLS + part * 4 * COLS
        if part < 2:
            summed = summed_ref[first : first + 4 * COLS]
        else:
            summed = jnp.concatenate([summed_ref[first:], row_ref[...]], axis=0)
        paired = dot(pair_ref[...], summed)
        for k in range(4):
            members_ref[k, pl.ds(part * quarter, quarter)] = paired[k * quarter : (k + 1) * quarter]
    width = 4 * D
    total = sum(jnp.sum(members_ref[k], axis=-1, keepdims=True) for k in range(4))
    center = total / width
    for k in range(4):
        members_ref[k] = members_ref[k] - center
    spread = sum(jnp.sum(members_ref[k] * members_ref[k], axis=-1, keepdims=True) for k in range(4)) / width
    scale = lax.rsqrt(spread + EPS)
    for k in range(4):
        members_ref[k] = members_ref[k] * scale
        normed_ref[k] = (members_ref[k] * gain_ref[k]).astype(bf16)
    flat = sum(jnp.sum(cot_ref[k], axis=-1, keepdims=True) for k in range(4)) / width
    along = sum(jnp.sum(cot_ref[k] * members_ref[k], axis=-1, keepdims=True) for k in range(4)) / width
    for k in range(4):
        members_ref[k] = (cot_ref[k] - flat - members_ref[k] * along) * scale
    for part in range(3):
        rows = pl.ds(part * quarter, quarter)
        block = jnp.concatenate([members_ref[k, rows].astype(bf16) for k in range(4)], axis=0)
        dsum_ref[pl.ds(part * 4 * COLS, 4 * COLS)] = dot(unpair_ref[...], block).astype(bf16)
    out_row_ref[...] = dsum_ref[TOKENS - COLS :]


def merge_kernel(normed_ref, wmerge_ref, unshift_ref, main_ref, lat_ref, lon_ref, diag_ref):
    total = dot(normed_ref[0], wmerge_ref[:D])
    for k in range(1, 4):
        total = total + dot(normed_ref[k], wmerge_ref[k * D : (k + 1) * D])
    pairs = dot(unshift_ref[...], total.astype(bf16)).astype(bf16)
    main_ref[...] = pairs[: PAIRS - PAIR_TOP]
    lat_ref[...] = halves(pairs[PAIRS - PAIR_TOP : PAIRS])
    lon_ref[...] = halves(pairs[PAIRS : PAIRS + PAIR_SIDE - PAIR_CORNER])
    diag_ref[...] = halves(pairs[PAIRS + PAIR_SIDE - PAIR_CORNER :])


def inner_back_kernel(
    dsum_ref, qkv_ref, probs_ref, wproj_ref, pick_ref, xs0_ref, xs_ref, mixed0_ref, mixed_ref,
    up_ref, dqkv_ref, xst_ref, mixt_ref,
    dmix_ref,
):
    xst_ref[...] = jnp.concatenate([xs0_ref[...], xs_ref[...]], axis=0).T
    mixt_ref[...] = jnp.concatenate([mixed0_ref[...], mixed_ref[...]], axis=0).T
    up_ref[...] = dot(pick_ref[...], dsum_ref[BAND_CELLS - COLS : TOKENS - COLS]).astype(bf16)
    dmix_ref[...] = dot_nt(up_ref[...], wproj_ref[...]).astype(bf16)
    attend_back([(qkv_ref, probs_ref, win) for win in range(1, REST)], dmix_ref, dqkv_ref, 0)


def outer_back_kernel(
    dsum_ref, row_ref, xst_ref, mixt_ref, up1_ref, dqkv1_ref, qkv0_ref, probs0_ref, qkv_ref, probs_ref,
    wproj_ref, pick_ref,
    dqkv_ref, keep_ref, send_ref,
    up_ref, dmix_ref,
):
    cells = jnp.concatenate([row_ref[...], dsum_ref[: BAND_CELLS - COLS]], axis=0)
    up_ref[:BAND] = dot(pick_ref[...], cells).astype(bf16)
    up_ref[BAND:] = up1_ref[...]
    dqkv_ref[BAND:] = dqkv1_ref[...]
    dmix_ref[...] = dot_nt(up_ref[:BAND], wproj_ref[...]).astype(bf16)
    windows = [(qkv0_ref, probs0_ref, win) for win in range(LOCAL)] + [(qkv_ref, probs_ref, 0)]
    attend_back(windows, dmix_ref, dqkv_ref, 0)
    lat_at, lon_at = lax.axis_index("lat"), lax.axis_index("lon")
    even_core = lax.rem(lon_at, 2) == 0
    my_x = lax.rem(lax.div(lon_at, 2), 4)
    my_y = lax.div(lat_at, 8) * 2 + lax.div(lon_at, 8)
    x_steps = [lax.bitwise_xor(my_x, jnp.int32(i)) for i in range(4)]
    y_steps = [lax.bitwise_xor(my_y, jnp.int32(i)) for i in range(4)]
    for col in range(8):
        if col < 6:
            grad = dot(xst_ref[...], dqkv_ref[:, col * 256 : (col + 1) * 256])
        else:
            grad = dot(mixt_ref[...], up_ref[:, (col - 6) * 256 : (col - 5) * 256])
        even, odd = grad[:, :128], grad[:, 128:]
        kept = jnp.where(even_core, even, odd).astype(bf16)
        sent = jnp.where(even_core, odd, even).astype(bf16)
        low, x = divmod(col, 4)
        for lat in range(16):
            high, z = divmod(lat, 8)
            y = high * 2 + low
            rows = slice(lat * 32, (lat + 1) * 32)
            on_even = x_steps[x], lat * 2 + low
            on_odd = y_steps[y], z * 4 + x
            mine = [jnp.where(even_core, a, b) for a, b in zip(on_even, on_odd)]
            other = [jnp.where(even_core, b, a) for a, b in zip(on_even, on_odd)]
            keep_ref[mine[0], mine[1]] = kept[rows]
            send_ref[other[0], other[1]] = sent[rows]


def cells_back_kernel(
    dqkv_ref, wqkv_ref, cells_pick_ref, unshift_ref, tok_ref, dsum_ref, row_ref, gain_ref, m_lon_ref, m_diag_ref,
    main_ref, lat_ref, lon_ref, diag_ref,
    dx_ref,
):
    dx_ref[...] = dot_nt(dqkv_ref[...], wqkv_ref[...]).astype(bf16)
    for band in range(2):
        if band == 0:
            above = jnp.concatenate([row_ref[...], dsum_ref[: BAND_CELLS - COLS]], axis=0)
        else:
            above = dsum_ref[BAND_CELLS - COLS : TOKENS - COLS]
        cot = dot(cells_pick_ref[...], dx_ref[pl.ds(band * BAND, BAND)]) * gain_ref[...]
        normed, scale = norm_parts(tok_ref[pl.ds(band * BAND_CELLS, BAND_CELLS)].astype(f32))
        flat = jnp.mean(cot, axis=-1, keepdims=True)
        along = jnp.mean(cot * normed, axis=-1, keepdims=True)
        grads = (above.astype(f32) + (cot - flat - normed * along) * scale).astype(bf16)
        cells = dot(unshift_ref[...], grads).astype(bf16)
        if band == 0:
            main_ref[:BAND_CELLS] = cells[:BAND_CELLS]
        else:
            main_ref[BAND_CELLS:] = cells[: BAND_CELLS - TOP]
            lat_ref[...] = cells[BAND_CELLS - TOP : BAND_CELLS]
            diag_ref[:SIDE] = cells[BAND_CELLS:]
        lon_ref[band * SIDE : (band + 1) * SIDE] = cells[BAND_CELLS:]
    lon_ref[EDGE:] = m_lon_ref[...]
    diag_ref[SIDE:] = m_diag_ref[...]


def fill_edge(field, side, rows, cols):
    width = field.shape[-1]
    field, side = field.astype(f32).reshape(rows, cols, width), side.astype(f32).reshape(rows, BORDER, width)
    first = field[:, :BORDER] + side
    return jnp.concatenate([first, field[:, BORDER:]], axis=1).reshape(rows * cols, width).astype(bf16)


def own_cells_kernel(main_ref, lat_ref, lon_ref, diag_ref, m_main_ref, m_lat_ref, tokens_ref, merged_ref):
    corner = diag_ref[:SIDE].astype(f32)[SIDE - CORNER :]
    beside = lon_ref[:EDGE].astype(f32)[: EDGE - CORNER]
    tokens_ref[:TOP] = fill_edge(lat_ref[...], corner, SHIFT_LAT, COLS)
    tokens_ref[TOP:] = fill_edge(main_ref[...], beside, ROWS - SHIFT_LAT, COLS)
    side_rows = PAIR_SIDE - PAIR_CORNER
    for half in range(2):
        cols = pl.ds(half * D, D)
        lat = m_lat_ref[half * PAIR_TOP : (half + 1) * PAIR_TOP]
        lon = lon_ref[EDGE + half * side_rows : EDGE + (half + 1) * side_rows]
        diag = diag_ref[SIDE + half * PAIR_CORNER : SIDE + (half + 1) * PAIR_CORNER]
        merged_ref[:PAIR_TOP, cols] = fill_edge(lat, diag, 2, PAIR_COLS)
        merged_ref[PAIR_TOP:, cols] = fill_edge(m_main_ref[:, cols], lon, PAIR_ROWS - 2, PAIR_COLS)


def add_kernel(a_ref, b_ref, *out_refs):
    for k, out_ref in enumerate(out_refs):
        out_ref[...] = (a_ref[k].astype(f32) + b_ref[k].astype(f32)).astype(bf16)


def join_kernel(a_ref, b_ref, c_ref, d_ref, out_ref):
    total = a_ref[...].astype(f32) + b_ref[...].astype(f32) + c_ref[...].astype(f32) + d_ref[...].astype(f32)
    out_ref[...] = total.astype(bf16)


def sum_kernel(parts_ref, out_ref):
    total = parts_ref[0].astype(f32)
    for i in range(1, parts_ref.shape[0]):
        total = total + parts_ref[i].astype(f32)
    out_ref[...] = total.astype(out_ref.dtype)


def call(kernel, outs, scratch=(), places=None, limit=20):
    spaces = {} if places is None else {
        "in_specs": [pl.BlockSpec(memory_space=(pltpu.VMEM, pl.ANY, pltpu.HBM)[p]) for p in places]
    }
    return pl.pallas_call(
        kernel,
        out_shape=[jax.ShapeDtypeStruct(s, t) for s, t in outs],
        scratch_shapes=[pltpu.VMEM(*s) if isinstance(s, tuple) else s for s in scratch],
        cost_estimate=pl.CostEstimate(flops=10**9, bytes_accessed=2 * 10**6, transcendentals=0),
        compiler_params=pltpu.CompilerParams(vmem_limit_bytes=limit * 1024 * 1024),
        **spaces,
    )


def saved(count):
    rows = count * PAD
    return [((rows, D), bf16), ((rows, 3 * D), bf16), ((rows, D), bf16), ((count, 2, PAD, GROUP * PAD), f32)]


def after(value, *others):
    return lax.optimization_barrier((value, *others))[0]


def chain(tok, gain, w_qkv, w_proj, gain_merge, w_merge, g_merged, fetch, up, down):
    tok, g_merged, top, g_top, edge, corner = call(
        border_kernel,
        [
            ((TOKENS, D), bf16), ((PAIRS, 2 * D), bf16),
            ((TOP, D), bf16), ((2 * PAIR_TOP, D), bf16),
            ((EDGE + 2 * PAIR_SIDE, D), bf16), ((SIDE + 2 * PAIR_CORNER, D), bf16),
        ],
        [pltpu.SemaphoreType.DMA((2,))],
        [2, 2],
    )(tok, g_merged)
    beside = fetch(top, edge, corner)
    g_lat = up(g_top)
    pair, band = pair_selector(), band_selector()
    shift = shift_selector(WIN_LAT, COLS, SHIFT_LON)
    pair_shift = shift_selector(PAIR_ROWS, PAIR_COLS, SHIFT_LON // 2)
    held = [gain, jnp.asarray(band @ shift, bf16), w_qkv, w_proj, gain_merge]
    held += [jnp.asarray(c, bf16) for c in (shift, band.T, pair, pair.T, pair_shift)]
    got = call(
        inner_kernel,
        [(h.shape, h.dtype) for h in held] + [((TOKENS - TOP, D), bf16)] + saved(LOCAL) + [((INNER, D), bf16)],
        [pltpu.SemaphoreType.DMA((HELD,))],
        [0] + [1] * HELD,
    )(tok, *held)
    gain, pick, w_qkv, w_proj, gain_merge, shift, cells_pick, pair, unpair, pair_shift = got[:HELD]
    cells, xs0, qkv0, mixed0, probs0, att0 = got[HELD:]
    xs1, qkv1, mixed1, probs1, tok, summed, row = call(
        outer_kernel,
        saved(REST) + [((TOKENS, D), bf16), ((TOKENS, D), bf16), ((COLS, D), bf16)],
        [((WIDTH, D), bf16)],
    )(tok, cells, *beside, gain, w_qkv, w_proj, pick, shift, cells_pick, att0)
    last = up(row)
    cots, w_merge = call(
        cotangent_kernel,
        [((4, PAIRS, D), f32), ((4 * D, 2 * D), bf16)],
        [pltpu.SemaphoreType.DMA],
        [0] * 6 + [1],
    )(after(g_merged, row), g_lat, *beside[1:], gain_merge, pair_shift, w_merge)
    d_summed, row, merge_normed = call(
        pair_kernel,
        [((TOKENS, D), bf16), ((COLS, D), bf16), ((4, PAIRS, D), bf16)],
        [((4, PAIRS, D), f32)],
    )(summed, last, gain_merge, cots, pair, unpair)
    first = down(row)
    band = jnp.asarray(band_selector(), bf16)
    unshift = jnp.asarray(shift_selector(WIN_LAT, COLS, SHIFT_LON).T, bf16)
    pair_unshift = jnp.asarray(shift_selector(PAIR_ROWS, PAIR_COLS, SHIFT_LON // 2).T, bf16)
    up1, dqkv1, xst, mixt = call(
        inner_back_kernel,
        [((BAND, D), bf16), ((BAND, 3 * D), bf16), ((D, WIDTH), bf16), ((D, WIDTH), bf16)],
        [((BAND, D), bf16)],
    )(d_summed, qkv1, probs1, w_proj, band, xs0, xs1, mixed0, mixed1)
    m_main, m_lat, m_lon, m_diag = call(
        merge_kernel,
        [
            ((PAIRS - PAIR_TOP, 2 * D), bf16), ((2 * PAIR_TOP, D), bf16),
            ((2 * (PAIR_SIDE - PAIR_CORNER), D), bf16), ((2 * PAIR_CORNER, D), bf16),
        ],
    )(merge_normed, w_merge, pair_unshift)
    m_lat = down(m_lat)
    dqkv, keep, sent = call(
        outer_back_kernel,
        [((WIDTH, 3 * D), bf16), ((4, 32, 32, 128), bf16), ((4, 32, 32, 128), bf16)],
        [((WIDTH, D), bf16), ((BAND, D), bf16)],
    )(d_summed, first, xst, mixt, after(up1, m_main), dqkv1, qkv0, probs0, qkv1, probs1, w_proj, band)
    main, to_lat, to_lon, to_diag = call(
        cells_back_kernel,
        [
            ((TOKENS - TOP, D), bf16), ((TOP, D), bf16),
            ((EDGE + 2 * (PAIR_SIDE - PAIR_CORNER), D), bf16), ((SIDE + 2 * PAIR_CORNER, D), bf16),
        ],
        [((WIDTH, D), bf16)],
    )(dqkv, w_qkv, cells_pick, unshift, tok, d_summed, first, gain, m_lon, m_diag)

    def finish(lat, lon, diag):
        grad_tokens, merged = call(own_cells_kernel, [((TOKENS, D), bf16), ((PAIRS, 2 * D), bf16)])(
            main, lat, lon, diag, m_main, m_lat
        )
        return merged, grad_tokens

    return finish, keep, sent, (to_lat, to_lon, to_diag), m_lat


def solution(mesh):
    lats, lons = mesh.shape["lat"], mesh.shape["lon"]
    count = lats * lons

    def send(block, down, right):
        route = [
            (i, (i // lons + down) % lats * lons + (i % lons + right) % lons) for i in range(count)
        ]
        return lax.ppermute(block, ("lat", "lon"), route)

    def fetch(top, edge, corner):
        return send(top, -1, 0), send(edge, 0, -1), send(corner, -1, -1)

    def place(i):
        lat, lon = divmod(i, lons)
        return lat // 8, lat % 8, lon // 8, lon // 2 % 4, lon % 2

    def across(i, step):
        high, z, low, x, core = place(i)
        if core:
            high, low = divmod((high * 2 + low) ^ step, 2)
        else:
            x = x ^ step
        return (high * 8 + z) * lons + low * 8 + x * 2 + core

    rest = {}
    for i in range(count):
        high, z, low, x, core = place(i)
        rest.setdefault((core, high * 2 + low if core else x), []).append(i)
    rest = list(rest.values())

    def swap(block, step):
        return lax.ppermute(block, ("lat", "lon"), [(i, across(i, step)) for i in range(count)])

    def reduce_across(keep, sent, to_lat):
        other = lax.ppermute(sent, ("lat", "lon"), [(i, i ^ 1) for i in range(count)])
        own, *others = call(add_kernel, [((32, 32, 128), bf16)] * 4)(keep, after(other, to_lat))
        got = [swap(block, step) for step, block in enumerate(others, 1)]
        return call(join_kernel, [((32, 32, 128), bf16)])(own, *got)[0]

    def reduce_rest(sums):
        parts = lax.all_to_all(sums, ("lat", "lon"), 0, 0, axis_index_groups=rest, tiled=True)
        return call(sum_kernel, [((32, 128), f32)])(parts)[0]

    def body(tokens, gain_attn, w_qkv, w_proj, gain_merge, w_merge, g_merged):
        finish, keep, sent, pieces, m_lat = chain(
            tokens.reshape(TOKENS, D), gain_attn.reshape(1, D), w_qkv, w_proj, gain_merge.reshape(4, 1, D),
            w_merge, g_merged.reshape(PAIRS, 2 * D), fetch,
            lambda row: send(row, -1, 0), lambda row: send(row, 1, 0),
        )
        sums = after(reduce_across(keep, sent, pieces[0]), m_lat)
        grad_weights = reduce_rest(sums)
        to_lat, to_lon, to_diag = (after(piece, sums) for piece in pieces)
        merged, grad_tokens = finish(send(to_lat, 1, 0), send(to_lon, 0, 1), send(to_diag, 1, 1))
        return (
            merged.reshape(ROWS // 2, COLS // 2, 2 * D),
            grad_tokens.reshape(ROWS, COLS, D),
            grad_weights,
        )

    return jax.shard_map(
        body,
        mesh=mesh,
        in_specs=(P("lat", "lon", None), P(), P(), P(), P(), P(), P("lat", "lon", None)),
        out_specs=(P("lat", "lon", None), P("lat", "lon", None), P("lat", "lon")),
        check_vma=False,
    )
```

```python
import jax
import jax.numpy as jnp
import numpy as np
from jax import lax
from jax.experimental import pallas as pl
from jax.experimental.pallas import tpu as pltpu
from jax.sharding import PartitionSpec as P

D = 512
HEADS = 8
HEAD = D // HEADS
WIN_LAT = 6
WIN_LON = 12
SHIFT_LAT = 3
SHIFT_LON = 6
EPS = 1e-05

ROWS, COLS = 12, 48
BORDER = 8
TOKENS = ROWS * COLS
LEN = WIN_LAT * WIN_LON
PAD = 80
PER_BAND = COLS // WIN_LON
BAND = PER_BAND * PAD
WINDOWS = 2 * PER_BAND
TOP = SHIFT_LAT * COLS
EDGE = ROWS * BORDER
CORNER = SHIFT_LAT * BORDER
SIDE = WIN_LAT * BORDER
TURN = 4 * BORDER
BAND_CELLS = WIN_LAT * COLS
GROUP = HEADS // 2
GROUP_WIDTH = GROUP * HEAD
LOCAL = PER_BAND - 1
INNER = LOCAL * PAD
REST = WINDOWS - LOCAL
OUTER = REST * PAD
PAIR_ROWS, PAIR_COLS = ROWS // 2, COLS // 2
PAIRS = PAIR_ROWS * PAIR_COLS
PAIR_TOP = 2 * PAIR_COLS
PAIR_SIDE = PAIR_ROWS * BORDER
PAIR_CORNER = 2 * BORDER
HELD = 10
WIDTH = WINDOWS * PAD
NEG = -1e30

f32 = jnp.float32
bf16 = jnp.bfloat16


def band_selector():
    pick = np.zeros((BAND, BAND_CELLS), np.float32)
    for win in range(PER_BAND):
        for i in range(WIN_LAT):
            for j in range(WIN_LON):
                pick[win * PAD + i * WIN_LON + j, i * COLS + win * WIN_LON + j] = 1.0
    return pick


def shift_selector(rows, cols, shift):
    pick = np.zeros((rows * cols, rows * (cols + BORDER)), np.float32)
    for i in range(rows):
        for j in range(cols):
            col = j + shift
            pick[i * cols + j, i * cols + col if col < cols else rows * cols + i * BORDER + col - cols] = 1.0
    return pick


def pair_selector():
    pick = np.zeros((4 * COLS, 4 * COLS), np.float32)
    quarter = COLS
    for a in range(2):
        for b in range(COLS // 2):
            for k, (i, j) in enumerate(((0, 0), (1, 0), (0, 1), (1, 1))):
                pick[k * quarter + a * (COLS // 2) + b, (2 * a + i) * COLS + 2 * b + j] = 1.0
    return pick


def dot(a, b):
    return lax.dot_general(a, b, (((1,), (0,)), ((), ())), preferred_element_type=f32)


def dot_nt(a, b):
    return lax.dot_general(a, b, (((1,), (1,)), ((), ())), preferred_element_type=f32)


def dot_tn(a, b):
    return lax.dot_general(a, b, (((0,), (0,)), ((), ())), preferred_element_type=f32)


def norm_parts(values):
    centred = values - jnp.mean(values, axis=-1, keepdims=True)
    scale = lax.rsqrt(jnp.mean(centred * centred, axis=-1, keepdims=True) + EPS)
    return centred * scale, scale


def band_sources(cells, lat, lon, diag):
    first = jnp.concatenate([cells[:BAND_CELLS], lon[CORNER : CORNER + SIDE].astype(bf16)], axis=0)
    beside = jnp.concatenate([lon[CORNER + SIDE : EDGE], diag[:CORNER]], axis=0).astype(bf16)
    second = jnp.concatenate([cells[BAND_CELLS:], lat, beside], axis=0)
    return first, second


def halves(block):
    return jnp.concatenate([block[:, :D], block[:, D:]], axis=0)


def head_masks():
    lane = lax.broadcasted_iota(jnp.int32, (1, GROUP_WIDTH), 1) // HEAD
    return [(lane == h).astype(f32).astype(bf16) for h in range(GROUP)]


def spread_heads(block, masks):
    return jnp.concatenate([block * m for m in masks], axis=0)


def per_head(stacked, block):
    first = lax.broadcasted_iota(jnp.int32, (1, 2 * HEAD), 1) < HEAD
    all_heads = dot_tn(stacked, block)
    out = []
    for pair in range(GROUP // 2):
        part = all_heads[:, pair * 2 * HEAD : (pair + 1) * 2 * HEAD]
        at = pair * 2 * PAD
        out.append(jnp.where(first, part[at : at + PAD], part[at + PAD : at + 2 * PAD]))
    return jnp.concatenate(out, axis=1)


def last_band():
    at_end = lax.axis_index("lat") == lax.axis_size("lat") - 1
    return jnp.where(at_end, f32(1), f32(0))


def halves_apart():
    shape = (LEN, GROUP * PAD)
    key = lax.broadcasted_iota(jnp.int32, shape, 0)
    query = lax.rem(lax.broadcasted_iota(jnp.int32, shape, 1), PAD)
    return jnp.where((key < LEN // 2) != (query < LEN // 2), f32(NEG), f32(0)) * last_band()


def attend(windows, qkv_ref, mixed_ref, probs_ref):
    masks = [m * HEAD ** (-0.5) for m in head_masks()]
    apart = halves_apart() if any(windows) else None
    for win, wraps in enumerate(windows):
        rows = pl.ds(win * PAD, PAD)
        for g in range(2):
            at = g * GROUP_WIDTH
            queries = spread_heads(qkv_ref[rows, at : at + GROUP_WIDTH], masks)
            keys = qkv_ref[rows, D + at : D + at + GROUP_WIDTH]
            values = qkv_ref[rows, 2 * D + at : 2 * D + at + GROUP_WIDTH]
            scores = dot_nt(keys, queries)[:LEN]
            if wraps:
                scores = scores + apart
            weights = jnp.exp(scores - jnp.max(scores, axis=0, keepdims=True))
            probs = weights * (1.0 / jnp.sum(weights, axis=0, keepdims=True))
            probs = jnp.concatenate([probs, jnp.zeros((PAD - LEN, GROUP * PAD), f32)], axis=0)
            probs_ref[win, g] = probs
            mixed_ref[rows, at : at + GROUP_WIDTH] = per_head(probs.astype(bf16), values).astype(bf16)


def attend_back(windows, dmix_ref, dqkv_ref, offset):
    masks = head_masks()
    scaled = [m * HEAD ** (-0.5) for m in masks]
    for win, (qkv_ref, probs_ref, place) in enumerate(windows):
        rows = pl.ds(place * PAD, PAD)
        out = pl.ds(offset + win * PAD, PAD)
        for g in range(2):
            at = g * GROUP_WIDTH
            queries = spread_heads(qkv_ref[rows, at : at + GROUP_WIDTH], scaled)
            keys = qkv_ref[rows, D + at : D + at + GROUP_WIDTH]
            values = qkv_ref[rows, 2 * D + at : 2 * D + at + GROUP_WIDTH]
            above = spread_heads(dmix_ref[pl.ds(win * PAD, PAD), at : at + GROUP_WIDTH], masks)
            probs = probs_ref[place, g]
            d_probs = dot_nt(values, above)
            along = jnp.sum(probs * d_probs, axis=0, keepdims=True)
            d_scores = (probs * (d_probs - along)).astype(bf16)
            d_queries = per_head(d_scores, keys) * HEAD ** (-0.5)
            d_keys = dot(d_scores, queries)
            d_values = dot(probs.astype(bf16), above)
            dqkv_ref[out, at : at + GROUP_WIDTH] = d_queries.astype(bf16)
            dqkv_ref[out, D + at : D + at + GROUP_WIDTH] = d_keys.astype(bf16)
            dqkv_ref[out, 2 * D + at : 2 * D + at + GROUP_WIDTH] = d_values.astype(bf16)


def border_kernel(tok_ref, g_ref, own_ref, own_g_ref, top_ref, g_top_ref, edge_ref, corner_ref, sem):
    copies = [
        pltpu.make_async_copy(tok_ref, own_ref, sem.at[0]),
        pltpu.make_async_copy(g_ref, own_g_ref, sem.at[1]),
    ]
    for copy in copies:
        copy.start()
    for copy in copies:
        copy.wait()
    edge = [own_ref[row * COLS : row * COLS + 16].astype(f32)[:BORDER] for row in range(ROWS)]
    cots = own_g_ref[...].astype(f32)
    side = [cots[row * PAIR_COLS : row * PAIR_COLS + BORDER] for row in range(PAIR_ROWS)]
    top_ref[...] = own_ref[:TOP]
    g_top_ref[...] = halves(own_g_ref[:PAIR_TOP])
    edge_ref[:EDGE] = jnp.concatenate(edge, axis=0).astype(bf16)
    edge_ref[EDGE:] = halves(jnp.concatenate(side, axis=0).astype(bf16))
    corner_ref[:TURN] = jnp.concatenate(edge[:4], axis=0).astype(bf16)
    corner_ref[TURN:] = halves(jnp.concatenate(side[:2], axis=0).astype(bf16))


def inner_kernel(tok_ref, *refs):
    held, got = refs[:HELD], refs[HELD : 2 * HELD]
    cells_ref, xs_ref, qkv_ref, mixed_ref, probs_ref, att_ref, sem = refs[2 * HELD :]
    copies = [pltpu.make_async_copy(a, b, sem.at[i]) for i, (a, b) in enumerate(zip(held, got))]
    for copy in copies:
        copy.start()
    gain_ref, pick_ref, wqkv_ref, wproj_ref = got[:4]
    normed = norm_parts(tok_ref[TOP:].astype(f32))[0]
    for copy in copies:
        copy.wait()
    cells_ref[...] = (normed * gain_ref[...]).astype(bf16)
    xs_ref[...] = dot(pick_ref[:INNER, :BAND_CELLS], cells_ref[:BAND_CELLS]).astype(bf16)
    qkv_ref[...] = dot(xs_ref[...], wqkv_ref[...]).astype(bf16)
    attend([False] * LOCAL, qkv_ref, mixed_ref, probs_ref)
    att_ref[...] = dot(mixed_ref[...], wproj_ref[...]).astype(bf16)


def outer_kernel(
    tok_ref, cells_ref, lat_ref, lon_ref, diag_ref, gain_ref, wqkv_ref, wproj_ref, pick_ref, shift_ref, cells_pick_ref,
    att0_ref,
    xs_ref, qkv_ref, mixed_ref, probs_ref, tok_out_ref, summed_ref, row_ref,
    att_ref,
):
    def normed(values):
        return norm_parts(values)[0] * gain_ref[...]

    lat, lon, diag = lat_ref[...], lon_ref[:EDGE].astype(f32), diag_ref[:TURN].astype(f32)
    first, second = band_sources(cells_ref[...], normed(lat.astype(f32)).astype(bf16), normed(lon), normed(diag))
    xs_ref[:PAD] = dot(pick_ref[INNER:], first).astype(bf16)
    xs_ref[PAD:] = dot(pick_ref[...], second).astype(bf16)
    qkv_ref[...] = dot(xs_ref[...], wqkv_ref[...]).astype(bf16)
    attend([False] + [True] * PER_BAND, qkv_ref, mixed_ref, probs_ref)
    att_ref[:INNER] = att0_ref[...]
    att_ref[INNER:] = dot(mixed_ref[...], wproj_ref[...]).astype(bf16)
    for band, source in enumerate(band_sources(tok_ref[TOP:], lat, lon, diag)):
        rows = pl.ds(band * BAND_CELLS, BAND_CELLS)
        tokens = dot(shift_ref[...], source)
        added = dot(cells_pick_ref[...], att_ref[pl.ds(band * BAND, BAND)])
        tok_out_ref[rows] = tokens.astype(bf16)
        summed_ref[rows] = (tokens + added).astype(bf16)
    row_ref[...] = summed_ref[:COLS]


def cotangent_kernel(
    g_ref, lat_ref, lon_ref, diag_ref, gain_ref, shift_ref, wmerge_ref, out_ref, weights_ref, sem
):
    copy = pltpu.make_async_copy(wmerge_ref, weights_ref, sem)
    copy.start()
    parts = []
    for half in range(2):
        lat = lat_ref[half * PAIR_TOP : (half + 1) * PAIR_TOP]
        at = EDGE + half * PAIR_SIDE
        lon = lon_ref[at + PAIR_CORNER : at + PAIR_SIDE]
        diag = diag_ref[TURN + half * PAIR_CORNER : TURN + (half + 1) * PAIR_CORNER]
        own = g_ref[PAIR_TOP:, half * D : (half + 1) * D]
        parts.append(dot(shift_ref[...], jnp.concatenate([own, lat, lon, diag], axis=0)).astype(bf16))
    cots = jnp.concatenate(parts, axis=1)
    copy.wait()
    for k in range(4):
        out_ref[k] = dot_nt(cots, weights_ref[k * D : (k + 1) * D]) * gain_ref[k]


def pair_kernel(
    summed_ref, row_ref, gain_ref, cot_ref, pair_ref, unpair_ref,
    dsum_ref, out_row_ref, normed_ref,
    members_ref,
):
    quarter = COLS
    for part in range(3):
        first = COLS + part * 4 * COLS
        if part < 2:
            summed = summed_ref[first : first + 4 * COLS]
        else:
            summed = jnp.concatenate([summed_ref[first:], row_ref[...]], axis=0)
        paired = dot(pair_ref[...], summed)
        for k in range(4):
            members_ref[k, pl.ds(part * quarter, quarter)] = paired[k * quarter : (k + 1) * quarter]
    width = 4 * D
    total = sum(jnp.sum(members_ref[k], axis=-1, keepdims=True) for k in range(4))
    center = total / width
    for k in range(4):
        members_ref[k] = members_ref[k] - center
    spread = sum(jnp.sum(members_ref[k] * members_ref[k], axis=-1, keepdims=True) for k in range(4)) / width
    scale = lax.rsqrt(spread + EPS)
    for k in range(4):
        members_ref[k] = members_ref[k] * scale
        normed_ref[k] = (members_ref[k] * gain_ref[k]).astype(bf16)
    flat = sum(jnp.sum(cot_ref[k], axis=-1, keepdims=True) for k in range(4)) / width
    along = sum(jnp.sum(cot_ref[k] * members_ref[k], axis=-1, keepdims=True) for k in range(4)) / width
    for k in range(4):
        members_ref[k] = (cot_ref[k] - flat - members_ref[k] * along) * scale
    for part in range(3):
        rows = pl.ds(part * quarter, quarter)
        block = jnp.concatenate([members_ref[k, rows].astype(bf16) for k in range(4)], axis=0)
        dsum_ref[pl.ds(part * 4 * COLS, 4 * COLS)] = dot(unpair_ref[...], block).astype(bf16)
    out_row_ref[...] = dsum_ref[TOKENS - COLS :]


def merge_kernel(normed_ref, wmerge_ref, unshift_ref, main_ref, lat_ref, lon_ref, diag_ref):
    total = dot(normed_ref[0], wmerge_ref[:D])
    for k in range(1, 4):
        total = total + dot(normed_ref[k], wmerge_ref[k * D : (k + 1) * D])
    pairs = dot(unshift_ref[...], total.astype(bf16)).astype(bf16)
    main_ref[...] = pairs[: PAIRS - PAIR_TOP]
    lat_ref[...] = halves(pairs[PAIRS - PAIR_TOP : PAIRS])
    lon_ref[...] = halves(pairs[PAIRS : PAIRS + PAIR_SIDE - PAIR_CORNER])
    diag_ref[...] = halves(pairs[PAIRS + PAIR_SIDE - PAIR_CORNER :])


def inner_back_kernel(
    dsum_ref, qkv_ref, probs_ref, wproj_ref, pick_ref, xs0_ref, xs_ref, mixed0_ref, mixed_ref,
    up_ref, dqkv_ref, xst_ref, mixt_ref,
    dmix_ref,
):
    xst_ref[...] = jnp.concatenate([xs0_ref[...], xs_ref[...]], axis=0).T
    mixt_ref[...] = jnp.concatenate([mixed0_ref[...], mixed_ref[...]], axis=0).T
    up_ref[...] = dot(pick_ref[...], dsum_ref[BAND_CELLS - COLS : TOKENS - COLS]).astype(bf16)
    dmix_ref[...] = dot_nt(up_ref[...], wproj_ref[...]).astype(bf16)
    attend_back([(qkv_ref, probs_ref, win) for win in range(1, REST)], dmix_ref, dqkv_ref, 0)


def outer_back_kernel(
    dsum_ref, row_ref, xst_ref, mixt_ref, up1_ref, dqkv1_ref, qkv0_ref, probs0_ref, qkv_ref, probs_ref,
    wproj_ref, pick_ref,
    dqkv_ref, keep_ref, send_ref,
    up_ref, dmix_ref,
):
    cells = jnp.concatenate([row_ref[...], dsum_ref[: BAND_CELLS - COLS]], axis=0)
    up_ref[:BAND] = dot(pick_ref[...], cells).astype(bf16)
    up_ref[BAND:] = up1_ref[...]
    dqkv_ref[BAND:] = dqkv1_ref[...]
    dmix_ref[...] = dot_nt(up_ref[:BAND], wproj_ref[...]).astype(bf16)
    windows = [(qkv0_ref, probs0_ref, win) for win in range(LOCAL)] + [(qkv_ref, probs_ref, 0)]
    attend_back(windows, dmix_ref, dqkv_ref, 0)
    lat_at, lon_at = lax.axis_index("lat"), lax.axis_index("lon")
    even_core = lax.rem(lon_at, 2) == 0
    my_x = lax.rem(lax.div(lon_at, 2), 4)
    my_y = lax.div(lat_at, 8) * 2 + lax.div(lon_at, 8)
    x_steps = [lax.bitwise_xor(my_x, jnp.int32(i)) for i in range(4)]
    y_steps = [lax.bitwise_xor(my_y, jnp.int32(i)) for i in range(4)]
    for col in range(8):
        if col < 6:
            grad = dot(xst_ref[...], dqkv_ref[:, col * 256 : (col + 1) * 256])
        else:
            grad = dot(mixt_ref[...], up_ref[:, (col - 6) * 256 : (col - 5) * 256])
        even, odd = grad[:, :128], grad[:, 128:]
        kept = jnp.where(even_core, even, odd).astype(bf16)
        sent = jnp.where(even_core, odd, even).astype(bf16)
        low, x = divmod(col, 4)
        for lat in range(16):
            high, z = divmod(lat, 8)
            y = high * 2 + low
            rows = slice(lat * 32, (lat + 1) * 32)
            on_even = x_steps[x], lat * 2 + low
            on_odd = y_steps[y], z * 4 + x
            mine = [jnp.where(even_core, a, b) for a, b in zip(on_even, on_odd)]
            other = [jnp.where(even_core, b, a) for a, b in zip(on_even, on_odd)]
            keep_ref[mine[0], mine[1]] = kept[rows]
            send_ref[other[0], other[1]] = sent[rows]


def cells_back_kernel(
    dqkv_ref, wqkv_ref, cells_pick_ref, unshift_ref, tok_ref, dsum_ref, row_ref, gain_ref, m_lon_ref, m_diag_ref,
    main_ref, lat_ref, lon_ref, diag_ref,
    dx_ref,
):
    dx_ref[...] = dot_nt(dqkv_ref[...], wqkv_ref[...]).astype(bf16)
    for band in range(2):
        if band == 0:
            above = jnp.concatenate([row_ref[...], dsum_ref[: BAND_CELLS - COLS]], axis=0)
        else:
            above = dsum_ref[BAND_CELLS - COLS : TOKENS - COLS]
        cot = dot(cells_pick_ref[...], dx_ref[pl.ds(band * BAND, BAND)]) * gain_ref[...]
        normed, scale = norm_parts(tok_ref[pl.ds(band * BAND_CELLS, BAND_CELLS)].astype(f32))
        flat = jnp.mean(cot, axis=-1, keepdims=True)
        along = jnp.mean(cot * normed, axis=-1, keepdims=True)
        grads = (above.astype(f32) + (cot - flat - normed * along) * scale).astype(bf16)
        cells = dot(unshift_ref[...], grads).astype(bf16)
        if band == 0:
            main_ref[:BAND_CELLS] = cells[:BAND_CELLS]
        else:
            main_ref[BAND_CELLS:] = cells[: BAND_CELLS - TOP]
            lat_ref[...] = cells[BAND_CELLS - TOP : BAND_CELLS]
            diag_ref[:TURN] = cells[BAND_CELLS + SIDE - TURN :]
        lon_ref[band * SIDE : (band + 1) * SIDE] = cells[BAND_CELLS:]
    lon_ref[EDGE:] = m_lon_ref[...]
    diag_ref[TURN:] = m_diag_ref[...]


def fill_edge(field, side, rows, cols):
    width = field.shape[-1]
    field, side = field.astype(f32).reshape(rows, cols, width), side.astype(f32).reshape(rows, BORDER, width)
    first = field[:, :BORDER] + side
    return jnp.concatenate([first, field[:, BORDER:]], axis=1).reshape(rows * cols, width).astype(bf16)


def own_cells_kernel(main_ref, lat_ref, lon_ref, diag_ref, m_main_ref, m_lat_ref, tokens_ref, merged_ref):
    corner = diag_ref[:TURN].astype(f32)[TURN - CORNER :]
    beside = lon_ref[:EDGE].astype(f32)[: EDGE - CORNER]
    tokens_ref[:TOP] = fill_edge(lat_ref[...], corner, SHIFT_LAT, COLS)
    tokens_ref[TOP:] = fill_edge(main_ref[...], beside, ROWS - SHIFT_LAT, COLS)
    side_rows = PAIR_SIDE - PAIR_CORNER
    for half in range(2):
        cols = pl.ds(half * D, D)
        lat = m_lat_ref[half * PAIR_TOP : (half + 1) * PAIR_TOP]
        lon = lon_ref[EDGE + half * side_rows : EDGE + (half + 1) * side_rows]
        diag = diag_ref[TURN + half * PAIR_CORNER : TURN + (half + 1) * PAIR_CORNER]
        merged_ref[:PAIR_TOP, cols] = fill_edge(lat, diag, 2, PAIR_COLS)
        merged_ref[PAIR_TOP:, cols] = fill_edge(m_main_ref[:, cols], lon, PAIR_ROWS - 2, PAIR_COLS)


def add_kernel(a_ref, b_ref, *out_refs):
    for k, out_ref in enumerate(out_refs):
        out_ref[...] = (a_ref[k].astype(f32) + b_ref[k].astype(f32)).astype(bf16)


def join_kernel(a_ref, b_ref, c_ref, d_ref, out_ref):
    total = a_ref[...].astype(f32) + b_ref[...].astype(f32) + c_ref[...].astype(f32) + d_ref[...].astype(f32)
    out_ref[...] = total.astype(bf16)


def sum_kernel(parts_ref, out_ref):
    total = parts_ref[0].astype(f32)
    for i in range(1, parts_ref.shape[0]):
        total = total + parts_ref[i].astype(f32)
    out_ref[...] = total.astype(out_ref.dtype)


def call(kernel, outs, scratch=(), places=None, limit=20):
    spaces = {} if places is None else {
        "in_specs": [pl.BlockSpec(memory_space=(pltpu.VMEM, pl.ANY, pltpu.HBM)[p]) for p in places]
    }
    return pl.pallas_call(
        kernel,
        out_shape=[jax.ShapeDtypeStruct(s, t) for s, t in outs],
        scratch_shapes=[pltpu.VMEM(*s) if isinstance(s, tuple) else s for s in scratch],
        cost_estimate=pl.CostEstimate(flops=10**9, bytes_accessed=2 * 10**6, transcendentals=0),
        compiler_params=pltpu.CompilerParams(vmem_limit_bytes=limit * 1024 * 1024),
        **spaces,
    )


def saved(count):
    rows = count * PAD
    return [((rows, D), bf16), ((rows, 3 * D), bf16), ((rows, D), bf16), ((count, 2, PAD, GROUP * PAD), f32)]


def after(value, *others):
    return lax.optimization_barrier((value, *others))[0]


def chain(tok, gain, w_qkv, w_proj, gain_merge, w_merge, g_merged, fetch, up, down):
    tok, g_merged, top, g_top, edge, corner = call(
        border_kernel,
        [
            ((TOKENS, D), bf16), ((PAIRS, 2 * D), bf16),
            ((TOP, D), bf16), ((2 * PAIR_TOP, D), bf16),
            ((EDGE + 2 * PAIR_SIDE, D), bf16), ((TURN + 2 * PAIR_CORNER, D), bf16),
        ],
        [pltpu.SemaphoreType.DMA((2,))],
        [2, 2],
    )(tok, g_merged)
    beside = fetch(top, edge, corner)
    g_lat = up(g_top)
    pair, band = pair_selector(), band_selector()
    shift = shift_selector(WIN_LAT, COLS, SHIFT_LON)
    pair_shift = shift_selector(PAIR_ROWS, PAIR_COLS, SHIFT_LON // 2)
    held = [gain, jnp.asarray(band @ shift, bf16), w_qkv, w_proj, gain_merge]
    held += [jnp.asarray(c, bf16) for c in (shift, band.T, pair, pair.T, pair_shift)]
    got = call(
        inner_kernel,
        [(h.shape, h.dtype) for h in held] + [((TOKENS - TOP, D), bf16)] + saved(LOCAL) + [((INNER, D), bf16)],
        [pltpu.SemaphoreType.DMA((HELD,))],
        [0] + [1] * HELD,
    )(tok, *held)
    gain, pick, w_qkv, w_proj, gain_merge, shift, cells_pick, pair, unpair, pair_shift = got[:HELD]
    cells, xs0, qkv0, mixed0, probs0, att0 = got[HELD:]
    xs1, qkv1, mixed1, probs1, tok, summed, row = call(
        outer_kernel,
        saved(REST) + [((TOKENS, D), bf16), ((TOKENS, D), bf16), ((COLS, D), bf16)],
        [((WIDTH, D), bf16)],
    )(tok, cells, *beside, gain, w_qkv, w_proj, pick, shift, cells_pick, att0)
    last = up(row)
    cots, w_merge = call(
        cotangent_kernel,
        [((4, PAIRS, D), f32), ((4 * D, 2 * D), bf16)],
        [pltpu.SemaphoreType.DMA],
        [0] * 6 + [1],
    )(after(g_merged, row), g_lat, *beside[1:], gain_merge, pair_shift, w_merge)
    d_summed, row, merge_normed = call(
        pair_kernel,
        [((TOKENS, D), bf16), ((COLS, D), bf16), ((4, PAIRS, D), bf16)],
        [((4, PAIRS, D), f32)],
    )(summed, last, gain_merge, cots, pair, unpair)
    first = down(row)
    band = jnp.asarray(band_selector(), bf16)
    unshift = jnp.asarray(shift_selector(WIN_LAT, COLS, SHIFT_LON).T, bf16)
    pair_unshift = jnp.asarray(shift_selector(PAIR_ROWS, PAIR_COLS, SHIFT_LON // 2).T, bf16)
    up1, dqkv1, xst, mixt = call(
        inner_back_kernel,
        [((BAND, D), bf16), ((BAND, 3 * D), bf16), ((D, WIDTH), bf16), ((D, WIDTH), bf16)],
        [((BAND, D), bf16)],
    )(d_summed, qkv1, probs1, w_proj, band, xs0, xs1, mixed0, mixed1)
    m_main, m_lat, m_lon, m_diag = call(
        merge_kernel,
        [
            ((PAIRS - PAIR_TOP, 2 * D), bf16), ((2 * PAIR_TOP, D), bf16),
            ((2 * (PAIR_SIDE - PAIR_CORNER), D), bf16), ((2 * PAIR_CORNER, D), bf16),
        ],
    )(merge_normed, w_merge, pair_unshift)
    m_lat = down(m_lat)
    dqkv, keep, sent = call(
        outer_back_kernel,
        [((WIDTH, 3 * D), bf16), ((4, 32, 32, 128), bf16), ((4, 32, 32, 128), bf16)],
        [((WIDTH, D), bf16), ((BAND, D), bf16)],
    )(d_summed, first, xst, mixt, after(up1, m_main), dqkv1, qkv0, probs0, qkv1, probs1, w_proj, band)
    main, to_lat, to_lon, to_diag = call(
        cells_back_kernel,
        [
            ((TOKENS - TOP, D), bf16), ((TOP, D), bf16),
            ((EDGE + 2 * (PAIR_SIDE - PAIR_CORNER), D), bf16), ((TURN + 2 * PAIR_CORNER, D), bf16),
        ],
        [((WIDTH, D), bf16)],
    )(dqkv, w_qkv, cells_pick, unshift, tok, d_summed, first, gain, m_lon, m_diag)

    def finish(lat, lon, diag):
        grad_tokens, merged = call(own_cells_kernel, [((TOKENS, D), bf16), ((PAIRS, 2 * D), bf16)])(
            main, lat, lon, diag, m_main, m_lat
        )
        return merged, grad_tokens

    return finish, keep, sent, (to_lat, to_lon, to_diag), m_lat


def solution(mesh):
    lats, lons = mesh.shape["lat"], mesh.shape["lon"]
    count = lats * lons

    def send(block, down, right):
        route = [
            (i, (i // lons + down) % lats * lons + (i % lons + right) % lons) for i in range(count)
        ]
        return lax.ppermute(block, ("lat", "lon"), route)

    def fetch(top, edge, corner):
        return send(top, -1, 0), send(edge, 0, -1), send(corner, -1, -1)

    def place(i):
        lat, lon = divmod(i, lons)
        return lat // 8, lat % 8, lon // 8, lon // 2 % 4, lon % 2

    def across(i, step):
        high, z, low, x, core = place(i)
        if core:
            high, low = divmod((high * 2 + low) ^ step, 2)
        else:
            x = x ^ step
        return (high * 8 + z) * lons + low * 8 + x * 2 + core

    rest = {}
    for i in range(count):
        high, z, low, x, core = place(i)
        rest.setdefault((core, high * 2 + low if core else x), []).append(i)
    rest = list(rest.values())

    def swap(block, step):
        return lax.ppermute(block, ("lat", "lon"), [(i, across(i, step)) for i in range(count)])

    def reduce_across(keep, sent, to_lat):
        other = lax.ppermute(sent, ("lat", "lon"), [(i, i ^ 1) for i in range(count)])
        own, *others = call(add_kernel, [((32, 32, 128), bf16)] * 4)(keep, after(other, to_lat))
        got = [swap(block, step) for step, block in enumerate(others, 1)]
        return call(join_kernel, [((32, 32, 128), bf16)])(own, *got)[0]

    def reduce_rest(sums):
        parts = lax.all_to_all(sums, ("lat", "lon"), 0, 0, axis_index_groups=rest, tiled=True)
        return call(sum_kernel, [((32, 128), f32)])(parts)[0]

    def body(tokens, gain_attn, w_qkv, w_proj, gain_merge, w_merge, g_merged):
        finish, keep, sent, pieces, m_lat = chain(
            tokens.reshape(TOKENS, D), gain_attn.reshape(1, D), w_qkv, w_proj, gain_merge.reshape(4, 1, D),
            w_merge, g_merged.reshape(PAIRS, 2 * D), fetch,
            lambda row: send(row, -1, 0), lambda row: send(row, 1, 0),
        )
        sums = after(reduce_across(keep, sent, pieces[0]), m_lat)
        grad_weights = reduce_rest(sums)
        to_lat, to_lon, to_diag = pieces
        beside = send(to_lat, 1, 0), send(to_lon, 0, 1), send(to_diag, 1, 1)
        merged, grad_tokens = finish(*(after(piece, sums) for piece in beside))
        return (
            merged.reshape(ROWS // 2, COLS // 2, 2 * D),
            grad_tokens.reshape(ROWS, COLS, D),
            grad_weights,
        )

    return jax.shard_map(
        body,
        mesh=mesh,
        in_specs=(P("lat", "lon", None), P(), P(), P(), P(), P(), P("lat", "lon", None)),
        out_specs=(P("lat", "lon", None), P("lat", "lon", None), P("lat", "lon")),
        check_vma=False,
    )
```

```python
import jax
import jax.numpy as jnp
import numpy as np
from jax import lax
from jax.experimental import pallas as pl
from jax.experimental.pallas import tpu as pltpu
from jax.sharding import PartitionSpec as P

D = 512
HEADS = 8
HEAD = D // HEADS
WIN_LAT = 6
WIN_LON = 12
SHIFT_LAT = 3
SHIFT_LON = 6
EPS = 1e-05

ROWS, COLS = 12, 48
BORDER = 8
TOKENS = ROWS * COLS
LEN = WIN_LAT * WIN_LON
PAD = 80
PER_BAND = COLS // WIN_LON
BAND = PER_BAND * PAD
WINDOWS = 2 * PER_BAND
TOP = SHIFT_LAT * COLS
EDGE = ROWS * BORDER
CORNER = SHIFT_LAT * BORDER
SIDE = WIN_LAT * BORDER
TURN = 4 * BORDER
BAND_CELLS = WIN_LAT * COLS
GROUP = HEADS // 2
GROUP_WIDTH = GROUP * HEAD
LOCAL = PER_BAND - 1
INNER = LOCAL * PAD
REST = WINDOWS - LOCAL
OUTER = REST * PAD
PAIR_ROWS, PAIR_COLS = ROWS // 2, COLS // 2
PAIRS = PAIR_ROWS * PAIR_COLS
PAIR_TOP = 2 * PAIR_COLS
PAIR_SIDE = PAIR_ROWS * BORDER
PAIR_CORNER = 2 * BORDER
HELD = 10
WIDTH = WINDOWS * PAD
NEG = -1e30

f32 = jnp.float32
bf16 = jnp.bfloat16


def band_selector():
    pick = np.zeros((BAND, BAND_CELLS), np.float32)
    for win in range(PER_BAND):
        for i in range(WIN_LAT):
            for j in range(WIN_LON):
                pick[win * PAD + i * WIN_LON + j, i * COLS + win * WIN_LON + j] = 1.0
    return pick


def shift_selector(rows, cols, shift):
    pick = np.zeros((rows * cols, rows * (cols + BORDER)), np.float32)
    for i in range(rows):
        for j in range(cols):
            col = j + shift
            pick[i * cols + j, i * cols + col if col < cols else rows * cols + i * BORDER + col - cols] = 1.0
    return pick


def pair_selector():
    pick = np.zeros((4 * COLS, 4 * COLS), np.float32)
    quarter = COLS
    for a in range(2):
        for b in range(COLS // 2):
            for k, (i, j) in enumerate(((0, 0), (1, 0), (0, 1), (1, 1))):
                pick[k * quarter + a * (COLS // 2) + b, (2 * a + i) * COLS + 2 * b + j] = 1.0
    return pick


def dot(a, b):
    return lax.dot_general(a, b, (((1,), (0,)), ((), ())), preferred_element_type=f32)


def dot_nt(a, b):
    return lax.dot_general(a, b, (((1,), (1,)), ((), ())), preferred_element_type=f32)


def dot_tn(a, b):
    return lax.dot_general(a, b, (((0,), (0,)), ((), ())), preferred_element_type=f32)


def norm_parts(values):
    centred = values - jnp.mean(values, axis=-1, keepdims=True)
    scale = lax.rsqrt(jnp.mean(centred * centred, axis=-1, keepdims=True) + EPS)
    return centred * scale, scale


def band_sources(cells, lat, lon, diag):
    first = jnp.concatenate([cells[:BAND_CELLS], lon[CORNER : CORNER + SIDE].astype(bf16)], axis=0)
    beside = jnp.concatenate([lon[CORNER + SIDE : EDGE], diag[:CORNER]], axis=0).astype(bf16)
    second = jnp.concatenate([cells[BAND_CELLS:], lat, beside], axis=0)
    return first, second


def halves(block):
    return jnp.concatenate([block[:, :D], block[:, D:]], axis=0)


def head_masks():
    lane = lax.broadcasted_iota(jnp.int32, (1, GROUP_WIDTH), 1) // HEAD
    return [(lane == h).astype(f32).astype(bf16) for h in range(GROUP)]


def spread_heads(block, masks):
    return jnp.concatenate([block * m for m in masks], axis=0)


def per_head(stacked, block):
    first = lax.broadcasted_iota(jnp.int32, (1, 2 * HEAD), 1) < HEAD
    all_heads = dot_tn(stacked, block)
    out = []
    for pair in range(GROUP // 2):
        part = all_heads[:, pair * 2 * HEAD : (pair + 1) * 2 * HEAD]
        at = pair * 2 * PAD
        out.append(jnp.where(first, part[at : at + PAD], part[at + PAD : at + 2 * PAD]))
    return jnp.concatenate(out, axis=1)


def last_band():
    at_end = lax.axis_index("lat") == lax.axis_size("lat") - 1
    return jnp.where(at_end, f32(1), f32(0))


def halves_apart():
    shape = (LEN, GROUP * PAD)
    key = lax.broadcasted_iota(jnp.int32, shape, 0)
    query = lax.rem(lax.broadcasted_iota(jnp.int32, shape, 1), PAD)
    return jnp.where((key < LEN // 2) != (query < LEN // 2), f32(NEG), f32(0)) * last_band()


def attend(windows, qkv_ref, mixed_ref, probs_ref):
    masks = [m * HEAD ** (-0.5) for m in head_masks()]
    apart = halves_apart() if any(windows) else None
    for win, wraps in enumerate(windows):
        rows = pl.ds(win * PAD, PAD)
        for g in range(2):
            at = g * GROUP_WIDTH
            queries = spread_heads(qkv_ref[rows, at : at + GROUP_WIDTH], masks)
            keys = qkv_ref[rows, D + at : D + at + GROUP_WIDTH]
            values = qkv_ref[rows, 2 * D + at : 2 * D + at + GROUP_WIDTH]
            scores = dot_nt(keys, queries)[:LEN]
            if wraps:
                scores = scores + apart
            weights = jnp.exp(scores - jnp.max(scores, axis=0, keepdims=True))
            probs = weights * (1.0 / jnp.sum(weights, axis=0, keepdims=True))
            probs = jnp.concatenate([probs, jnp.zeros((PAD - LEN, GROUP * PAD), f32)], axis=0)
            probs_ref[win, g] = probs
            mixed_ref[rows, at : at + GROUP_WIDTH] = per_head(probs.astype(bf16), values).astype(bf16)


def attend_back(windows, dmix_ref, dqkv_ref, offset):
    masks = head_masks()
    scaled = [m * HEAD ** (-0.5) for m in masks]
    for win, (qkv_ref, probs_ref, place) in enumerate(windows):
        rows = pl.ds(place * PAD, PAD)
        out = pl.ds(offset + win * PAD, PAD)
        for g in range(2):
            at = g * GROUP_WIDTH
            queries = spread_heads(qkv_ref[rows, at : at + GROUP_WIDTH], scaled)
            keys = qkv_ref[rows, D + at : D + at + GROUP_WIDTH]
            values = qkv_ref[rows, 2 * D + at : 2 * D + at + GROUP_WIDTH]
            above = spread_heads(dmix_ref[pl.ds(win * PAD, PAD), at : at + GROUP_WIDTH], masks)
            probs = probs_ref[place, g]
            d_probs = dot_nt(values, above)
            along = jnp.sum(probs * d_probs, axis=0, keepdims=True)
            d_scores = (probs * (d_probs - along)).astype(bf16)
            d_queries = per_head(d_scores, keys) * HEAD ** (-0.5)
            d_keys = dot(d_scores, queries)
            d_values = dot(probs.astype(bf16), above)
            dqkv_ref[out, at : at + GROUP_WIDTH] = d_queries.astype(bf16)
            dqkv_ref[out, D + at : D + at + GROUP_WIDTH] = d_keys.astype(bf16)
            dqkv_ref[out, 2 * D + at : 2 * D + at + GROUP_WIDTH] = d_values.astype(bf16)


def border_kernel(tok_ref, g_ref, own_ref, own_g_ref, top_ref, g_top_ref, edge_ref, corner_ref, sem):
    copies = [
        pltpu.make_async_copy(tok_ref, own_ref, sem.at[0]),
        pltpu.make_async_copy(g_ref, own_g_ref, sem.at[1]),
    ]
    for copy in copies:
        copy.start()
    for copy in copies:
        copy.wait()
    edge = [own_ref[row * COLS : row * COLS + 16].astype(f32)[:BORDER] for row in range(ROWS)]
    cots = own_g_ref[...].astype(f32)
    side = [cots[row * PAIR_COLS : row * PAIR_COLS + BORDER] for row in range(PAIR_ROWS)]
    top_ref[...] = own_ref[:TOP]
    g_top_ref[...] = halves(own_g_ref[:PAIR_TOP])
    edge_ref[:EDGE] = jnp.concatenate(edge, axis=0).astype(bf16)
    edge_ref[EDGE:] = halves(jnp.concatenate(side, axis=0).astype(bf16))
    corner_ref[:TURN] = jnp.concatenate(edge[:4], axis=0).astype(bf16)
    corner_ref[TURN:] = halves(jnp.concatenate(side[:2], axis=0).astype(bf16))


def inner_kernel(tok_ref, *refs):
    held, got = refs[:HELD], refs[HELD : 2 * HELD]
    cells_ref, xs_ref, qkv_ref, mixed_ref, probs_ref, att_ref, sem = refs[2 * HELD :]
    copies = [pltpu.make_async_copy(a, b, sem.at[i]) for i, (a, b) in enumerate(zip(held, got))]
    for copy in copies:
        copy.start()
    gain_ref, pick_ref, wqkv_ref, wproj_ref = got[:4]
    normed = norm_parts(tok_ref[TOP:].astype(f32))[0]
    for copy in copies:
        copy.wait()
    cells_ref[...] = (normed * gain_ref[...]).astype(bf16)
    xs_ref[...] = dot(pick_ref[:INNER, :BAND_CELLS], cells_ref[:BAND_CELLS]).astype(bf16)
    qkv_ref[...] = dot(xs_ref[...], wqkv_ref[...]).astype(bf16)
    attend([False] * LOCAL, qkv_ref, mixed_ref, probs_ref)
    att_ref[...] = dot(mixed_ref[...], wproj_ref[...]).astype(bf16)


def outer_kernel(
    tok_ref, cells_ref, lat_ref, lon_ref, diag_ref, gain_ref, wqkv_ref, wproj_ref, pick_ref, shift_ref, cells_pick_ref,
    att0_ref,
    xs_ref, qkv_ref, mixed_ref, probs_ref, tok_out_ref, summed_ref, row_ref,
    att_ref,
):
    def normed(values):
        return norm_parts(values)[0] * gain_ref[...]

    lat, lon, diag = lat_ref[...], lon_ref[:EDGE].astype(f32), diag_ref[:TURN].astype(f32)
    first, second = band_sources(cells_ref[...], normed(lat.astype(f32)).astype(bf16), normed(lon), normed(diag))
    xs_ref[:PAD] = dot(pick_ref[INNER:], first).astype(bf16)
    xs_ref[PAD:] = dot(pick_ref[...], second).astype(bf16)
    qkv_ref[...] = dot(xs_ref[...], wqkv_ref[...]).astype(bf16)
    attend([False] + [True] * PER_BAND, qkv_ref, mixed_ref, probs_ref)
    att_ref[:INNER] = att0_ref[...]
    att_ref[INNER:] = dot(mixed_ref[...], wproj_ref[...]).astype(bf16)
    for band, source in enumerate(band_sources(tok_ref[TOP:], lat, lon, diag)):
        rows = pl.ds(band * BAND_CELLS, BAND_CELLS)
        tokens = dot(shift_ref[...], source)
        added = dot(cells_pick_ref[...], att_ref[pl.ds(band * BAND, BAND)])
        tok_out_ref[rows] = tokens.astype(bf16)
        summed_ref[rows] = (tokens + added).astype(bf16)
    row_ref[...] = summed_ref[:COLS]


def cotangent_kernel(
    g_ref, lat_ref, lon_ref, diag_ref, gain_ref, shift_ref, xs0_ref, xs_ref, mixed0_ref, mixed_ref, wmerge_ref,
    out_ref, weights_ref, xst_ref, mixt_ref, sem
):
    copy = pltpu.make_async_copy(wmerge_ref, weights_ref, sem)
    copy.start()
    xst_ref[...] = jnp.concatenate([xs0_ref[...], xs_ref[...]], axis=0).T
    mixt_ref[...] = jnp.concatenate([mixed0_ref[...], mixed_ref[...]], axis=0).T
    parts = []
    for half in range(2):
        lat = lat_ref[half * PAIR_TOP : (half + 1) * PAIR_TOP]
        at = EDGE + half * PAIR_SIDE
        lon = lon_ref[at + PAIR_CORNER : at + PAIR_SIDE]
        diag = diag_ref[TURN + half * PAIR_CORNER : TURN + (half + 1) * PAIR_CORNER]
        own = g_ref[PAIR_TOP:, half * D : (half + 1) * D]
        parts.append(dot(shift_ref[...], jnp.concatenate([own, lat, lon, diag], axis=0)).astype(bf16))
    cots = jnp.concatenate(parts, axis=1)
    copy.wait()
    for k in range(4):
        out_ref[k] = dot_nt(cots, weights_ref[k * D : (k + 1) * D]) * gain_ref[k]


def pair_kernel(
    summed_ref, row_ref, gain_ref, cot_ref, pair_ref, unpair_ref,
    dsum_ref, out_row_ref, normed_ref,
    members_ref,
):
    quarter = COLS
    for part in range(3):
        first = COLS + part * 4 * COLS
        if part < 2:
            summed = summed_ref[first : first + 4 * COLS]
        else:
            summed = jnp.concatenate([summed_ref[first:], row_ref[...]], axis=0)
        paired = dot(pair_ref[...], summed)
        for k in range(4):
            members_ref[k, pl.ds(part * quarter, quarter)] = paired[k * quarter : (k + 1) * quarter]
    width = 4 * D
    total = sum(jnp.sum(members_ref[k], axis=-1, keepdims=True) for k in range(4))
    center = total / width
    for k in range(4):
        members_ref[k] = members_ref[k] - center
    spread = sum(jnp.sum(members_ref[k] * members_ref[k], axis=-1, keepdims=True) for k in range(4)) / width
    scale = lax.rsqrt(spread + EPS)
    for k in range(4):
        members_ref[k] = members_ref[k] * scale
        normed_ref[k] = (members_ref[k] * gain_ref[k]).astype(bf16)
    flat = sum(jnp.sum(cot_ref[k], axis=-1, keepdims=True) for k in range(4)) / width
    along = sum(jnp.sum(cot_ref[k] * members_ref[k], axis=-1, keepdims=True) for k in range(4)) / width
    for k in range(4):
        members_ref[k] = (cot_ref[k] - flat - members_ref[k] * along) * scale
    for part in range(3):
        rows = pl.ds(part * quarter, quarter)
        block = jnp.concatenate([members_ref[k, rows].astype(bf16) for k in range(4)], axis=0)
        dsum_ref[pl.ds(part * 4 * COLS, 4 * COLS)] = dot(unpair_ref[...], block).astype(bf16)
    out_row_ref[...] = dsum_ref[TOKENS - COLS :]


def merge_kernel(
    normed_ref, wmerge_ref, unshift_ref, cells_lon_ref, cells_diag_ref, main_ref, lat_ref, lon_ref, diag_ref
):
    total = dot(normed_ref[0], wmerge_ref[:D])
    for k in range(1, 4):
        total = total + dot(normed_ref[k], wmerge_ref[k * D : (k + 1) * D])
    pairs = dot(unshift_ref[...], total.astype(bf16)).astype(bf16)
    main_ref[...] = pairs[: PAIRS - PAIR_TOP]
    lat_ref[...] = halves(pairs[PAIRS - PAIR_TOP : PAIRS])
    lon_ref[:EDGE] = cells_lon_ref[...]
    lon_ref[EDGE:] = halves(pairs[PAIRS : PAIRS + PAIR_SIDE - PAIR_CORNER])
    diag_ref[:TURN] = cells_diag_ref[...]
    diag_ref[TURN:] = halves(pairs[PAIRS + PAIR_SIDE - PAIR_CORNER :])


def inner_back_kernel(
    dsum_ref, qkv_ref, probs_ref, wproj_ref, pick_ref,
    up_ref, dqkv_ref,
    dmix_ref,
):
    up_ref[...] = dot(pick_ref[...], dsum_ref[BAND_CELLS - COLS : TOKENS - COLS]).astype(bf16)
    dmix_ref[...] = dot_nt(up_ref[...], wproj_ref[...]).astype(bf16)
    attend_back([(qkv_ref, probs_ref, win) for win in range(1, REST)], dmix_ref, dqkv_ref, 0)


def outer_back_kernel(
    dsum_ref, row_ref, xst_ref, mixt_ref, up1_ref, dqkv1_ref, qkv0_ref, probs0_ref, qkv_ref, probs_ref,
    wproj_ref, pick_ref,
    dqkv_ref, keep_ref, send_ref,
    up_ref, dmix_ref,
):
    cells = jnp.concatenate([row_ref[...], dsum_ref[: BAND_CELLS - COLS]], axis=0)
    up_ref[:BAND] = dot(pick_ref[...], cells).astype(bf16)
    up_ref[BAND:] = up1_ref[...]
    dqkv_ref[BAND:] = dqkv1_ref[...]
    dmix_ref[...] = dot_nt(up_ref[:BAND], wproj_ref[...]).astype(bf16)
    windows = [(qkv0_ref, probs0_ref, win) for win in range(LOCAL)] + [(qkv_ref, probs_ref, 0)]
    attend_back(windows, dmix_ref, dqkv_ref, 0)
    lat_at, lon_at = lax.axis_index("lat"), lax.axis_index("lon")
    even_core = lax.rem(lon_at, 2) == 0
    my_x = lax.rem(lax.div(lon_at, 2), 4)
    my_y = lax.div(lat_at, 8) * 2 + lax.div(lon_at, 8)
    x_steps = [lax.bitwise_xor(my_x, jnp.int32(i)) for i in range(4)]
    y_steps = [lax.bitwise_xor(my_y, jnp.int32(i)) for i in range(4)]
    for col in range(8):
        if col < 6:
            grad = dot(xst_ref[...], dqkv_ref[:, col * 256 : (col + 1) * 256])
        else:
            grad = dot(mixt_ref[...], up_ref[:, (col - 6) * 256 : (col - 5) * 256])
        even, odd = grad[:, :128], grad[:, 128:]
        kept = jnp.where(even_core, even, odd).astype(bf16)
        sent = jnp.where(even_core, odd, even).astype(bf16)
        low, x = divmod(col, 4)
        for lat in range(16):
            high, z = divmod(lat, 8)
            y = high * 2 + low
            rows = slice(lat * 32, (lat + 1) * 32)
            on_even = x_steps[x], lat * 2 + low
            on_odd = y_steps[y], z * 4 + x
            mine = [jnp.where(even_core, a, b) for a, b in zip(on_even, on_odd)]
            other = [jnp.where(even_core, b, a) for a, b in zip(on_even, on_odd)]
            keep_ref[mine[0], mine[1]] = kept[rows]
            send_ref[other[0], other[1]] = sent[rows]


def cells_back_kernel(
    dqkv_ref, wqkv_ref, cells_pick_ref, unshift_ref, tok_ref, dsum_ref, row_ref, gain_ref,
    main_ref, lat_ref, lon_ref, diag_ref,
    dx_ref,
):
    dx_ref[...] = dot_nt(dqkv_ref[...], wqkv_ref[...]).astype(bf16)
    for band in range(2):
        if band == 0:
            above = jnp.concatenate([row_ref[...], dsum_ref[: BAND_CELLS - COLS]], axis=0)
        else:
            above = dsum_ref[BAND_CELLS - COLS : TOKENS - COLS]
        cot = dot(cells_pick_ref[...], dx_ref[pl.ds(band * BAND, BAND)]) * gain_ref[...]
        normed, scale = norm_parts(tok_ref[pl.ds(band * BAND_CELLS, BAND_CELLS)].astype(f32))
        flat = jnp.mean(cot, axis=-1, keepdims=True)
        along = jnp.mean(cot * normed, axis=-1, keepdims=True)
        grads = (above.astype(f32) + (cot - flat - normed * along) * scale).astype(bf16)
        cells = dot(unshift_ref[...], grads).astype(bf16)
        if band == 0:
            main_ref[:BAND_CELLS] = cells[:BAND_CELLS]
        else:
            main_ref[BAND_CELLS:] = cells[: BAND_CELLS - TOP]
            lat_ref[...] = cells[BAND_CELLS - TOP : BAND_CELLS]
            diag_ref[...] = cells[BAND_CELLS + SIDE - TURN :]
        lon_ref[band * SIDE : (band + 1) * SIDE] = cells[BAND_CELLS:]


def fill_edge(field, side, rows, cols):
    width = field.shape[-1]
    field, side = field.astype(f32).reshape(rows, cols, width), side.astype(f32).reshape(rows, BORDER, width)
    first = field[:, :BORDER] + side
    return jnp.concatenate([first, field[:, BORDER:]], axis=1).reshape(rows * cols, width).astype(bf16)


def own_cells_kernel(main_ref, lat_ref, lon_ref, diag_ref, m_main_ref, m_lat_ref, tokens_ref, merged_ref):
    corner = diag_ref[:TURN].astype(f32)[TURN - CORNER :]
    beside = lon_ref[:EDGE].astype(f32)[: EDGE - CORNER]
    tokens_ref[:TOP] = fill_edge(lat_ref[...], corner, SHIFT_LAT, COLS)
    tokens_ref[TOP:] = fill_edge(main_ref[...], beside, ROWS - SHIFT_LAT, COLS)
    side_rows = PAIR_SIDE - PAIR_CORNER
    for half in range(2):
        cols = pl.ds(half * D, D)
        lat = m_lat_ref[half * PAIR_TOP : (half + 1) * PAIR_TOP]
        lon = lon_ref[EDGE + half * side_rows : EDGE + (half + 1) * side_rows]
        diag = diag_ref[TURN + half * PAIR_CORNER : TURN + (half + 1) * PAIR_CORNER]
        merged_ref[:PAIR_TOP, cols] = fill_edge(lat, diag, 2, PAIR_COLS)
        merged_ref[PAIR_TOP:, cols] = fill_edge(m_main_ref[:, cols], lon, PAIR_ROWS - 2, PAIR_COLS)


def add_kernel(a_ref, b_ref, *out_refs):
    for k, out_ref in enumerate(out_refs):
        out_ref[...] = (a_ref[k].astype(f32) + b_ref[k].astype(f32)).astype(bf16)


def join_kernel(a_ref, b_ref, c_ref, d_ref, out_ref):
    total = a_ref[...].astype(f32) + b_ref[...].astype(f32) + c_ref[...].astype(f32) + d_ref[...].astype(f32)
    out_ref[...] = total.astype(bf16)


def sum_kernel(parts_ref, out_ref):
    total = parts_ref[0].astype(f32)
    for i in range(1, parts_ref.shape[0]):
        total = total + parts_ref[i].astype(f32)
    out_ref[...] = total.astype(out_ref.dtype)


def call(kernel, outs, scratch=(), places=None, limit=20):
    spaces = {} if places is None else {
        "in_specs": [pl.BlockSpec(memory_space=(pltpu.VMEM, pl.ANY, pltpu.HBM)[p]) for p in places]
    }
    return pl.pallas_call(
        kernel,
        out_shape=[jax.ShapeDtypeStruct(s, t) for s, t in outs],
        scratch_shapes=[pltpu.VMEM(*s) if isinstance(s, tuple) else s for s in scratch],
        cost_estimate=pl.CostEstimate(flops=10**9, bytes_accessed=2 * 10**6, transcendentals=0),
        compiler_params=pltpu.CompilerParams(vmem_limit_bytes=limit * 1024 * 1024),
        **spaces,
    )


def saved(count):
    rows = count * PAD
    return [((rows, D), bf16), ((rows, 3 * D), bf16), ((rows, D), bf16), ((count, 2, PAD, GROUP * PAD), f32)]


def after(value, *others):
    return lax.optimization_barrier((value, *others))[0]


def chain(tok, gain, w_qkv, w_proj, gain_merge, w_merge, g_merged, fetch, up, down):
    tok, g_merged, top, g_top, edge, corner = call(
        border_kernel,
        [
            ((TOKENS, D), bf16), ((PAIRS, 2 * D), bf16),
            ((TOP, D), bf16), ((2 * PAIR_TOP, D), bf16),
            ((EDGE + 2 * PAIR_SIDE, D), bf16), ((TURN + 2 * PAIR_CORNER, D), bf16),
        ],
        [pltpu.SemaphoreType.DMA((2,))],
        [2, 2],
    )(tok, g_merged)
    beside = fetch(top, edge, corner)
    g_lat = up(g_top)
    pair, band = pair_selector(), band_selector()
    shift = shift_selector(WIN_LAT, COLS, SHIFT_LON)
    pair_shift = shift_selector(PAIR_ROWS, PAIR_COLS, SHIFT_LON // 2)
    held = [gain, jnp.asarray(band @ shift, bf16), w_qkv, w_proj, gain_merge]
    held += [jnp.asarray(c, bf16) for c in (shift, band.T, pair, pair.T, pair_shift)]
    got = call(
        inner_kernel,
        [(h.shape, h.dtype) for h in held] + [((TOKENS - TOP, D), bf16)] + saved(LOCAL) + [((INNER, D), bf16)],
        [pltpu.SemaphoreType.DMA((HELD,))],
        [0] + [1] * HELD,
    )(tok, *held)
    gain, pick, w_qkv, w_proj, gain_merge, shift, cells_pick, pair, unpair, pair_shift = got[:HELD]
    cells, xs0, qkv0, mixed0, probs0, att0 = got[HELD:]
    xs1, qkv1, mixed1, probs1, tok, summed, row = call(
        outer_kernel,
        saved(REST) + [((TOKENS, D), bf16), ((TOKENS, D), bf16), ((COLS, D), bf16)],
        [((WIDTH, D), bf16)],
    )(tok, cells, *beside, gain, w_qkv, w_proj, pick, shift, cells_pick, att0)
    last = up(row)
    cots, w_merge, xst, mixt = call(
        cotangent_kernel,
        [((4, PAIRS, D), f32), ((4 * D, 2 * D), bf16), ((D, WIDTH), bf16), ((D, WIDTH), bf16)],
        [pltpu.SemaphoreType.DMA],
        [0] * 10 + [1],
    )(after(g_merged, row), g_lat, *beside[1:], gain_merge, pair_shift, xs0, xs1, mixed0, mixed1, w_merge)
    d_summed, row, merge_normed = call(
        pair_kernel,
        [((TOKENS, D), bf16), ((COLS, D), bf16), ((4, PAIRS, D), bf16)],
        [((4, PAIRS, D), f32)],
    )(summed, last, gain_merge, cots, pair, unpair)
    first = down(row)
    band = jnp.asarray(band_selector(), bf16)
    unshift = jnp.asarray(shift_selector(WIN_LAT, COLS, SHIFT_LON).T, bf16)
    pair_unshift = jnp.asarray(shift_selector(PAIR_ROWS, PAIR_COLS, SHIFT_LON // 2).T, bf16)
    up1, dqkv1 = call(
        inner_back_kernel, [((BAND, D), bf16), ((BAND, 3 * D), bf16)], [((BAND, D), bf16)]
    )(d_summed, qkv1, probs1, w_proj, band)
    dqkv, keep, sent = call(
        outer_back_kernel,
        [((WIDTH, 3 * D), bf16), ((4, 32, 32, 128), bf16), ((4, 32, 32, 128), bf16)],
        [((WIDTH, D), bf16), ((BAND, D), bf16)],
    )(d_summed, first, xst, mixt, up1, dqkv1, qkv0, probs0, qkv1, probs1, w_proj, band)
    main, to_lat, to_lon, to_diag = call(
        cells_back_kernel,
        [((TOKENS - TOP, D), bf16), ((TOP, D), bf16), ((EDGE, D), bf16), ((TURN, D), bf16)],
        [((WIDTH, D), bf16)],
    )(dqkv, w_qkv, cells_pick, unshift, tok, d_summed, first, gain)

    def merge(ready):
        m_main, m_lat, lon, diag = call(
            merge_kernel,
            [
                ((PAIRS - PAIR_TOP, 2 * D), bf16), ((2 * PAIR_TOP, D), bf16),
                ((EDGE + 2 * (PAIR_SIDE - PAIR_CORNER), D), bf16), ((TURN + 2 * PAIR_CORNER, D), bf16),
            ],
        )(after(merge_normed, ready), w_merge, pair_unshift, to_lon, to_diag)
        return m_main, down(m_lat), to_lat, lon, diag

    def finish(lat, lon, diag, m_main, m_lat):
        grad_tokens, merged = call(own_cells_kernel, [((TOKENS, D), bf16), ((PAIRS, 2 * D), bf16)])(
            main, lat, lon, diag, m_main, m_lat
        )
        return merged, grad_tokens

    return merge, finish, keep, sent, to_lat


def solution(mesh):
    lats, lons = mesh.shape["lat"], mesh.shape["lon"]
    count = lats * lons

    def send(block, down, right):
        route = [
            (i, (i // lons + down) % lats * lons + (i % lons + right) % lons) for i in range(count)
        ]
        return lax.ppermute(block, ("lat", "lon"), route)

    def fetch(top, edge, corner):
        return send(top, -1, 0), send(edge, 0, -1), send(corner, -1, -1)

    def place(i):
        lat, lon = divmod(i, lons)
        return lat // 8, lat % 8, lon // 8, lon // 2 % 4, lon % 2

    def across(i, step):
        high, z, low, x, core = place(i)
        if core:
            high, low = divmod((high * 2 + low) ^ step, 2)
        else:
            x = x ^ step
        return (high * 8 + z) * lons + low * 8 + x * 2 + core

    rest = {}
    for i in range(count):
        high, z, low, x, core = place(i)
        rest.setdefault((core, high * 2 + low if core else x), []).append(i)
    rest = list(rest.values())

    def swap(block, step):
        return lax.ppermute(block, ("lat", "lon"), [(i, across(i, step)) for i in range(count)])

    def reduce_across(keep, sent, to_lat, merge):
        other = lax.ppermute(sent, ("lat", "lon"), [(i, i ^ 1) for i in range(count)])
        own, *others = call(add_kernel, [((32, 32, 128), bf16)] * 4)(keep, after(other, to_lat))
        got = [swap(block, step) for step, block in enumerate(others, 1)]
        m_main, m_lat, *pieces = merge(own)
        sums = call(join_kernel, [((32, 32, 128), bf16)])(after(own, m_main), *got)[0]
        return after(sums, m_lat), m_main, m_lat, pieces

    def reduce_rest(sums):
        parts = lax.all_to_all(sums, ("lat", "lon"), 0, 0, axis_index_groups=rest, tiled=True)
        return call(sum_kernel, [((32, 128), f32)])(parts)[0]

    def body(tokens, gain_attn, w_qkv, w_proj, gain_merge, w_merge, g_merged):
        merge, finish, keep, sent, to_lat = chain(
            tokens.reshape(TOKENS, D), gain_attn.reshape(1, D), w_qkv, w_proj, gain_merge.reshape(4, 1, D),
            w_merge, g_merged.reshape(PAIRS, 2 * D), fetch,
            lambda row: send(row, -1, 0), lambda row: send(row, 1, 0),
        )
        sums, m_main, m_lat, (to_lat, to_lon, to_diag) = reduce_across(keep, sent, to_lat, merge)
        grad_weights = reduce_rest(sums)
        beside = send(to_lat, 1, 0), send(to_lon, 0, 1), send(to_diag, 1, 1)
        merged, grad_tokens = finish(*(after(piece, sums) for piece in beside), m_main, m_lat)
        return (
            merged.reshape(ROWS // 2, COLS // 2, 2 * D),
            grad_tokens.reshape(ROWS, COLS, D),
            grad_weights,
        )

    return jax.shard_map(
        body,
        mesh=mesh,
        in_specs=(P("lat", "lon", None), P(), P(), P(), P(), P(), P("lat", "lon", None)),
        out_specs=(P("lat", "lon", None), P("lat", "lon", None), P("lat", "lon")),
        check_vma=False,
    )
```

```python
import jax
import jax.numpy as jnp
import numpy as np
from jax import lax
from jax.experimental import pallas as pl
from jax.experimental.pallas import tpu as pltpu
from jax.sharding import PartitionSpec as P

D = 512
HEADS = 8
HEAD = D // HEADS
WIN_LAT = 6
WIN_LON = 12
SHIFT_LAT = 3
SHIFT_LON = 6
EPS = 1e-05

ROWS, COLS = 12, 48
BORDER = 8
TOKENS = ROWS * COLS
LEN = WIN_LAT * WIN_LON
PAD = 80
PER_BAND = COLS // WIN_LON
BAND = PER_BAND * PAD
WINDOWS = 2 * PER_BAND
TOP = SHIFT_LAT * COLS
EDGE = ROWS * BORDER
CORNER = SHIFT_LAT * BORDER
SIDE = WIN_LAT * BORDER
TURN = 4 * BORDER
BAND_CELLS = WIN_LAT * COLS
GROUP = HEADS // 2
GROUP_WIDTH = GROUP * HEAD
LOCAL = PER_BAND - 1
INNER = LOCAL * PAD
REST = WINDOWS - LOCAL
OUTER = REST * PAD
PAIR_ROWS, PAIR_COLS = ROWS // 2, COLS // 2
PAIRS = PAIR_ROWS * PAIR_COLS
PAIR_TOP = PAIR_COLS
PAIR_SIDE = PAIR_ROWS * BORDER
PAIR_CORNER = BORDER
HELD = 10
WIDTH = WINDOWS * PAD
NEG = -1e30

f32 = jnp.float32
bf16 = jnp.bfloat16


def band_selector():
    pick = np.zeros((BAND, BAND_CELLS), np.float32)
    for win in range(PER_BAND):
        for i in range(WIN_LAT):
            for j in range(WIN_LON):
                pick[win * PAD + i * WIN_LON + j, i * COLS + win * WIN_LON + j] = 1.0
    return pick


def shift_selector(rows, cols, shift):
    pick = np.zeros((rows * cols, rows * (cols + BORDER)), np.float32)
    for i in range(rows):
        for j in range(cols):
            col = j + shift
            pick[i * cols + j, i * cols + col if col < cols else rows * cols + i * BORDER + col - cols] = 1.0
    return pick


def pair_selector():
    pick = np.zeros((4 * COLS, 4 * COLS), np.float32)
    quarter = COLS
    for a in range(2):
        for b in range(COLS // 2):
            for k, (i, j) in enumerate(((0, 0), (1, 0), (0, 1), (1, 1))):
                pick[k * quarter + a * (COLS // 2) + b, (2 * a + i) * COLS + 2 * b + j] = 1.0
    return pick


def dot(a, b):
    return lax.dot_general(a, b, (((1,), (0,)), ((), ())), preferred_element_type=f32)


def dot_nt(a, b):
    return lax.dot_general(a, b, (((1,), (1,)), ((), ())), preferred_element_type=f32)


def dot_tn(a, b):
    return lax.dot_general(a, b, (((0,), (0,)), ((), ())), preferred_element_type=f32)


def norm_parts(values):
    centred = values - jnp.mean(values, axis=-1, keepdims=True)
    scale = lax.rsqrt(jnp.mean(centred * centred, axis=-1, keepdims=True) + EPS)
    return centred * scale, scale


def band_sources(cells, lat, lon, diag):
    first = jnp.concatenate([cells[:BAND_CELLS], lon[CORNER : CORNER + SIDE].astype(bf16)], axis=0)
    beside = jnp.concatenate([lon[CORNER + SIDE : EDGE], diag[:CORNER]], axis=0).astype(bf16)
    second = jnp.concatenate([cells[BAND_CELLS:], lat, beside], axis=0)
    return first, second


def halves(block):
    return jnp.concatenate([block[:, :D], block[:, D:]], axis=0)


def head_masks():
    lane = lax.broadcasted_iota(jnp.int32, (1, GROUP_WIDTH), 1) // HEAD
    return [(lane == h).astype(f32).astype(bf16) for h in range(GROUP)]


def spread_heads(block, masks):
    return jnp.concatenate([block * m for m in masks], axis=0)


def per_head(stacked, block):
    first = lax.broadcasted_iota(jnp.int32, (1, 2 * HEAD), 1) < HEAD
    all_heads = dot_tn(stacked, block)
    out = []
    for pair in range(GROUP // 2):
        part = all_heads[:, pair * 2 * HEAD : (pair + 1) * 2 * HEAD]
        at = pair * 2 * PAD
        out.append(jnp.where(first, part[at : at + PAD], part[at + PAD : at + 2 * PAD]))
    return jnp.concatenate(out, axis=1)


def last_band():
    at_end = lax.axis_index("lat") == lax.axis_size("lat") - 1
    return jnp.where(at_end, f32(1), f32(0))


def halves_apart():
    shape = (LEN, GROUP * PAD)
    key = lax.broadcasted_iota(jnp.int32, shape, 0)
    query = lax.rem(lax.broadcasted_iota(jnp.int32, shape, 1), PAD)
    return jnp.where((key < LEN // 2) != (query < LEN // 2), f32(NEG), f32(0)) * last_band()


def attend(windows, qkv_ref, mixed_ref, probs_ref):
    masks = [m * HEAD ** (-0.5) for m in head_masks()]
    apart = halves_apart() if any(windows) else None
    for win, wraps in enumerate(windows):
        rows = pl.ds(win * PAD, PAD)
        for g in range(2):
            at = g * GROUP_WIDTH
            queries = spread_heads(qkv_ref[rows, at : at + GROUP_WIDTH], masks)
            keys = qkv_ref[rows, D + at : D + at + GROUP_WIDTH]
            values = qkv_ref[rows, 2 * D + at : 2 * D + at + GROUP_WIDTH]
            scores = dot_nt(keys, queries)[:LEN]
            if wraps:
                scores = scores + apart
            weights = jnp.exp(scores - jnp.max(scores, axis=0, keepdims=True))
            probs = weights * (1.0 / jnp.sum(weights, axis=0, keepdims=True))
            probs = jnp.concatenate([probs, jnp.zeros((PAD - LEN, GROUP * PAD), f32)], axis=0)
            probs_ref[win, g] = probs
            mixed_ref[rows, at : at + GROUP_WIDTH] = per_head(probs.astype(bf16), values).astype(bf16)


def attend_back(windows, dmix_ref, dqkv_ref, offset):
    masks = head_masks()
    scaled = [m * HEAD ** (-0.5) for m in masks]
    for win, (qkv_ref, probs_ref, place) in enumerate(windows):
        rows = pl.ds(place * PAD, PAD)
        out = pl.ds(offset + win * PAD, PAD)
        for g in range(2):
            at = g * GROUP_WIDTH
            queries = spread_heads(qkv_ref[rows, at : at + GROUP_WIDTH], scaled)
            keys = qkv_ref[rows, D + at : D + at + GROUP_WIDTH]
            values = qkv_ref[rows, 2 * D + at : 2 * D + at + GROUP_WIDTH]
            above = spread_heads(dmix_ref[pl.ds(win * PAD, PAD), at : at + GROUP_WIDTH], masks)
            probs = probs_ref[place, g]
            d_probs = dot_nt(values, above)
            along = jnp.sum(probs * d_probs, axis=0, keepdims=True)
            d_scores = (probs * (d_probs - along)).astype(bf16)
            d_queries = per_head(d_scores, keys) * HEAD ** (-0.5)
            d_keys = dot(d_scores, queries)
            d_values = dot(probs.astype(bf16), above)
            dqkv_ref[out, at : at + GROUP_WIDTH] = d_queries.astype(bf16)
            dqkv_ref[out, D + at : D + at + GROUP_WIDTH] = d_keys.astype(bf16)
            dqkv_ref[out, 2 * D + at : 2 * D + at + GROUP_WIDTH] = d_values.astype(bf16)


def border_kernel(tok_ref, g_ref, own_ref, own_g_ref, top_ref, g_top_ref, edge_ref, corner_ref, sem):
    copies = [
        pltpu.make_async_copy(tok_ref, own_ref, sem.at[0]),
        pltpu.make_async_copy(g_ref, own_g_ref, sem.at[1]),
    ]
    for copy in copies:
        copy.start()
    for copy in copies:
        copy.wait()
    edge = [own_ref[row * COLS : row * COLS + 16].astype(f32)[:BORDER] for row in range(ROWS)]
    cots = own_g_ref[...].astype(f32)
    side = [cots[row * PAIR_COLS : row * PAIR_COLS + BORDER] for row in range(PAIR_ROWS)]
    top_ref[...] = own_ref[:TOP]
    g_top_ref[...] = halves(cots[:PAIR_TOP]).astype(bf16)
    edge_ref[:EDGE] = jnp.concatenate(edge, axis=0).astype(bf16)
    edge_ref[EDGE:] = halves(jnp.concatenate(side, axis=0).astype(bf16))
    corner_ref[:TURN] = jnp.concatenate(edge[:4], axis=0).astype(bf16)
    corner_ref[TURN:] = halves(side[0]).astype(bf16)


def inner_kernel(tok_ref, *refs):
    held, got = refs[:HELD], refs[HELD : 2 * HELD]
    cells_ref, xs_ref, qkv_ref, mixed_ref, probs_ref, att_ref, sem = refs[2 * HELD :]
    copies = [pltpu.make_async_copy(a, b, sem.at[i]) for i, (a, b) in enumerate(zip(held, got))]
    for copy in copies:
        copy.start()
    gain_ref, pick_ref, wqkv_ref, wproj_ref = got[:4]
    normed = norm_parts(tok_ref[TOP:].astype(f32))[0]
    for copy in copies:
        copy.wait()
    cells_ref[...] = (normed * gain_ref[...]).astype(bf16)
    xs_ref[...] = dot(pick_ref[:INNER, :BAND_CELLS], cells_ref[:BAND_CELLS]).astype(bf16)
    qkv_ref[...] = dot(xs_ref[...], wqkv_ref[...]).astype(bf16)
    attend([False] * LOCAL, qkv_ref, mixed_ref, probs_ref)
    att_ref[...] = dot(mixed_ref[...], wproj_ref[...]).astype(bf16)


def outer_kernel(
    tok_ref, cells_ref, lat_ref, lon_ref, diag_ref, gain_ref, wqkv_ref, wproj_ref, pick_ref, shift_ref, cells_pick_ref,
    att0_ref,
    xs_ref, qkv_ref, mixed_ref, probs_ref, tok_out_ref, summed_ref, row_ref,
    att_ref,
):
    def normed(values):
        return norm_parts(values)[0] * gain_ref[...]

    lat, lon, diag = lat_ref[...], lon_ref[:EDGE].astype(f32), diag_ref[:TURN].astype(f32)
    first, second = band_sources(cells_ref[...], normed(lat.astype(f32)).astype(bf16), normed(lon), normed(diag))
    xs_ref[:PAD] = dot(pick_ref[INNER:], first).astype(bf16)
    xs_ref[PAD:] = dot(pick_ref[...], second).astype(bf16)
    qkv_ref[...] = dot(xs_ref[...], wqkv_ref[...]).astype(bf16)
    attend([False] + [True] * PER_BAND, qkv_ref, mixed_ref, probs_ref)
    att_ref[:INNER] = att0_ref[...]
    att_ref[INNER:] = dot(mixed_ref[...], wproj_ref[...]).astype(bf16)
    for band, source in enumerate(band_sources(tok_ref[TOP:], lat, lon, diag)):
        rows = pl.ds(band * BAND_CELLS, BAND_CELLS)
        tokens = dot(shift_ref[...], source)
        added = dot(cells_pick_ref[...], att_ref[pl.ds(band * BAND, BAND)])
        tok_out_ref[rows] = tokens.astype(bf16)
        summed_ref[rows] = (tokens + added).astype(bf16)
    row_ref[...] = summed_ref[TOKENS - COLS :]


def cotangent_kernel(
    g_ref, lat_ref, lon_ref, diag_ref, gain_ref, shift_ref, wmerge_ref, out_ref, weights_ref, sem
):
    copy = pltpu.make_async_copy(wmerge_ref, weights_ref, sem)
    copy.start()
    parts = []
    for half in range(2):
        lat = lat_ref[...].astype(f32)[half * PAIR_TOP : (half + 1) * PAIR_TOP]
        at = EDGE + half * PAIR_SIDE
        lon = lon_ref[at : at + PAIR_SIDE].astype(f32)[PAIR_CORNER:]
        diag = diag_ref[TURN:].astype(f32)[half * PAIR_CORNER : (half + 1) * PAIR_CORNER]
        own = g_ref[:, half * D : (half + 1) * D].astype(f32)[PAIR_TOP:]
        source = jnp.concatenate([own, lat, lon, diag], axis=0).astype(bf16)
        parts.append(dot(shift_ref[...], source).astype(bf16))
    cots = jnp.concatenate(parts, axis=1)
    copy.wait()
    for k in range(4):
        out_ref[k] = dot_nt(cots, weights_ref[k * D : (k + 1) * D]) * gain_ref[k]


def pair_kernel(
    summed_ref, row_ref, gain_ref, cot_ref, pair_ref, unpair_ref,
    dsum_ref, out_row_ref, normed_ref,
    members_ref,
):
    quarter = COLS
    for part in range(3):
        first = part * 4 * COLS - COLS
        if part:
            summed = summed_ref[first : first + 4 * COLS]
        else:
            summed = jnp.concatenate([row_ref[...], summed_ref[: 3 * COLS]], axis=0)
        paired = dot(pair_ref[...], summed)
        for k in range(4):
            members_ref[k, pl.ds(part * quarter, quarter)] = paired[k * quarter : (k + 1) * quarter]
    width = 4 * D
    total = sum(jnp.sum(members_ref[k], axis=-1, keepdims=True) for k in range(4))
    center = total / width
    for k in range(4):
        members_ref[k] = members_ref[k] - center
    spread = sum(jnp.sum(members_ref[k] * members_ref[k], axis=-1, keepdims=True) for k in range(4)) / width
    scale = lax.rsqrt(spread + EPS)
    for k in range(4):
        members_ref[k] = members_ref[k] * scale
        normed_ref[k] = (members_ref[k] * gain_ref[k]).astype(bf16)
    flat = sum(jnp.sum(cot_ref[k], axis=-1, keepdims=True) for k in range(4)) / width
    along = sum(jnp.sum(cot_ref[k] * members_ref[k], axis=-1, keepdims=True) for k in range(4)) / width
    for k in range(4):
        members_ref[k] = (cot_ref[k] - flat - members_ref[k] * along) * scale
    for part in range(3):
        rows = pl.ds(part * quarter, quarter)
        block = jnp.concatenate([members_ref[k, rows].astype(bf16) for k in range(4)], axis=0)
        dsum_ref[pl.ds(part * 4 * COLS, 4 * COLS)] = dot(unpair_ref[...], block).astype(bf16)
    out_row_ref[...] = dsum_ref[:COLS]


def merge_kernel(normed_ref, wmerge_ref, unshift_ref, main_ref, lat_ref, lon_ref, diag_ref):
    total = dot(normed_ref[0], wmerge_ref[:D])
    for k in range(1, 4):
        total = total + dot(normed_ref[k], wmerge_ref[k * D : (k + 1) * D])
    pairs = dot(unshift_ref[...], total.astype(bf16))
    main_ref[...] = pairs[:PAIRS].astype(bf16)
    lat_ref[...] = halves(pairs[PAIRS - PAIR_TOP : PAIRS]).astype(bf16)
    lon_ref[...] = halves(pairs[PAIRS : PAIRS + PAIR_SIDE - PAIR_CORNER]).astype(bf16)
    diag_ref[...] = halves(pairs[PAIRS + PAIR_SIDE - PAIR_CORNER :]).astype(bf16)


def inner_back_kernel(
    dsum_ref, qkv0_ref, probs0_ref, qkv_ref, probs_ref, wproj_ref, pick_ref, xs0_ref, xs_ref, mixed0_ref, mixed_ref,
    up_ref, dqkv_ref, xst_ref, mixt_ref,
    dmix_ref,
):
    xst_ref[...] = jnp.concatenate([xs0_ref[...], xs_ref[...]], axis=0).T
    mixt_ref[...] = jnp.concatenate([mixed0_ref[...], mixed_ref[...]], axis=0).T
    up_ref[...] = dot(pick_ref[...], dsum_ref[COLS : COLS + BAND_CELLS]).astype(bf16)
    dmix_ref[...] = dot_nt(up_ref[...], wproj_ref[...]).astype(bf16)
    windows = [(qkv0_ref, probs0_ref, win) for win in range(LOCAL)] + [(qkv_ref, probs_ref, 0)]
    attend_back(windows, dmix_ref, dqkv_ref, 0)


def outer_back_kernel(
    dsum_ref, row_ref, xst_ref, mixt_ref, up0_ref, dqkv0_ref, qkv_ref, probs_ref, wproj_ref, pick_ref,
    dqkv_ref, keep_ref, send_ref,
    up_ref, dmix_ref,
):
    cells = jnp.concatenate([dsum_ref[COLS + BAND_CELLS :], row_ref[...]], axis=0)
    up_ref[:BAND] = up0_ref[...]
    up_ref[BAND:] = dot(pick_ref[...], cells).astype(bf16)
    dqkv_ref[:BAND] = dqkv0_ref[...]
    dmix_ref[...] = dot_nt(up_ref[BAND:], wproj_ref[...]).astype(bf16)
    attend_back([(qkv_ref, probs_ref, win) for win in range(1, REST)], dmix_ref, dqkv_ref, BAND)
    lat_at, lon_at = lax.axis_index("lat"), lax.axis_index("lon")
    even_core = lax.rem(lon_at, 2) == 0
    my_x = lax.rem(lax.div(lon_at, 2), 4)
    my_y = lax.div(lat_at, 8) * 2 + lax.div(lon_at, 8)
    x_steps = [lax.bitwise_xor(my_x, jnp.int32(i)) for i in range(4)]
    y_steps = [lax.bitwise_xor(my_y, jnp.int32(i)) for i in range(4)]
    for col in range(8):
        if col < 6:
            grad = dot(xst_ref[...], dqkv_ref[:, col * 256 : (col + 1) * 256])
        else:
            grad = dot(mixt_ref[...], up_ref[:, (col - 6) * 256 : (col - 5) * 256])
        even, odd = grad[:, :128], grad[:, 128:]
        kept = jnp.where(even_core, even, odd).astype(bf16)
        sent = jnp.where(even_core, odd, even).astype(bf16)
        low, x = divmod(col, 4)
        for lat in range(16):
            high, z = divmod(lat, 8)
            y = high * 2 + low
            rows = slice(lat * 32, (lat + 1) * 32)
            on_even = x_steps[x], lat * 2 + low
            on_odd = y_steps[y], z * 4 + x
            mine = [jnp.where(even_core, a, b) for a, b in zip(on_even, on_odd)]
            other = [jnp.where(even_core, b, a) for a, b in zip(on_even, on_odd)]
            keep_ref[mine[0], mine[1]] = kept[rows]
            send_ref[other[0], other[1]] = sent[rows]


def cells_back_kernel(
    dqkv_ref, wqkv_ref, cells_pick_ref, unshift_ref, tok_ref, dsum_ref, row_ref, gain_ref, m_lon_ref, m_diag_ref,
    main_ref, lat_ref, lon_ref, diag_ref,
    dx_ref,
):
    dx_ref[...] = dot_nt(dqkv_ref[...], wqkv_ref[...]).astype(bf16)
    for band in range(2):
        if band == 0:
            above = dsum_ref[COLS : COLS + BAND_CELLS]
        else:
            above = jnp.concatenate([dsum_ref[COLS + BAND_CELLS :], row_ref[...]], axis=0)
        cot = dot(cells_pick_ref[...], dx_ref[pl.ds(band * BAND, BAND)]) * gain_ref[...]
        normed, scale = norm_parts(tok_ref[pl.ds(band * BAND_CELLS, BAND_CELLS)].astype(f32))
        flat = jnp.mean(cot, axis=-1, keepdims=True)
        along = jnp.mean(cot * normed, axis=-1, keepdims=True)
        grads = (above.astype(f32) + (cot - flat - normed * along) * scale).astype(bf16)
        cells = dot(unshift_ref[...], grads).astype(bf16)
        if band == 0:
            main_ref[:BAND_CELLS] = cells[:BAND_CELLS]
        else:
            main_ref[BAND_CELLS:] = cells[: BAND_CELLS - TOP]
            lat_ref[...] = cells[BAND_CELLS - TOP : BAND_CELLS]
            diag_ref[:TURN] = cells[BAND_CELLS + SIDE - TURN :]
        lon_ref[band * SIDE : (band + 1) * SIDE] = cells[BAND_CELLS:]
    lon_ref[EDGE:] = m_lon_ref[...]
    diag_ref[TURN:] = m_diag_ref[...]


def fill_edge(field, side, rows, cols):
    width = field.shape[-1]
    field, side = field.astype(f32).reshape(rows, cols, width), side.astype(f32).reshape(rows, BORDER, width)
    first = field[:, :BORDER] + side
    return jnp.concatenate([first, field[:, BORDER:]], axis=1).reshape(rows * cols, width)


def own_cells_kernel(main_ref, lat_ref, lon_ref, diag_ref, m_main_ref, m_lat_ref, tokens_ref, merged_ref):
    corner = diag_ref[:TURN].astype(f32)[TURN - CORNER :]
    beside = lon_ref[:EDGE].astype(f32)[: EDGE - CORNER]
    tokens_ref[:TOP] = fill_edge(lat_ref[...], corner, SHIFT_LAT, COLS).astype(bf16)
    tokens_ref[TOP:] = fill_edge(main_ref[...], beside, ROWS - SHIFT_LAT, COLS).astype(bf16)
    side_rows = PAIR_SIDE - PAIR_CORNER
    for half in range(2):
        cols = pl.ds(half * D, D)
        lat = m_lat_ref[...].astype(f32)[half * PAIR_TOP : (half + 1) * PAIR_TOP]
        lon = lon_ref[EDGE:].astype(f32)[half * side_rows : (half + 1) * side_rows]
        diag = diag_ref[TURN:].astype(f32)[half * PAIR_CORNER : (half + 1) * PAIR_CORNER]
        own = m_main_ref[:, cols].astype(f32)[: PAIRS - PAIR_TOP]
        field, side = jnp.concatenate([lat, own], axis=0), jnp.concatenate([diag, lon], axis=0)
        merged_ref[:, cols] = fill_edge(field, side, PAIR_ROWS, PAIR_COLS).astype(bf16)


def add_kernel(a_ref, b_ref, *out_refs):
    for k, out_ref in enumerate(out_refs):
        out_ref[...] = (a_ref[k].astype(f32) + b_ref[k].astype(f32)).astype(bf16)


def join_kernel(a_ref, b_ref, c_ref, d_ref, out_ref):
    total = a_ref[...].astype(f32) + b_ref[...].astype(f32) + c_ref[...].astype(f32) + d_ref[...].astype(f32)
    out_ref[...] = total.astype(bf16)


def sum_kernel(parts_ref, out_ref):
    total = parts_ref[0].astype(f32)
    for i in range(1, parts_ref.shape[0]):
        total = total + parts_ref[i].astype(f32)
    out_ref[...] = total.astype(out_ref.dtype)


def call(kernel, outs, scratch=(), places=None, limit=20):
    spaces = {} if places is None else {
        "in_specs": [pl.BlockSpec(memory_space=(pltpu.VMEM, pl.ANY, pltpu.HBM)[p]) for p in places]
    }
    return pl.pallas_call(
        kernel,
        out_shape=[jax.ShapeDtypeStruct(s, t) for s, t in outs],
        scratch_shapes=[pltpu.VMEM(*s) if isinstance(s, tuple) else s for s in scratch],
        cost_estimate=pl.CostEstimate(flops=10**9, bytes_accessed=2 * 10**6, transcendentals=0),
        compiler_params=pltpu.CompilerParams(vmem_limit_bytes=limit * 1024 * 1024),
        **spaces,
    )


def saved(count):
    rows = count * PAD
    return [((rows, D), bf16), ((rows, 3 * D), bf16), ((rows, D), bf16), ((count, 2, PAD, GROUP * PAD), f32)]


def after(value, *others):
    return lax.optimization_barrier((value, *others))[0]


def chain(tok, gain, w_qkv, w_proj, gain_merge, w_merge, g_merged, fetch, up, down):
    tok, g_merged, top, g_top, edge, corner = call(
        border_kernel,
        [
            ((TOKENS, D), bf16), ((PAIRS, 2 * D), bf16),
            ((TOP, D), bf16), ((2 * PAIR_TOP, D), bf16),
            ((EDGE + 2 * PAIR_SIDE, D), bf16), ((TURN + 2 * PAIR_CORNER, D), bf16),
        ],
        [pltpu.SemaphoreType.DMA((2,))],
        [2, 2],
    )(tok, g_merged)
    beside = fetch(top, edge, corner)
    g_lat = up(g_top)
    pair, band = pair_selector(), band_selector()
    shift = shift_selector(WIN_LAT, COLS, SHIFT_LON)
    pair_shift = shift_selector(PAIR_ROWS, PAIR_COLS, SHIFT_LON // 2)
    held = [gain, jnp.asarray(band @ shift, bf16), w_qkv, w_proj, gain_merge]
    held += [jnp.asarray(c, bf16) for c in (shift, band.T, pair, pair.T, pair_shift)]
    got = call(
        inner_kernel,
        [(h.shape, h.dtype) for h in held] + [((TOKENS - TOP, D), bf16)] + saved(LOCAL) + [((INNER, D), bf16)],
        [pltpu.SemaphoreType.DMA((HELD,))],
        [0] + [1] * HELD,
    )(tok, *held)
    gain, pick, w_qkv, w_proj, gain_merge, shift, cells_pick, pair, unpair, pair_shift = got[:HELD]
    cells, xs0, qkv0, mixed0, probs0, att0 = got[HELD:]
    xs1, qkv1, mixed1, probs1, tok, summed, row = call(
        outer_kernel,
        saved(REST) + [((TOKENS, D), bf16), ((TOKENS, D), bf16), ((COLS, D), bf16)],
        [((WIDTH, D), bf16)],
    )(tok, cells, *beside, gain, w_qkv, w_proj, pick, shift, cells_pick, att0)
    behind = down(row)
    cots, w_merge = call(
        cotangent_kernel,
        [((4, PAIRS, D), f32), ((4 * D, 2 * D), bf16)],
        [pltpu.SemaphoreType.DMA],
        [0] * 6 + [1],
    )(after(g_merged, row), g_lat, *beside[1:], gain_merge, pair_shift, w_merge)
    d_summed, row, merge_normed = call(
        pair_kernel,
        [((TOKENS, D), bf16), ((COLS, D), bf16), ((4, PAIRS, D), bf16)],
        [((4, PAIRS, D), f32)],
    )(summed, behind, gain_merge, cots, pair, unpair)
    last = up(row)
    band = jnp.asarray(band_selector(), bf16)
    unshift = jnp.asarray(shift_selector(WIN_LAT, COLS, SHIFT_LON).T, bf16)
    pair_unshift = jnp.asarray(shift_selector(PAIR_ROWS, PAIR_COLS, SHIFT_LON // 2).T, bf16)
    up0, dqkv0, xst, mixt = call(
        inner_back_kernel,
        [((BAND, D), bf16), ((BAND, 3 * D), bf16), ((D, WIDTH), bf16), ((D, WIDTH), bf16)],
        [((BAND, D), bf16)],
    )(d_summed, qkv0, probs0, qkv1, probs1, w_proj, band, xs0, xs1, mixed0, mixed1)
    m_main, m_lat, m_lon, m_diag = call(
        merge_kernel,
        [
            ((PAIRS, 2 * D), bf16), ((2 * PAIR_TOP, D), bf16),
            ((2 * (PAIR_SIDE - PAIR_CORNER), D), bf16), ((2 * PAIR_CORNER, D), bf16),
        ],
    )(merge_normed, w_merge, pair_unshift)
    m_lat = down(m_lat)
    dqkv, keep, sent = call(
        outer_back_kernel,
        [((WIDTH, 3 * D), bf16), ((4, 32, 32, 128), bf16), ((4, 32, 32, 128), bf16)],
        [((WIDTH, D), bf16), ((BAND, D), bf16)],
    )(d_summed, last, xst, mixt, after(up0, m_main), dqkv0, qkv1, probs1, w_proj, band)
    main, to_lat, to_lon, to_diag = call(
        cells_back_kernel,
        [
            ((TOKENS - TOP, D), bf16), ((TOP, D), bf16),
            ((EDGE + 2 * (PAIR_SIDE - PAIR_CORNER), D), bf16), ((TURN + 2 * PAIR_CORNER, D), bf16),
        ],
        [((WIDTH, D), bf16)],
    )(dqkv, w_qkv, cells_pick, unshift, tok, d_summed, last, gain, m_lon, m_diag)

    def finish(lat, lon, diag):
        grad_tokens, merged = call(own_cells_kernel, [((TOKENS, D), bf16), ((PAIRS, 2 * D), bf16)])(
            main, lat, lon, diag, m_main, m_lat
        )
        return merged, grad_tokens

    return finish, keep, sent, (to_lat, to_lon, to_diag), m_lat


def solution(mesh):
    lats, lons = mesh.shape["lat"], mesh.shape["lon"]
    count = lats * lons

    def send(block, down, right):
        route = [
            (i, (i // lons + down) % lats * lons + (i % lons + right) % lons) for i in range(count)
        ]
        return lax.ppermute(block, ("lat", "lon"), route)

    def fetch(top, edge, corner):
        return send(top, -1, 0), send(edge, 0, -1), send(corner, -1, -1)

    def place(i):
        lat, lon = divmod(i, lons)
        return lat // 8, lat % 8, lon // 8, lon // 2 % 4, lon % 2

    def across(i, step):
        high, z, low, x, core = place(i)
        if core:
            high, low = divmod((high * 2 + low) ^ step, 2)
        else:
            x = x ^ step
        return (high * 8 + z) * lons + low * 8 + x * 2 + core

    rest = {}
    for i in range(count):
        high, z, low, x, core = place(i)
        rest.setdefault((core, high * 2 + low if core else x), []).append(i)
    rest = list(rest.values())

    def swap(block, step):
        return lax.ppermute(block, ("lat", "lon"), [(i, across(i, step)) for i in range(count)])

    def reduce_across(keep, sent, to_lat):
        other = lax.ppermute(sent, ("lat", "lon"), [(i, i ^ 1) for i in range(count)])
        own, *others = call(add_kernel, [((32, 32, 128), bf16)] * 4)(keep, after(other, to_lat))
        got = [swap(block, step) for step, block in enumerate(others, 1)]
        return call(join_kernel, [((32, 32, 128), bf16)])(own, *got)[0]

    def reduce_rest(sums):
        parts = lax.all_to_all(sums, ("lat", "lon"), 0, 0, axis_index_groups=rest, tiled=True)
        return call(sum_kernel, [((32, 128), f32)])(parts)[0]

    def body(tokens, gain_attn, w_qkv, w_proj, gain_merge, w_merge, g_merged):
        finish, keep, sent, pieces, m_lat = chain(
            tokens.reshape(TOKENS, D), gain_attn.reshape(1, D), w_qkv, w_proj, gain_merge.reshape(4, 1, D),
            w_merge, g_merged.reshape(PAIRS, 2 * D), fetch,
            lambda row: send(row, -1, 0), lambda row: send(row, 1, 0),
        )
        sums = after(reduce_across(keep, sent, pieces[0]), m_lat)
        grad_weights = reduce_rest(sums)
        to_lat, to_lon, to_diag = pieces
        beside = send(to_lat, 1, 0), send(to_lon, 0, 1), send(to_diag, 1, 1)
        merged, grad_tokens = finish(*(after(piece, sums) for piece in beside))
        return (
            merged.reshape(ROWS // 2, COLS // 2, 2 * D),
            grad_tokens.reshape(ROWS, COLS, D),
            grad_weights,
        )

    return jax.shard_map(
        body,
        mesh=mesh,
        in_specs=(P("lat", "lon", None), P(), P(), P(), P(), P(), P("lat", "lon", None)),
        out_specs=(P("lat", "lon", None), P("lat", "lon", None), P("lat", "lon")),
        check_vma=False,
    )
```

```python
import jax
import jax.numpy as jnp
import numpy as np
from jax import lax
from jax.experimental import pallas as pl
from jax.experimental.pallas import tpu as pltpu
from jax.sharding import PartitionSpec as P

D = 512
HEADS = 8
HEAD = D // HEADS
WIN_LAT = 6
WIN_LON = 12
SHIFT_LAT = 3
SHIFT_LON = 6
EPS = 1e-05

ROWS, COLS = 12, 48
BORDER = 8
TOKENS = ROWS * COLS
LEN = WIN_LAT * WIN_LON
PAD = 80
PER_BAND = COLS // WIN_LON
BAND = PER_BAND * PAD
WINDOWS = 2 * PER_BAND
TOP = SHIFT_LAT * COLS
EDGE = ROWS * BORDER
CORNER = SHIFT_LAT * BORDER
SIDE = WIN_LAT * BORDER
TURN = 4 * BORDER
BAND_CELLS = WIN_LAT * COLS
GROUP = HEADS // 2
GROUP_WIDTH = GROUP * HEAD
LOCAL = PER_BAND - 1
INNER = LOCAL * PAD
REST = WINDOWS - LOCAL
OUTER = REST * PAD
PAIR_ROWS, PAIR_COLS = ROWS // 2, COLS // 2
PAIRS = PAIR_ROWS * PAIR_COLS
PAIR_TOP = PAIR_COLS
PAIR_SIDE = PAIR_ROWS * BORDER
PAIR_CORNER = BORDER
HELD = 10
WIDTH = WINDOWS * PAD
NEG = -1e30

f32 = jnp.float32
bf16 = jnp.bfloat16


def band_selector():
    pick = np.zeros((BAND, BAND_CELLS), np.float32)
    for win in range(PER_BAND):
        for i in range(WIN_LAT):
            for j in range(WIN_LON):
                pick[win * PAD + i * WIN_LON + j, i * COLS + win * WIN_LON + j] = 1.0
    return pick


def shift_selector(rows, cols, shift):
    pick = np.zeros((rows * cols, rows * (cols + BORDER)), np.float32)
    for i in range(rows):
        for j in range(cols):
            col = j + shift
            pick[i * cols + j, i * cols + col if col < cols else rows * cols + i * BORDER + col - cols] = 1.0
    return pick


def pair_selector():
    pick = np.zeros((4 * COLS, 4 * COLS), np.float32)
    quarter = COLS
    for a in range(2):
        for b in range(COLS // 2):
            for k, (i, j) in enumerate(((0, 0), (1, 0), (0, 1), (1, 1))):
                pick[k * quarter + a * (COLS // 2) + b, (2 * a + i) * COLS + 2 * b + j] = 1.0
    return pick


def dot(a, b):
    return lax.dot_general(a, b, (((1,), (0,)), ((), ())), preferred_element_type=f32)


def dot_nt(a, b):
    return lax.dot_general(a, b, (((1,), (1,)), ((), ())), preferred_element_type=f32)


def dot_tn(a, b):
    return lax.dot_general(a, b, (((0,), (0,)), ((), ())), preferred_element_type=f32)


def norm_parts(values):
    centred = values - jnp.mean(values, axis=-1, keepdims=True)
    scale = lax.rsqrt(jnp.mean(centred * centred, axis=-1, keepdims=True) + EPS)
    return centred * scale, scale


def band_sources(cells, lat, lon, diag):
    first = jnp.concatenate([cells[:BAND_CELLS], lon[CORNER : CORNER + SIDE].astype(bf16)], axis=0)
    beside = jnp.concatenate([lon[CORNER + SIDE : EDGE], diag[:CORNER]], axis=0).astype(bf16)
    second = jnp.concatenate([cells[BAND_CELLS:], lat, beside], axis=0)
    return first, second


def halves(block):
    return jnp.concatenate([block[:, :D], block[:, D:]], axis=0)


def head_masks():
    lane = lax.broadcasted_iota(jnp.int32, (1, GROUP_WIDTH), 1) // HEAD
    return [(lane == h).astype(f32).astype(bf16) for h in range(GROUP)]


def spread_heads(block, masks):
    return jnp.concatenate([block * m for m in masks], axis=0)


def per_head(stacked, block):
    first = lax.broadcasted_iota(jnp.int32, (1, 2 * HEAD), 1) < HEAD
    all_heads = dot_tn(stacked, block)
    out = []
    for pair in range(GROUP // 2):
        part = all_heads[:, pair * 2 * HEAD : (pair + 1) * 2 * HEAD]
        at = pair * 2 * PAD
        out.append(jnp.where(first, part[at : at + PAD], part[at + PAD : at + 2 * PAD]))
    return jnp.concatenate(out, axis=1)


def last_band():
    at_end = lax.axis_index("lat") == lax.axis_size("lat") - 1
    return jnp.where(at_end, f32(1), f32(0))


def halves_apart():
    shape = (LEN, GROUP * PAD)
    key = lax.broadcasted_iota(jnp.int32, shape, 0)
    query = lax.rem(lax.broadcasted_iota(jnp.int32, shape, 1), PAD)
    return jnp.where((key < LEN // 2) != (query < LEN // 2), f32(NEG), f32(0)) * last_band()


def attend(windows, qkv_ref, mixed_ref, probs_ref):
    masks = [m * HEAD ** (-0.5) for m in head_masks()]
    apart = halves_apart() if any(windows) else None
    for win, wraps in enumerate(windows):
        rows = pl.ds(win * PAD, PAD)
        for g in range(2):
            at = g * GROUP_WIDTH
            queries = spread_heads(qkv_ref[rows, at : at + GROUP_WIDTH], masks)
            keys = qkv_ref[rows, D + at : D + at + GROUP_WIDTH]
            values = qkv_ref[rows, 2 * D + at : 2 * D + at + GROUP_WIDTH]
            scores = dot_nt(keys, queries)[:LEN]
            if wraps:
                scores = scores + apart
            weights = jnp.exp(scores - jnp.max(scores, axis=0, keepdims=True))
            probs = weights * (1.0 / jnp.sum(weights, axis=0, keepdims=True))
            probs = jnp.concatenate([probs, jnp.zeros((PAD - LEN, GROUP * PAD), f32)], axis=0)
            probs_ref[win, g] = probs
            mixed_ref[rows, at : at + GROUP_WIDTH] = per_head(probs.astype(bf16), values).astype(bf16)


def attend_back(windows, dmix_ref, dqkv_ref, offset):
    masks = head_masks()
    scaled = [m * HEAD ** (-0.5) for m in masks]
    for win, (qkv_ref, probs_ref, place) in enumerate(windows):
        rows = pl.ds(place * PAD, PAD)
        out = pl.ds(offset + win * PAD, PAD)
        for g in range(2):
            at = g * GROUP_WIDTH
            queries = spread_heads(qkv_ref[rows, at : at + GROUP_WIDTH], scaled)
            keys = qkv_ref[rows, D + at : D + at + GROUP_WIDTH]
            values = qkv_ref[rows, 2 * D + at : 2 * D + at + GROUP_WIDTH]
            above = spread_heads(dmix_ref[pl.ds(win * PAD, PAD), at : at + GROUP_WIDTH], masks)
            probs = probs_ref[place, g]
            d_probs = dot_nt(values, above)
            along = jnp.sum(probs * d_probs, axis=0, keepdims=True)
            d_scores = (probs * (d_probs - along)).astype(bf16)
            d_queries = per_head(d_scores, keys) * HEAD ** (-0.5)
            d_keys = dot(d_scores, queries)
            d_values = dot(probs.astype(bf16), above)
            dqkv_ref[out, at : at + GROUP_WIDTH] = d_queries.astype(bf16)
            dqkv_ref[out, D + at : D + at + GROUP_WIDTH] = d_keys.astype(bf16)
            dqkv_ref[out, 2 * D + at : 2 * D + at + GROUP_WIDTH] = d_values.astype(bf16)


def border_kernel(tok_ref, own_ref, top_ref, edge_ref, sem):
    copy = pltpu.make_async_copy(tok_ref, own_ref, sem)
    copy.start()
    copy.wait()
    edge = [own_ref[row * COLS : row * COLS + 16].astype(f32)[:BORDER] for row in range(ROWS)]
    top_ref[...] = own_ref[:TOP]
    edge_ref[...] = jnp.concatenate(edge, axis=0).astype(bf16)


def border_pairs_kernel(g_ref, cells_ref, own_g_ref, g_top_ref, edge_ref, corner_ref, sem):
    copy = pltpu.make_async_copy(g_ref, own_g_ref, sem)
    copy.start()
    edge_ref[:EDGE] = cells_ref[...]
    corner_ref[:TURN] = cells_ref[:TURN]
    copy.wait()
    cots = own_g_ref[...].astype(f32)
    side = [cots[row * PAIR_COLS : row * PAIR_COLS + BORDER] for row in range(PAIR_ROWS)]
    g_top_ref[...] = halves(cots[:PAIR_TOP]).astype(bf16)
    edge_ref[EDGE:] = halves(jnp.concatenate(side, axis=0).astype(bf16))
    corner_ref[TURN:] = halves(side[0]).astype(bf16)


def inner_kernel(tok_ref, *refs):
    held, got = refs[:HELD], refs[HELD : 2 * HELD]
    cells_ref, xs_ref, qkv_ref, mixed_ref, probs_ref, att_ref, sem = refs[2 * HELD :]
    copies = [pltpu.make_async_copy(a, b, sem.at[i]) for i, (a, b) in enumerate(zip(held, got))]
    for copy in copies:
        copy.start()
    gain_ref, pick_ref, wqkv_ref, wproj_ref = got[:4]
    normed = norm_parts(tok_ref[TOP:].astype(f32))[0]
    for copy in copies:
        copy.wait()
    cells_ref[...] = (normed * gain_ref[...]).astype(bf16)
    xs_ref[...] = dot(pick_ref[:INNER, :BAND_CELLS], cells_ref[:BAND_CELLS]).astype(bf16)
    qkv_ref[...] = dot(xs_ref[...], wqkv_ref[...]).astype(bf16)
    attend([False] * LOCAL, qkv_ref, mixed_ref, probs_ref)
    att_ref[...] = dot(mixed_ref[...], wproj_ref[...]).astype(bf16)


def outer_kernel(
    tok_ref, cells_ref, lat_ref, lon_ref, diag_ref, gain_ref, wqkv_ref, wproj_ref, pick_ref, shift_ref, cells_pick_ref,
    att0_ref,
    xs_ref, qkv_ref, mixed_ref, probs_ref, tok_out_ref, summed_ref, row_ref,
    att_ref,
):
    def normed(values):
        return norm_parts(values)[0] * gain_ref[...]

    lat, lon, diag = lat_ref[...], lon_ref[:EDGE].astype(f32), diag_ref[:TURN].astype(f32)
    first, second = band_sources(cells_ref[...], normed(lat.astype(f32)).astype(bf16), normed(lon), normed(diag))
    xs_ref[:PAD] = dot(pick_ref[INNER:], first).astype(bf16)
    xs_ref[PAD:] = dot(pick_ref[...], second).astype(bf16)
    qkv_ref[...] = dot(xs_ref[...], wqkv_ref[...]).astype(bf16)
    attend([False] + [True] * PER_BAND, qkv_ref, mixed_ref, probs_ref)
    att_ref[:INNER] = att0_ref[...]
    att_ref[INNER:] = dot(mixed_ref[...], wproj_ref[...]).astype(bf16)
    for band, source in enumerate(band_sources(tok_ref[TOP:], lat, lon, diag)):
        rows = pl.ds(band * BAND_CELLS, BAND_CELLS)
        tokens = dot(shift_ref[...], source)
        added = dot(cells_pick_ref[...], att_ref[pl.ds(band * BAND, BAND)])
        tok_out_ref[rows] = tokens.astype(bf16)
        summed_ref[rows] = (tokens + added).astype(bf16)
    row_ref[...] = summed_ref[TOKENS - COLS :]


def cotangent_kernel(
    g_ref, lat_ref, lon_ref, diag_ref, gain_ref, shift_ref, wmerge_ref, out_ref, weights_ref, sem
):
    copy = pltpu.make_async_copy(wmerge_ref, weights_ref, sem)
    copy.start()
    parts = []
    for half in range(2):
        lat = lat_ref[...].astype(f32)[half * PAIR_TOP : (half + 1) * PAIR_TOP]
        at = EDGE + half * PAIR_SIDE
        lon = lon_ref[at : at + PAIR_SIDE].astype(f32)[PAIR_CORNER:]
        diag = diag_ref[TURN:].astype(f32)[half * PAIR_CORNER : (half + 1) * PAIR_CORNER]
        own = g_ref[:, half * D : (half + 1) * D].astype(f32)[PAIR_TOP:]
        source = jnp.concatenate([own, lat, lon, diag], axis=0).astype(bf16)
        parts.append(dot(shift_ref[...], source).astype(bf16))
    cots = jnp.concatenate(parts, axis=1)
    copy.wait()
    for k in range(4):
        out_ref[k] = dot_nt(cots, weights_ref[k * D : (k + 1) * D]) * gain_ref[k]


def pair_kernel(
    summed_ref, row_ref, gain_ref, cot_ref, pair_ref, unpair_ref,
    dsum_ref, out_row_ref, normed_ref,
    members_ref,
):
    quarter = COLS
    for part in range(3):
        first = part * 4 * COLS - COLS
        if part:
            summed = summed_ref[first : first + 4 * COLS]
        else:
            summed = jnp.concatenate([row_ref[...], summed_ref[: 3 * COLS]], axis=0)
        paired = dot(pair_ref[...], summed)
        for k in range(4):
            members_ref[k, pl.ds(part * quarter, quarter)] = paired[k * quarter : (k + 1) * quarter]
    width = 4 * D
    total = sum(jnp.sum(members_ref[k], axis=-1, keepdims=True) for k in range(4))
    center = total / width
    for k in range(4):
        members_ref[k] = members_ref[k] - center
    spread = sum(jnp.sum(members_ref[k] * members_ref[k], axis=-1, keepdims=True) for k in range(4)) / width
    scale = lax.rsqrt(spread + EPS)
    for k in range(4):
        members_ref[k] = members_ref[k] * scale
        normed_ref[k] = (members_ref[k] * gain_ref[k]).astype(bf16)
    flat = sum(jnp.sum(cot_ref[k], axis=-1, keepdims=True) for k in range(4)) / width
    along = sum(jnp.sum(cot_ref[k] * members_ref[k], axis=-1, keepdims=True) for k in range(4)) / width
    for k in range(4):
        members_ref[k] = (cot_ref[k] - flat - members_ref[k] * along) * scale
    for part in range(3):
        rows = pl.ds(part * quarter, quarter)
        block = jnp.concatenate([members_ref[k, rows].astype(bf16) for k in range(4)], axis=0)
        dsum_ref[pl.ds(part * 4 * COLS, 4 * COLS)] = dot(unpair_ref[...], block).astype(bf16)
    out_row_ref[...] = dsum_ref[:COLS]


def merge_kernel(normed_ref, wmerge_ref, unshift_ref, main_ref, lat_ref, lon_ref, diag_ref):
    total = dot(normed_ref[0], wmerge_ref[:D])
    for k in range(1, 4):
        total = total + dot(normed_ref[k], wmerge_ref[k * D : (k + 1) * D])
    pairs = dot(unshift_ref[...], total.astype(bf16))
    main_ref[...] = pairs[:PAIRS].astype(bf16)
    lat_ref[...] = halves(pairs[PAIRS - PAIR_TOP : PAIRS]).astype(bf16)
    lon_ref[...] = halves(pairs[PAIRS : PAIRS + PAIR_SIDE - PAIR_CORNER]).astype(bf16)
    diag_ref[...] = halves(pairs[PAIRS + PAIR_SIDE - PAIR_CORNER :]).astype(bf16)


def inner_back_kernel(
    dsum_ref, qkv0_ref, probs0_ref, qkv_ref, probs_ref, wproj_ref, pick_ref, xs0_ref, xs_ref, mixed0_ref, mixed_ref,
    up_ref, dqkv_ref, xst_ref, mixt_ref,
    dmix_ref,
):
    xst_ref[...] = jnp.concatenate([xs0_ref[...], xs_ref[...]], axis=0).T
    mixt_ref[...] = jnp.concatenate([mixed0_ref[...], mixed_ref[...]], axis=0).T
    up_ref[...] = dot(pick_ref[...], dsum_ref[COLS : COLS + BAND_CELLS]).astype(bf16)
    dmix_ref[...] = dot_nt(up_ref[...], wproj_ref[...]).astype(bf16)
    windows = [(qkv0_ref, probs0_ref, win) for win in range(LOCAL)] + [(qkv_ref, probs_ref, 0)]
    attend_back(windows, dmix_ref, dqkv_ref, 0)


def outer_back_kernel(
    dsum_ref, row_ref, xst_ref, mixt_ref, up0_ref, dqkv0_ref, qkv_ref, probs_ref, wproj_ref, pick_ref,
    dqkv_ref, keep_ref, send_ref,
    up_ref, dmix_ref,
):
    cells = jnp.concatenate([dsum_ref[COLS + BAND_CELLS :], row_ref[...]], axis=0)
    up_ref[:BAND] = up0_ref[...]
    up_ref[BAND:] = dot(pick_ref[...], cells).astype(bf16)
    dqkv_ref[:BAND] = dqkv0_ref[...]
    dmix_ref[...] = dot_nt(up_ref[BAND:], wproj_ref[...]).astype(bf16)
    attend_back([(qkv_ref, probs_ref, win) for win in range(1, REST)], dmix_ref, dqkv_ref, BAND)
    lat_at, lon_at = lax.axis_index("lat"), lax.axis_index("lon")
    even_core = lax.rem(lon_at, 2) == 0
    my_x = lax.rem(lax.div(lon_at, 2), 4)
    my_y = lax.div(lat_at, 8) * 2 + lax.div(lon_at, 8)
    x_steps = [lax.bitwise_xor(my_x, jnp.int32(i)) for i in range(4)]
    y_steps = [lax.bitwise_xor(my_y, jnp.int32(i)) for i in range(4)]
    for col in range(8):
        if col < 6:
            grad = dot(xst_ref[...], dqkv_ref[:, col * 256 : (col + 1) * 256])
        else:
            grad = dot(mixt_ref[...], up_ref[:, (col - 6) * 256 : (col - 5) * 256])
        even, odd = grad[:, :128], grad[:, 128:]
        kept = jnp.where(even_core, even, odd).astype(bf16)
        sent = jnp.where(even_core, odd, even).astype(bf16)
        low, x = divmod(col, 4)
        for lat in range(16):
            high, z = divmod(lat, 8)
            y = high * 2 + low
            rows = slice(lat * 32, (lat + 1) * 32)
            on_even = x_steps[x], lat * 2 + low
            on_odd = y_steps[y], z * 4 + x
            mine = [jnp.where(even_core, a, b) for a, b in zip(on_even, on_odd)]
            other = [jnp.where(even_core, b, a) for a, b in zip(on_even, on_odd)]
            keep_ref[mine[0], mine[1]] = kept[rows]
            send_ref[other[0], other[1]] = sent[rows]


def cells_back_kernel(
    dqkv_ref, wqkv_ref, cells_pick_ref, unshift_ref, tok_ref, dsum_ref, row_ref, gain_ref, m_lon_ref, m_diag_ref,
    main_ref, lat_ref, lon_ref, diag_ref,
    dx_ref,
):
    dx_ref[...] = dot_nt(dqkv_ref[...], wqkv_ref[...]).astype(bf16)
    for band in range(2):
        if band == 0:
            above = dsum_ref[COLS : COLS + BAND_CELLS]
        else:
            above = jnp.concatenate([dsum_ref[COLS + BAND_CELLS :], row_ref[...]], axis=0)
        cot = dot(cells_pick_ref[...], dx_ref[pl.ds(band * BAND, BAND)]) * gain_ref[...]
        normed, scale = norm_parts(tok_ref[pl.ds(band * BAND_CELLS, BAND_CELLS)].astype(f32))
        flat = jnp.mean(cot, axis=-1, keepdims=True)
        along = jnp.mean(cot * normed, axis=-1, keepdims=True)
        grads = (above.astype(f32) + (cot - flat - normed * along) * scale).astype(bf16)
        cells = dot(unshift_ref[...], grads).astype(bf16)
        if band == 0:
            main_ref[:BAND_CELLS] = cells[:BAND_CELLS]
        else:
            main_ref[BAND_CELLS:] = cells[: BAND_CELLS - TOP]
            lat_ref[...] = cells[BAND_CELLS - TOP : BAND_CELLS]
            diag_ref[:TURN] = cells[BAND_CELLS + SIDE - TURN :]
        lon_ref[band * SIDE : (band + 1) * SIDE] = cells[BAND_CELLS:]
    lon_ref[EDGE:] = m_lon_ref[...]
    diag_ref[TURN:] = m_diag_ref[...]


def fill_edge(field, side, rows, cols):
    width = field.shape[-1]
    field, side = field.astype(f32).reshape(rows, cols, width), side.astype(f32).reshape(rows, BORDER, width)
    first = field[:, :BORDER] + side
    return jnp.concatenate([first, field[:, BORDER:]], axis=1).reshape(rows * cols, width)


def own_cells_kernel(main_ref, lat_ref, lon_ref, diag_ref, m_main_ref, m_lat_ref, tokens_ref, merged_ref):
    corner = diag_ref[:TURN].astype(f32)[TURN - CORNER :]
    beside = lon_ref[:EDGE].astype(f32)[: EDGE - CORNER]
    tokens_ref[:TOP] = fill_edge(lat_ref[...], corner, SHIFT_LAT, COLS).astype(bf16)
    tokens_ref[TOP:] = fill_edge(main_ref[...], beside, ROWS - SHIFT_LAT, COLS).astype(bf16)
    side_rows = PAIR_SIDE - PAIR_CORNER
    for half in range(2):
        cols = pl.ds(half * D, D)
        lat = m_lat_ref[...].astype(f32)[half * PAIR_TOP : (half + 1) * PAIR_TOP]
        lon = lon_ref[EDGE:].astype(f32)[half * side_rows : (half + 1) * side_rows]
        diag = diag_ref[TURN:].astype(f32)[half * PAIR_CORNER : (half + 1) * PAIR_CORNER]
        own = m_main_ref[:, cols].astype(f32)[: PAIRS - PAIR_TOP]
        field, side = jnp.concatenate([lat, own], axis=0), jnp.concatenate([diag, lon], axis=0)
        merged_ref[:, cols] = fill_edge(field, side, PAIR_ROWS, PAIR_COLS).astype(bf16)


def add_kernel(a_ref, b_ref, *out_refs):
    for k, out_ref in enumerate(out_refs):
        out_ref[...] = (a_ref[k].astype(f32) + b_ref[k].astype(f32)).astype(bf16)


def join_kernel(a_ref, b_ref, c_ref, d_ref, out_ref):
    total = a_ref[...].astype(f32) + b_ref[...].astype(f32) + c_ref[...].astype(f32) + d_ref[...].astype(f32)
    out_ref[...] = total.astype(bf16)


def sum_kernel(parts_ref, out_ref):
    total = parts_ref[0].astype(f32)
    for i in range(1, parts_ref.shape[0]):
        total = total + parts_ref[i].astype(f32)
    out_ref[...] = total.astype(out_ref.dtype)


def call(kernel, outs, scratch=(), places=None, limit=20):
    spaces = {} if places is None else {
        "in_specs": [pl.BlockSpec(memory_space=(pltpu.VMEM, pl.ANY, pltpu.HBM)[p]) for p in places]
    }
    return pl.pallas_call(
        kernel,
        out_shape=[jax.ShapeDtypeStruct(s, t) for s, t in outs],
        scratch_shapes=[pltpu.VMEM(*s) if isinstance(s, tuple) else s for s in scratch],
        cost_estimate=pl.CostEstimate(flops=10**9, bytes_accessed=2 * 10**6, transcendentals=0),
        compiler_params=pltpu.CompilerParams(vmem_limit_bytes=limit * 1024 * 1024),
        **spaces,
    )


def saved(count):
    rows = count * PAD
    return [((rows, D), bf16), ((rows, 3 * D), bf16), ((rows, D), bf16), ((count, 2, PAD, GROUP * PAD), f32)]


def after(value, *others):
    return lax.optimization_barrier((value, *others))[0]


def chain(tok, gain, w_qkv, w_proj, gain_merge, w_merge, g_merged, fetch, up, down):
    tok, top, edge = call(
        border_kernel,
        [((TOKENS, D), bf16), ((TOP, D), bf16), ((EDGE, D), bf16)],
        [pltpu.SemaphoreType.DMA],
        [2],
    )(tok)
    g_merged, g_top, edge, corner = call(
        border_pairs_kernel,
        [
            ((PAIRS, 2 * D), bf16), ((2 * PAIR_TOP, D), bf16),
            ((EDGE + 2 * PAIR_SIDE, D), bf16), ((TURN + 2 * PAIR_CORNER, D), bf16),
        ],
        [pltpu.SemaphoreType.DMA],
        [2, 0],
    )(g_merged, edge)
    beside = fetch(top, edge, corner)
    g_lat = up(g_top)
    pair, band = pair_selector(), band_selector()
    shift = shift_selector(WIN_LAT, COLS, SHIFT_LON)
    pair_shift = shift_selector(PAIR_ROWS, PAIR_COLS, SHIFT_LON // 2)
    held = [gain, jnp.asarray(band @ shift, bf16), w_qkv, w_proj, gain_merge]
    held += [jnp.asarray(c, bf16) for c in (shift, band.T, pair, pair.T, pair_shift)]
    got = call(
        inner_kernel,
        [(h.shape, h.dtype) for h in held] + [((TOKENS - TOP, D), bf16)] + saved(LOCAL) + [((INNER, D), bf16)],
        [pltpu.SemaphoreType.DMA((HELD,))],
        [0] + [1] * HELD,
    )(tok, *held)
    gain, pick, w_qkv, w_proj, gain_merge, shift, cells_pick, pair, unpair, pair_shift = got[:HELD]
    cells, xs0, qkv0, mixed0, probs0, att0 = got[HELD:]
    xs1, qkv1, mixed1, probs1, tok, summed, row = call(
        outer_kernel,
        saved(REST) + [((TOKENS, D), bf16), ((TOKENS, D), bf16), ((COLS, D), bf16)],
        [((WIDTH, D), bf16)],
    )(tok, cells, *beside, gain, w_qkv, w_proj, pick, shift, cells_pick, att0)
    behind = down(row)
    cots, w_merge = call(
        cotangent_kernel,
        [((4, PAIRS, D), f32), ((4 * D, 2 * D), bf16)],
        [pltpu.SemaphoreType.DMA],
        [0] * 6 + [1],
    )(after(g_merged, row), g_lat, *beside[1:], gain_merge, pair_shift, w_merge)
    d_summed, row, merge_normed = call(
        pair_kernel,
        [((TOKENS, D), bf16), ((COLS, D), bf16), ((4, PAIRS, D), bf16)],
        [((4, PAIRS, D), f32)],
    )(summed, behind, gain_merge, cots, pair, unpair)
    last = up(row)
    band = jnp.asarray(band_selector(), bf16)
    unshift = jnp.asarray(shift_selector(WIN_LAT, COLS, SHIFT_LON).T, bf16)
    pair_unshift = jnp.asarray(shift_selector(PAIR_ROWS, PAIR_COLS, SHIFT_LON // 2).T, bf16)
    up0, dqkv0, xst, mixt = call(
        inner_back_kernel,
        [((BAND, D), bf16), ((BAND, 3 * D), bf16), ((D, WIDTH), bf16), ((D, WIDTH), bf16)],
        [((BAND, D), bf16)],
    )(d_summed, qkv0, probs0, qkv1, probs1, w_proj, band, xs0, xs1, mixed0, mixed1)
    m_main, m_lat, m_lon, m_diag = call(
        merge_kernel,
        [
            ((PAIRS, 2 * D), bf16), ((2 * PAIR_TOP, D), bf16),
            ((2 * (PAIR_SIDE - PAIR_CORNER), D), bf16), ((2 * PAIR_CORNER, D), bf16),
        ],
    )(merge_normed, w_merge, pair_unshift)
    m_lat = down(m_lat)
    dqkv, keep, sent = call(
        outer_back_kernel,
        [((WIDTH, 3 * D), bf16), ((4, 32, 32, 128), bf16), ((4, 32, 32, 128), bf16)],
        [((WIDTH, D), bf16), ((BAND, D), bf16)],
    )(d_summed, last, xst, mixt, after(up0, m_main), dqkv0, qkv1, probs1, w_proj, band)
    main, to_lat, to_lon, to_diag = call(
        cells_back_kernel,
        [
            ((TOKENS - TOP, D), bf16), ((TOP, D), bf16),
            ((EDGE + 2 * (PAIR_SIDE - PAIR_CORNER), D), bf16), ((TURN + 2 * PAIR_CORNER, D), bf16),
        ],
        [((WIDTH, D), bf16)],
    )(dqkv, w_qkv, cells_pick, unshift, tok, d_summed, last, gain, m_lon, m_diag)

    def finish(lat, lon, diag):
        grad_tokens, merged = call(own_cells_kernel, [((TOKENS, D), bf16), ((PAIRS, 2 * D), bf16)])(
            main, lat, lon, diag, m_main, m_lat
        )
        return merged, grad_tokens

    return finish, keep, sent, (to_lat, to_lon, to_diag), m_lat


def solution(mesh):
    lats, lons = mesh.shape["lat"], mesh.shape["lon"]
    count = lats * lons

    def send(block, down, right):
        route = [
            (i, (i // lons + down) % lats * lons + (i % lons + right) % lons) for i in range(count)
        ]
        return lax.ppermute(block, ("lat", "lon"), route)

    def fetch(top, edge, corner):
        return send(top, -1, 0), send(edge, 0, -1), send(corner, -1, -1)

    def place(i):
        lat, lon = divmod(i, lons)
        return lat // 8, lat % 8, lon // 8, lon // 2 % 4, lon % 2

    def across(i, step):
        high, z, low, x, core = place(i)
        if core:
            high, low = divmod((high * 2 + low) ^ step, 2)
        else:
            x = x ^ step
        return (high * 8 + z) * lons + low * 8 + x * 2 + core

    rest = {}
    for i in range(count):
        high, z, low, x, core = place(i)
        rest.setdefault((core, high * 2 + low if core else x), []).append(i)
    rest = list(rest.values())

    def swap(block, step):
        return lax.ppermute(block, ("lat", "lon"), [(i, across(i, step)) for i in range(count)])

    def reduce_across(keep, sent, to_lat):
        other = lax.ppermute(sent, ("lat", "lon"), [(i, i ^ 1) for i in range(count)])
        own, *others = call(add_kernel, [((32, 32, 128), bf16)] * 4)(keep, after(other, to_lat))
        got = [swap(block, step) for step, block in enumerate(others, 1)]
        return call(join_kernel, [((32, 32, 128), bf16)])(own, *got)[0]

    def reduce_rest(sums):
        parts = lax.all_to_all(sums, ("lat", "lon"), 0, 0, axis_index_groups=rest, tiled=True)
        return call(sum_kernel, [((32, 128), f32)])(parts)[0]

    def body(tokens, gain_attn, w_qkv, w_proj, gain_merge, w_merge, g_merged):
        finish, keep, sent, pieces, m_lat = chain(
            tokens.reshape(TOKENS, D), gain_attn.reshape(1, D), w_qkv, w_proj, gain_merge.reshape(4, 1, D),
            w_merge, g_merged.reshape(PAIRS, 2 * D), fetch,
            lambda row: send(row, -1, 0), lambda row: send(row, 1, 0),
        )
        sums = after(reduce_across(keep, sent, pieces[0]), m_lat)
        grad_weights = reduce_rest(sums)
        to_lat, to_lon, to_diag = pieces
        beside = send(to_lat, 1, 0), send(to_lon, 0, 1), send(to_diag, 1, 1)
        merged, grad_tokens = finish(*(after(piece, sums) for piece in beside))
        return (
            merged.reshape(ROWS // 2, COLS // 2, 2 * D),
            grad_tokens.reshape(ROWS, COLS, D),
            grad_weights,
        )

    return jax.shard_map(
        body,
        mesh=mesh,
        in_specs=(P("lat", "lon", None), P(), P(), P(), P(), P(), P("lat", "lon", None)),
        out_specs=(P("lat", "lon", None), P("lat", "lon", None), P("lat", "lon")),
        check_vma=False,
    )
```

```python
import jax
import jax.numpy as jnp
import numpy as np
from jax import lax
from jax.experimental import pallas as pl
from jax.experimental.pallas import tpu as pltpu
from jax.sharding import PartitionSpec as P

D = 512
HEADS = 8
HEAD = D // HEADS
WIN_LAT = 6
WIN_LON = 12
SHIFT_LAT = 3
SHIFT_LON = 6
EPS = 1e-05

ROWS, COLS = 12, 48
BORDER = 8
TOKENS = ROWS * COLS
LEN = WIN_LAT * WIN_LON
PAD = 80
PER_BAND = COLS // WIN_LON
BAND = PER_BAND * PAD
WINDOWS = 2 * PER_BAND
TOP = SHIFT_LAT * COLS
EDGE = ROWS * BORDER
CORNER = SHIFT_LAT * BORDER
SIDE = WIN_LAT * BORDER
TURN = 4 * BORDER
BAND_CELLS = WIN_LAT * COLS
GROUP = HEADS // 2
GROUP_WIDTH = GROUP * HEAD
LOCAL = PER_BAND - 1
INNER = LOCAL * PAD
REST = WINDOWS - LOCAL
OUTER = REST * PAD
PAIR_ROWS, PAIR_COLS = ROWS // 2, COLS // 2
PAIRS = PAIR_ROWS * PAIR_COLS
PAIR_TOP = PAIR_COLS
PAIR_SIDE = PAIR_ROWS * BORDER
PAIR_CORNER = BORDER
HELD = 10
WIDTH = WINDOWS * PAD
NEG = -1e30

f32 = jnp.float32
bf16 = jnp.bfloat16


def band_selector():
    pick = np.zeros((BAND, BAND_CELLS), np.float32)
    for win in range(PER_BAND):
        for i in range(WIN_LAT):
            for j in range(WIN_LON):
                pick[win * PAD + i * WIN_LON + j, i * COLS + win * WIN_LON + j] = 1.0
    return pick


def shift_selector(rows, cols, shift):
    pick = np.zeros((rows * cols, rows * (cols + BORDER)), np.float32)
    for i in range(rows):
        for j in range(cols):
            col = j + shift
            pick[i * cols + j, i * cols + col if col < cols else rows * cols + i * BORDER + col - cols] = 1.0
    return pick


def pair_selector():
    pick = np.zeros((4 * COLS, 4 * COLS), np.float32)
    quarter = COLS
    for a in range(2):
        for b in range(COLS // 2):
            for k, (i, j) in enumerate(((0, 0), (1, 0), (0, 1), (1, 1))):
                pick[k * quarter + a * (COLS // 2) + b, (2 * a + i) * COLS + 2 * b + j] = 1.0
    return pick


def dot(a, b):
    return lax.dot_general(a, b, (((1,), (0,)), ((), ())), preferred_element_type=f32)


def dot_nt(a, b):
    return lax.dot_general(a, b, (((1,), (1,)), ((), ())), preferred_element_type=f32)


def dot_tn(a, b):
    return lax.dot_general(a, b, (((0,), (0,)), ((), ())), preferred_element_type=f32)


def norm_parts(values):
    centred = values - jnp.mean(values, axis=-1, keepdims=True)
    scale = lax.rsqrt(jnp.mean(centred * centred, axis=-1, keepdims=True) + EPS)
    return centred * scale, scale


def band_sources(cells, lat, lon, diag):
    first = jnp.concatenate([cells[:BAND_CELLS], lon[CORNER : CORNER + SIDE].astype(bf16)], axis=0)
    beside = jnp.concatenate([lon[CORNER + SIDE : EDGE], diag[:CORNER]], axis=0).astype(bf16)
    second = jnp.concatenate([cells[BAND_CELLS:], lat, beside], axis=0)
    return first, second


def halves(block):
    return jnp.concatenate([block[:, :D], block[:, D:]], axis=0)


def head_masks():
    lane = lax.broadcasted_iota(jnp.int32, (1, GROUP_WIDTH), 1) // HEAD
    return [(lane == h).astype(f32).astype(bf16) for h in range(GROUP)]


def spread_heads(block, masks):
    return jnp.concatenate([block * m for m in masks], axis=0)


def per_head(stacked, block):
    first = lax.broadcasted_iota(jnp.int32, (1, 2 * HEAD), 1) < HEAD
    all_heads = dot_tn(stacked, block)
    out = []
    for pair in range(GROUP // 2):
        part = all_heads[:, pair * 2 * HEAD : (pair + 1) * 2 * HEAD]
        at = pair * 2 * PAD
        out.append(jnp.where(first, part[at : at + PAD], part[at + PAD : at + 2 * PAD]))
    return jnp.concatenate(out, axis=1)


def last_band():
    at_end = lax.axis_index("lat") == lax.axis_size("lat") - 1
    return jnp.where(at_end, f32(1), f32(0))


def halves_apart():
    shape = (LEN, GROUP * PAD)
    key = lax.broadcasted_iota(jnp.int32, shape, 0)
    query = lax.rem(lax.broadcasted_iota(jnp.int32, shape, 1), PAD)
    return jnp.where((key < LEN // 2) != (query < LEN // 2), f32(NEG), f32(0)) * last_band()


def attend(windows, qkv_ref, mixed_ref, probs_ref):
    masks = [m * HEAD ** (-0.5) for m in head_masks()]
    apart = halves_apart() if any(windows) else None
    for win, wraps in enumerate(windows):
        rows = pl.ds(win * PAD, PAD)
        for g in range(2):
            at = g * GROUP_WIDTH
            queries = spread_heads(qkv_ref[rows, at : at + GROUP_WIDTH], masks)
            keys = qkv_ref[rows, D + at : D + at + GROUP_WIDTH]
            values = qkv_ref[rows, 2 * D + at : 2 * D + at + GROUP_WIDTH]
            scores = dot_nt(keys, queries)[:LEN]
            if wraps:
                scores = scores + apart
            weights = jnp.exp(scores - jnp.max(scores, axis=0, keepdims=True))
            probs = weights * (1.0 / jnp.sum(weights, axis=0, keepdims=True))
            probs = jnp.concatenate([probs, jnp.zeros((PAD - LEN, GROUP * PAD), f32)], axis=0)
            probs_ref[win, g] = probs
            mixed_ref[rows, at : at + GROUP_WIDTH] = per_head(probs.astype(bf16), values).astype(bf16)


def attend_back(windows, dmix_ref, dqkv_ref, offset):
    masks = head_masks()
    scaled = [m * HEAD ** (-0.5) for m in masks]
    for win, (qkv_ref, probs_ref, place) in enumerate(windows):
        rows = pl.ds(place * PAD, PAD)
        out = pl.ds(offset + win * PAD, PAD)
        for g in range(2):
            at = g * GROUP_WIDTH
            queries = spread_heads(qkv_ref[rows, at : at + GROUP_WIDTH], scaled)
            keys = qkv_ref[rows, D + at : D + at + GROUP_WIDTH]
            values = qkv_ref[rows, 2 * D + at : 2 * D + at + GROUP_WIDTH]
            above = spread_heads(dmix_ref[pl.ds(win * PAD, PAD), at : at + GROUP_WIDTH], masks)
            probs = probs_ref[place, g]
            d_probs = dot_nt(values, above)
            along = jnp.sum(probs * d_probs, axis=0, keepdims=True)
            d_scores = (probs * (d_probs - along)).astype(bf16)
            d_queries = per_head(d_scores, keys) * HEAD ** (-0.5)
            d_keys = dot(d_scores, queries)
            d_values = dot(probs.astype(bf16), above)
            dqkv_ref[out, at : at + GROUP_WIDTH] = d_queries.astype(bf16)
            dqkv_ref[out, D + at : D + at + GROUP_WIDTH] = d_keys.astype(bf16)
            dqkv_ref[out, 2 * D + at : 2 * D + at + GROUP_WIDTH] = d_values.astype(bf16)


def border_kernel(tok_ref, g_ref, own_ref, own_g_ref, top_ref, g_top_ref, edge_ref, corner_ref, sem):
    copies = [
        pltpu.make_async_copy(tok_ref, own_ref, sem.at[0]),
        pltpu.make_async_copy(g_ref, own_g_ref, sem.at[1]),
    ]
    for copy in copies:
        copy.start()
    for copy in copies:
        copy.wait()
    edge = [own_ref[row * COLS : row * COLS + 16].astype(f32)[:BORDER] for row in range(ROWS)]
    cots = own_g_ref[...].astype(f32)
    side = [cots[row * PAIR_COLS : row * PAIR_COLS + BORDER] for row in range(PAIR_ROWS)]
    top_ref[...] = own_ref[:TOP]
    g_top_ref[...] = halves(cots[:PAIR_TOP]).astype(bf16)
    edge_ref[:EDGE] = jnp.concatenate(edge, axis=0).astype(bf16)
    edge_ref[EDGE:] = halves(jnp.concatenate(side, axis=0).astype(bf16))
    corner_ref[:TURN] = jnp.concatenate(edge[:4], axis=0).astype(bf16)
    corner_ref[TURN:] = halves(side[0]).astype(bf16)


def inner_kernel(tok_ref, *refs):
    held, got = refs[:HELD], refs[HELD : 2 * HELD]
    cells_ref, xs_ref, qkv_ref, mixed_ref, probs_ref, att_ref, sem = refs[2 * HELD :]
    copies = [pltpu.make_async_copy(a, b, sem.at[i]) for i, (a, b) in enumerate(zip(held, got))]
    for copy in copies:
        copy.start()
    gain_ref, pick_ref, wqkv_ref, wproj_ref = got[:4]
    normed = norm_parts(tok_ref[TOP:].astype(f32))[0]
    for copy in copies:
        copy.wait()
    cells_ref[...] = (normed * gain_ref[...]).astype(bf16)
    xs_ref[...] = dot(pick_ref[:INNER, :BAND_CELLS], cells_ref[:BAND_CELLS]).astype(bf16)
    qkv_ref[...] = dot(xs_ref[...], wqkv_ref[...]).astype(bf16)
    attend([False] * LOCAL, qkv_ref, mixed_ref, probs_ref)
    att_ref[...] = dot(mixed_ref[...], wproj_ref[...]).astype(bf16)


def outer_kernel(
    tok_ref, cells_ref, lat_ref, lon_ref, diag_ref, gain_ref, wqkv_ref, wproj_ref, pick_ref, shift_ref, cells_pick_ref,
    att0_ref,
    xs_ref, qkv_ref, mixed_ref, probs_ref, tok_out_ref, summed_ref, row_ref,
    att_ref,
):
    def normed(values):
        return norm_parts(values)[0] * gain_ref[...]

    lat, lon, diag = lat_ref[...], lon_ref[:EDGE].astype(f32), diag_ref[:TURN].astype(f32)
    first, second = band_sources(cells_ref[...], normed(lat.astype(f32)).astype(bf16), normed(lon), normed(diag))
    xs_ref[:PAD] = dot(pick_ref[INNER:], first).astype(bf16)
    xs_ref[PAD:] = dot(pick_ref[...], second).astype(bf16)
    qkv_ref[...] = dot(xs_ref[...], wqkv_ref[...]).astype(bf16)
    attend([False] + [True] * PER_BAND, qkv_ref, mixed_ref, probs_ref)
    att_ref[:INNER] = att0_ref[...]
    att_ref[INNER:] = dot(mixed_ref[...], wproj_ref[...]).astype(bf16)
    for band, source in enumerate(band_sources(tok_ref[TOP:], lat, lon, diag)):
        rows = pl.ds(band * BAND_CELLS, BAND_CELLS)
        tokens = dot(shift_ref[...], source)
        added = dot(cells_pick_ref[...], att_ref[pl.ds(band * BAND, BAND)])
        tok_out_ref[rows] = tokens.astype(bf16)
        summed_ref[rows] = (tokens + added).astype(bf16)
    row_ref[...] = summed_ref[TOKENS - COLS :]


def cotangent_kernel(
    g_ref, lat_ref, lon_ref, diag_ref, gain_ref, shift_ref, xs0_ref, xs_ref, mixed0_ref, mixed_ref, wmerge_ref,
    out_ref, weights_ref, xst_ref, mixt_ref, sem
):
    copy = pltpu.make_async_copy(wmerge_ref, weights_ref, sem)
    copy.start()
    xst_ref[...] = jnp.concatenate([xs0_ref[...], xs_ref[...]], axis=0).T
    mixt_ref[...] = jnp.concatenate([mixed0_ref[...], mixed_ref[...]], axis=0).T
    parts = []
    for half in range(2):
        lat = lat_ref[...].astype(f32)[half * PAIR_TOP : (half + 1) * PAIR_TOP]
        at = EDGE + half * PAIR_SIDE
        lon = lon_ref[at : at + PAIR_SIDE].astype(f32)[PAIR_CORNER:]
        diag = diag_ref[TURN:].astype(f32)[half * PAIR_CORNER : (half + 1) * PAIR_CORNER]
        own = g_ref[:, half * D : (half + 1) * D].astype(f32)[PAIR_TOP:]
        source = jnp.concatenate([own, lat, lon, diag], axis=0).astype(bf16)
        parts.append(dot(shift_ref[...], source).astype(bf16))
    cots = jnp.concatenate(parts, axis=1)
    copy.wait()
    for k in range(4):
        out_ref[k] = dot_nt(cots, weights_ref[k * D : (k + 1) * D]) * gain_ref[k]


def pair_kernel(
    summed_ref, row_ref, gain_ref, cot_ref, pair_ref, unpair_ref,
    dsum_ref, out_row_ref, normed_ref,
    members_ref,
):
    quarter = COLS
    for part in range(3):
        first = part * 4 * COLS - COLS
        if part:
            summed = summed_ref[first : first + 4 * COLS]
        else:
            summed = jnp.concatenate([row_ref[...], summed_ref[: 3 * COLS]], axis=0)
        paired = dot(pair_ref[...], summed)
        for k in range(4):
            members_ref[k, pl.ds(part * quarter, quarter)] = paired[k * quarter : (k + 1) * quarter]
    width = 4 * D
    total = sum(jnp.sum(members_ref[k], axis=-1, keepdims=True) for k in range(4))
    center = total / width
    for k in range(4):
        members_ref[k] = members_ref[k] - center
    spread = sum(jnp.sum(members_ref[k] * members_ref[k], axis=-1, keepdims=True) for k in range(4)) / width
    scale = lax.rsqrt(spread + EPS)
    for k in range(4):
        members_ref[k] = members_ref[k] * scale
        normed_ref[k] = (members_ref[k] * gain_ref[k]).astype(bf16)
    flat = sum(jnp.sum(cot_ref[k], axis=-1, keepdims=True) for k in range(4)) / width
    along = sum(jnp.sum(cot_ref[k] * members_ref[k], axis=-1, keepdims=True) for k in range(4)) / width
    for k in range(4):
        members_ref[k] = (cot_ref[k] - flat - members_ref[k] * along) * scale
    for part in range(3):
        rows = pl.ds(part * quarter, quarter)
        block = jnp.concatenate([members_ref[k, rows].astype(bf16) for k in range(4)], axis=0)
        dsum_ref[pl.ds(part * 4 * COLS, 4 * COLS)] = dot(unpair_ref[...], block).astype(bf16)
    out_row_ref[...] = dsum_ref[:COLS]


def merge_kernel(normed_ref, wmerge_ref, unshift_ref, main_ref, lat_ref, lon_ref, diag_ref):
    total = dot(normed_ref[0], wmerge_ref[:D])
    for k in range(1, 4):
        total = total + dot(normed_ref[k], wmerge_ref[k * D : (k + 1) * D])
    pairs = dot(unshift_ref[...], total.astype(bf16))
    main_ref[...] = pairs[:PAIRS].astype(bf16)
    lat_ref[...] = halves(pairs[PAIRS - PAIR_TOP : PAIRS]).astype(bf16)
    lon_ref[...] = halves(pairs[PAIRS : PAIRS + PAIR_SIDE - PAIR_CORNER]).astype(bf16)
    diag_ref[...] = halves(pairs[PAIRS + PAIR_SIDE - PAIR_CORNER :]).astype(bf16)


def inner_back_kernel(
    dsum_ref, qkv0_ref, probs0_ref, qkv_ref, probs_ref, wproj_ref, pick_ref,
    up_ref, dqkv_ref,
    dmix_ref,
):
    up_ref[...] = dot(pick_ref[...], dsum_ref[COLS : COLS + BAND_CELLS]).astype(bf16)
    dmix_ref[...] = dot_nt(up_ref[...], wproj_ref[...]).astype(bf16)
    windows = [(qkv0_ref, probs0_ref, win) for win in range(LOCAL)] + [(qkv_ref, probs_ref, 0)]
    attend_back(windows, dmix_ref, dqkv_ref, 0)


def outer_back_kernel(
    dsum_ref, row_ref, xst_ref, mixt_ref, up0_ref, dqkv0_ref, qkv_ref, probs_ref, wproj_ref, pick_ref,
    dqkv_ref, keep_ref, send_ref,
    up_ref, dmix_ref,
):
    cells = jnp.concatenate([dsum_ref[COLS + BAND_CELLS :], row_ref[...]], axis=0)
    up_ref[:BAND] = up0_ref[...]
    up_ref[BAND:] = dot(pick_ref[...], cells).astype(bf16)
    dqkv_ref[:BAND] = dqkv0_ref[...]
    dmix_ref[...] = dot_nt(up_ref[BAND:], wproj_ref[...]).astype(bf16)
    attend_back([(qkv_ref, probs_ref, win) for win in range(1, REST)], dmix_ref, dqkv_ref, BAND)
    lat_at, lon_at = lax.axis_index("lat"), lax.axis_index("lon")
    even_core = lax.rem(lon_at, 2) == 0
    my_x = lax.rem(lax.div(lon_at, 2), 4)
    my_y = lax.div(lat_at, 8) * 2 + lax.div(lon_at, 8)
    x_steps = [lax.bitwise_xor(my_x, jnp.int32(i)) for i in range(4)]
    y_steps = [lax.bitwise_xor(my_y, jnp.int32(i)) for i in range(4)]
    for col in range(8):
        if col < 6:
            grad = dot(xst_ref[...], dqkv_ref[:, col * 256 : (col + 1) * 256])
        else:
            grad = dot(mixt_ref[...], up_ref[:, (col - 6) * 256 : (col - 5) * 256])
        even, odd = grad[:, :128], grad[:, 128:]
        kept = jnp.where(even_core, even, odd).astype(bf16)
        sent = jnp.where(even_core, odd, even).astype(bf16)
        low, x = divmod(col, 4)
        for lat in range(16):
            high, z = divmod(lat, 8)
            y = high * 2 + low
            rows = slice(lat * 32, (lat + 1) * 32)
            on_even = x_steps[x], lat * 2 + low
            on_odd = y_steps[y], z * 4 + x
            mine = [jnp.where(even_core, a, b) for a, b in zip(on_even, on_odd)]
            other = [jnp.where(even_core, b, a) for a, b in zip(on_even, on_odd)]
            keep_ref[mine[0], mine[1]] = kept[rows]
            send_ref[other[0], other[1]] = sent[rows]


def cells_back_kernel(
    dqkv_ref, wqkv_ref, cells_pick_ref, unshift_ref, tok_ref, dsum_ref, row_ref, gain_ref, m_lon_ref, m_diag_ref,
    main_ref, lat_ref, lon_ref, diag_ref,
    dx_ref,
):
    dx_ref[...] = dot_nt(dqkv_ref[...], wqkv_ref[...]).astype(bf16)
    for band in range(2):
        if band == 0:
            above = dsum_ref[COLS : COLS + BAND_CELLS]
        else:
            above = jnp.concatenate([dsum_ref[COLS + BAND_CELLS :], row_ref[...]], axis=0)
        cot = dot(cells_pick_ref[...], dx_ref[pl.ds(band * BAND, BAND)]) * gain_ref[...]
        normed, scale = norm_parts(tok_ref[pl.ds(band * BAND_CELLS, BAND_CELLS)].astype(f32))
        flat = jnp.mean(cot, axis=-1, keepdims=True)
        along = jnp.mean(cot * normed, axis=-1, keepdims=True)
        grads = (above.astype(f32) + (cot - flat - normed * along) * scale).astype(bf16)
        cells = dot(unshift_ref[...], grads).astype(bf16)
        if band == 0:
            main_ref[:BAND_CELLS] = cells[:BAND_CELLS]
        else:
            main_ref[BAND_CELLS:] = cells[: BAND_CELLS - TOP]
            lat_ref[...] = cells[BAND_CELLS - TOP : BAND_CELLS]
            diag_ref[:TURN] = cells[BAND_CELLS + SIDE - TURN :]
        lon_ref[band * SIDE : (band + 1) * SIDE] = cells[BAND_CELLS:]
    lon_ref[EDGE:] = m_lon_ref[...]
    diag_ref[TURN:] = m_diag_ref[...]


def fill_edge(field, side, rows, cols):
    width = field.shape[-1]
    field, side = field.astype(f32).reshape(rows, cols, width), side.astype(f32).reshape(rows, BORDER, width)
    first = field[:, :BORDER] + side
    return jnp.concatenate([first, field[:, BORDER:]], axis=1).reshape(rows * cols, width)


def own_cells_kernel(main_ref, lat_ref, lon_ref, diag_ref, m_main_ref, m_lat_ref, tokens_ref, merged_ref):
    corner = diag_ref[:TURN].astype(f32)[TURN - CORNER :]
    beside = lon_ref[:EDGE].astype(f32)[: EDGE - CORNER]
    tokens_ref[:TOP] = fill_edge(lat_ref[...], corner, SHIFT_LAT, COLS).astype(bf16)
    tokens_ref[TOP:] = fill_edge(main_ref[...], beside, ROWS - SHIFT_LAT, COLS).astype(bf16)
    side_rows = PAIR_SIDE - PAIR_CORNER
    for half in range(2):
        cols = pl.ds(half * D, D)
        lat = m_lat_ref[...].astype(f32)[half * PAIR_TOP : (half + 1) * PAIR_TOP]
        lon = lon_ref[EDGE:].astype(f32)[half * side_rows : (half + 1) * side_rows]
        diag = diag_ref[TURN:].astype(f32)[half * PAIR_CORNER : (half + 1) * PAIR_CORNER]
        own = m_main_ref[:, cols].astype(f32)[: PAIRS - PAIR_TOP]
        field, side = jnp.concatenate([lat, own], axis=0), jnp.concatenate([diag, lon], axis=0)
        merged_ref[:, cols] = fill_edge(field, side, PAIR_ROWS, PAIR_COLS).astype(bf16)


def add_kernel(a_ref, b_ref, *out_refs):
    for k, out_ref in enumerate(out_refs):
        out_ref[...] = (a_ref[k].astype(f32) + b_ref[k].astype(f32)).astype(bf16)


def join_kernel(a_ref, b_ref, c_ref, d_ref, out_ref):
    total = a_ref[...].astype(f32) + b_ref[...].astype(f32) + c_ref[...].astype(f32) + d_ref[...].astype(f32)
    out_ref[...] = total.astype(bf16)


def sum_kernel(parts_ref, out_ref):
    total = parts_ref[0].astype(f32)
    for i in range(1, parts_ref.shape[0]):
        total = total + parts_ref[i].astype(f32)
    out_ref[...] = total.astype(out_ref.dtype)


def call(kernel, outs, scratch=(), places=None, limit=20):
    spaces = {} if places is None else {
        "in_specs": [pl.BlockSpec(memory_space=(pltpu.VMEM, pl.ANY, pltpu.HBM)[p]) for p in places]
    }
    return pl.pallas_call(
        kernel,
        out_shape=[jax.ShapeDtypeStruct(s, t) for s, t in outs],
        scratch_shapes=[pltpu.VMEM(*s) if isinstance(s, tuple) else s for s in scratch],
        cost_estimate=pl.CostEstimate(flops=10**9, bytes_accessed=2 * 10**6, transcendentals=0),
        compiler_params=pltpu.CompilerParams(vmem_limit_bytes=limit * 1024 * 1024),
        **spaces,
    )


def saved(count):
    rows = count * PAD
    return [((rows, D), bf16), ((rows, 3 * D), bf16), ((rows, D), bf16), ((count, 2, PAD, GROUP * PAD), f32)]


def after(value, *others):
    return lax.optimization_barrier((value, *others))[0]


def chain(tok, gain, w_qkv, w_proj, gain_merge, w_merge, g_merged, fetch, up, down):
    tok, g_merged, top, g_top, edge, corner = call(
        border_kernel,
        [
            ((TOKENS, D), bf16), ((PAIRS, 2 * D), bf16),
            ((TOP, D), bf16), ((2 * PAIR_TOP, D), bf16),
            ((EDGE + 2 * PAIR_SIDE, D), bf16), ((TURN + 2 * PAIR_CORNER, D), bf16),
        ],
        [pltpu.SemaphoreType.DMA((2,))],
        [2, 2],
    )(tok, g_merged)
    beside = fetch(top, edge, corner)
    g_lat = up(g_top)
    pair, band = pair_selector(), band_selector()
    shift = shift_selector(WIN_LAT, COLS, SHIFT_LON)
    pair_shift = shift_selector(PAIR_ROWS, PAIR_COLS, SHIFT_LON // 2)
    held = [gain, jnp.asarray(band @ shift, bf16), w_qkv, w_proj, gain_merge]
    held += [jnp.asarray(c, bf16) for c in (shift, band.T, pair, pair.T, pair_shift)]
    got = call(
        inner_kernel,
        [(h.shape, h.dtype) for h in held] + [((TOKENS - TOP, D), bf16)] + saved(LOCAL) + [((INNER, D), bf16)],
        [pltpu.SemaphoreType.DMA((HELD,))],
        [0] + [1] * HELD,
    )(tok, *held)
    gain, pick, w_qkv, w_proj, gain_merge, shift, cells_pick, pair, unpair, pair_shift = got[:HELD]
    cells, xs0, qkv0, mixed0, probs0, att0 = got[HELD:]
    xs1, qkv1, mixed1, probs1, tok, summed, row = call(
        outer_kernel,
        saved(REST) + [((TOKENS, D), bf16), ((TOKENS, D), bf16), ((COLS, D), bf16)],
        [((WIDTH, D), bf16)],
    )(tok, cells, *beside, gain, w_qkv, w_proj, pick, shift, cells_pick, att0)
    behind = down(row)
    cots, w_merge, xst, mixt = call(
        cotangent_kernel,
        [((4, PAIRS, D), f32), ((4 * D, 2 * D), bf16), ((D, WIDTH), bf16), ((D, WIDTH), bf16)],
        [pltpu.SemaphoreType.DMA],
        [0] * 10 + [1],
    )(after(g_merged, row), g_lat, *beside[1:], gain_merge, pair_shift, xs0, xs1, mixed0, mixed1, w_merge)
    d_summed, row, merge_normed = call(
        pair_kernel,
        [((TOKENS, D), bf16), ((COLS, D), bf16), ((4, PAIRS, D), bf16)],
        [((4, PAIRS, D), f32)],
    )(summed, behind, gain_merge, cots, pair, unpair)
    last = up(row)
    band = jnp.asarray(band_selector(), bf16)
    unshift = jnp.asarray(shift_selector(WIN_LAT, COLS, SHIFT_LON).T, bf16)
    pair_unshift = jnp.asarray(shift_selector(PAIR_ROWS, PAIR_COLS, SHIFT_LON // 2).T, bf16)
    up0, dqkv0 = call(
        inner_back_kernel, [((BAND, D), bf16), ((BAND, 3 * D), bf16)], [((BAND, D), bf16)]
    )(d_summed, qkv0, probs0, qkv1, probs1, w_proj, band)
    m_main, m_lat, m_lon, m_diag = call(
        merge_kernel,
        [
            ((PAIRS, 2 * D), bf16), ((2 * PAIR_TOP, D), bf16),
            ((2 * (PAIR_SIDE - PAIR_CORNER), D), bf16), ((2 * PAIR_CORNER, D), bf16),
        ],
    )(merge_normed, w_merge, pair_unshift)
    m_lat = down(m_lat)
    dqkv, keep, sent = call(
        outer_back_kernel,
        [((WIDTH, 3 * D), bf16), ((4, 32, 32, 128), bf16), ((4, 32, 32, 128), bf16)],
        [((WIDTH, D), bf16), ((BAND, D), bf16)],
    )(d_summed, last, xst, mixt, after(up0, m_main), dqkv0, qkv1, probs1, w_proj, band)
    main, to_lat, to_lon, to_diag = call(
        cells_back_kernel,
        [
            ((TOKENS - TOP, D), bf16), ((TOP, D), bf16),
            ((EDGE + 2 * (PAIR_SIDE - PAIR_CORNER), D), bf16), ((TURN + 2 * PAIR_CORNER, D), bf16),
        ],
        [((WIDTH, D), bf16)],
    )(dqkv, w_qkv, cells_pick, unshift, tok, d_summed, last, gain, m_lon, m_diag)

    def finish(lat, lon, diag):
        grad_tokens, merged = call(own_cells_kernel, [((TOKENS, D), bf16), ((PAIRS, 2 * D), bf16)])(
            main, lat, lon, diag, m_main, m_lat
        )
        return merged, grad_tokens

    return finish, keep, sent, (to_lat, to_lon, to_diag), m_lat


def solution(mesh):
    lats, lons = mesh.shape["lat"], mesh.shape["lon"]
    count = lats * lons

    def send(block, down, right):
        route = [
            (i, (i // lons + down) % lats * lons + (i % lons + right) % lons) for i in range(count)
        ]
        return lax.ppermute(block, ("lat", "lon"), route)

    def fetch(top, edge, corner):
        return send(top, -1, 0), send(edge, 0, -1), send(corner, -1, -1)

    def place(i):
        lat, lon = divmod(i, lons)
        return lat // 8, lat % 8, lon // 8, lon // 2 % 4, lon % 2

    def across(i, step):
        high, z, low, x, core = place(i)
        if core:
            high, low = divmod((high * 2 + low) ^ step, 2)
        else:
            x = x ^ step
        return (high * 8 + z) * lons + low * 8 + x * 2 + core

    rest = {}
    for i in range(count):
        high, z, low, x, core = place(i)
        rest.setdefault((core, high * 2 + low if core else x), []).append(i)
    rest = list(rest.values())

    def swap(block, step):
        return lax.ppermute(block, ("lat", "lon"), [(i, across(i, step)) for i in range(count)])

    def reduce_across(keep, sent, to_lat):
        other = lax.ppermute(sent, ("lat", "lon"), [(i, i ^ 1) for i in range(count)])
        own, *others = call(add_kernel, [((32, 32, 128), bf16)] * 4)(keep, after(other, to_lat))
        got = [swap(block, step) for step, block in enumerate(others, 1)]
        return call(join_kernel, [((32, 32, 128), bf16)])(own, *got)[0]

    def reduce_rest(sums):
        parts = lax.all_to_all(sums, ("lat", "lon"), 0, 0, axis_index_groups=rest, tiled=True)
        return call(sum_kernel, [((32, 128), f32)])(parts)[0]

    def body(tokens, gain_attn, w_qkv, w_proj, gain_merge, w_merge, g_merged):
        finish, keep, sent, pieces, m_lat = chain(
            tokens.reshape(TOKENS, D), gain_attn.reshape(1, D), w_qkv, w_proj, gain_merge.reshape(4, 1, D),
            w_merge, g_merged.reshape(PAIRS, 2 * D), fetch,
            lambda row: send(row, -1, 0), lambda row: send(row, 1, 0),
        )
        sums = after(reduce_across(keep, sent, pieces[0]), m_lat)
        grad_weights = reduce_rest(sums)
        to_lat, to_lon, to_diag = pieces
        beside = send(to_lat, 1, 0), send(to_lon, 0, 1), send(to_diag, 1, 1)
        merged, grad_tokens = finish(*(after(piece, sums) for piece in beside))
        return (
            merged.reshape(ROWS // 2, COLS // 2, 2 * D),
            grad_tokens.reshape(ROWS, COLS, D),
            grad_weights,
        )

    return jax.shard_map(
        body,
        mesh=mesh,
        in_specs=(P("lat", "lon", None), P(), P(), P(), P(), P(), P("lat", "lon", None)),
        out_specs=(P("lat", "lon", None), P("lat", "lon", None), P("lat", "lon")),
        check_vma=False,
    )
```

```python
import jax
import jax.numpy as jnp
import numpy as np
from jax import lax
from jax.experimental import pallas as pl
from jax.experimental.pallas import tpu as pltpu
from jax.sharding import PartitionSpec as P

D = 512
HEADS = 8
HEAD = D // HEADS
WIN_LAT = 6
WIN_LON = 12
SHIFT_LAT = 3
SHIFT_LON = 6
EPS = 1e-05

ROWS, COLS = 12, 48
BORDER = 8
TOKENS = ROWS * COLS
LEN = WIN_LAT * WIN_LON
PAD = 80
PER_BAND = COLS // WIN_LON
BAND = PER_BAND * PAD
WINDOWS = 2 * PER_BAND
TOP = SHIFT_LAT * COLS
EDGE = ROWS * BORDER
CORNER = SHIFT_LAT * BORDER
SIDE = WIN_LAT * BORDER
TURN = 4 * BORDER
BAND_CELLS = WIN_LAT * COLS
GROUP = HEADS // 2
GROUP_WIDTH = GROUP * HEAD
LOCAL = PER_BAND - 1
INNER = LOCAL * PAD
REST = WINDOWS - LOCAL
OUTER = REST * PAD
PAIR_ROWS, PAIR_COLS = ROWS // 2, COLS // 2
PAIRS = PAIR_ROWS * PAIR_COLS
PAIR_TOP = PAIR_COLS
PAIR_SIDE = PAIR_ROWS * BORDER
PAIR_CORNER = BORDER
HELD = 10
WIDTH = WINDOWS * PAD
NEG = -1e30

f32 = jnp.float32
bf16 = jnp.bfloat16


def band_selector():
    pick = np.zeros((BAND, BAND_CELLS), np.float32)
    for win in range(PER_BAND):
        for i in range(WIN_LAT):
            for j in range(WIN_LON):
                pick[win * PAD + i * WIN_LON + j, i * COLS + win * WIN_LON + j] = 1.0
    return pick


def shift_selector(rows, cols, shift):
    pick = np.zeros((rows * cols, rows * (cols + BORDER)), np.float32)
    for i in range(rows):
        for j in range(cols):
            col = j + shift
            pick[i * cols + j, i * cols + col if col < cols else rows * cols + i * BORDER + col - cols] = 1.0
    return pick


def pair_selector():
    pick = np.zeros((4 * COLS, 4 * COLS), np.float32)
    quarter = COLS
    for a in range(2):
        for b in range(COLS // 2):
            for k, (i, j) in enumerate(((0, 0), (1, 0), (0, 1), (1, 1))):
                pick[k * quarter + a * (COLS // 2) + b, (2 * a + i) * COLS + 2 * b + j] = 1.0
    return pick


def dot(a, b):
    return lax.dot_general(a, b, (((1,), (0,)), ((), ())), preferred_element_type=f32)


def dot_nt(a, b):
    return lax.dot_general(a, b, (((1,), (1,)), ((), ())), preferred_element_type=f32)


def dot_tn(a, b):
    return lax.dot_general(a, b, (((0,), (0,)), ((), ())), preferred_element_type=f32)


def norm_parts(values):
    centred = values - jnp.mean(values, axis=-1, keepdims=True)
    scale = lax.rsqrt(jnp.mean(centred * centred, axis=-1, keepdims=True) + EPS)
    return centred * scale, scale


def band_sources(cells, lat, lon, diag):
    first = jnp.concatenate([cells[:BAND_CELLS], lon[CORNER : CORNER + SIDE].astype(bf16)], axis=0)
    beside = jnp.concatenate([lon[CORNER + SIDE : EDGE], diag[:CORNER]], axis=0).astype(bf16)
    second = jnp.concatenate([cells[BAND_CELLS:], lat, beside], axis=0)
    return first, second


def halves(block):
    return jnp.concatenate([block[:, :D], block[:, D:]], axis=0)


def head_masks():
    lane = lax.broadcasted_iota(jnp.int32, (1, GROUP_WIDTH), 1) // HEAD
    return [(lane == h).astype(f32).astype(bf16) for h in range(GROUP)]


def spread_heads(block, masks):
    return jnp.concatenate([block * m for m in masks], axis=0)


def per_head(stacked, block):
    first = lax.broadcasted_iota(jnp.int32, (1, 2 * HEAD), 1) < HEAD
    all_heads = dot_tn(stacked, block)
    out = []
    for pair in range(GROUP // 2):
        part = all_heads[:, pair * 2 * HEAD : (pair + 1) * 2 * HEAD]
        at = pair * 2 * PAD
        out.append(jnp.where(first, part[at : at + PAD], part[at + PAD : at + 2 * PAD]))
    return jnp.concatenate(out, axis=1)


def last_band():
    at_end = lax.axis_index("lat") == lax.axis_size("lat") - 1
    return jnp.where(at_end, f32(1), f32(0))


def halves_apart():
    shape = (LEN, GROUP * PAD)
    key = lax.broadcasted_iota(jnp.int32, shape, 0)
    query = lax.rem(lax.broadcasted_iota(jnp.int32, shape, 1), PAD)
    return jnp.where((key < LEN // 2) != (query < LEN // 2), f32(NEG), f32(0)) * last_band()


def attend(windows, qkv_ref, mixed_ref, probs_ref):
    masks = [m * HEAD ** (-0.5) for m in head_masks()]
    apart = halves_apart() if any(windows) else None
    for win, wraps in enumerate(windows):
        rows = pl.ds(win * PAD, PAD)
        for g in range(2):
            at = g * GROUP_WIDTH
            queries = spread_heads(qkv_ref[rows, at : at + GROUP_WIDTH], masks)
            keys = qkv_ref[rows, D + at : D + at + GROUP_WIDTH]
            values = qkv_ref[rows, 2 * D + at : 2 * D + at + GROUP_WIDTH]
            scores = dot_nt(keys, queries)[:LEN]
            if wraps:
                scores = scores + apart
            weights = jnp.exp(scores - jnp.max(scores, axis=0, keepdims=True))
            probs = weights * (1.0 / jnp.sum(weights, axis=0, keepdims=True))
            probs = jnp.concatenate([probs, jnp.zeros((PAD - LEN, GROUP * PAD), f32)], axis=0)
            probs_ref[win, g] = probs
            mixed_ref[rows, at : at + GROUP_WIDTH] = per_head(probs.astype(bf16), values).astype(bf16)


def attend_back(windows, dmix_ref, dqkv_ref, offset):
    masks = head_masks()
    scaled = [m * HEAD ** (-0.5) for m in masks]
    for win, (qkv_ref, probs_ref, place) in enumerate(windows):
        rows = pl.ds(place * PAD, PAD)
        out = pl.ds(offset + win * PAD, PAD)
        for g in range(2):
            at = g * GROUP_WIDTH
            queries = spread_heads(qkv_ref[rows, at : at + GROUP_WIDTH], scaled)
            keys = qkv_ref[rows, D + at : D + at + GROUP_WIDTH]
            values = qkv_ref[rows, 2 * D + at : 2 * D + at + GROUP_WIDTH]
            above = spread_heads(dmix_ref[pl.ds(win * PAD, PAD), at : at + GROUP_WIDTH], masks)
            probs = probs_ref[place, g]
            d_probs = dot_nt(values, above)
            along = jnp.sum(probs * d_probs, axis=0, keepdims=True)
            d_scores = (probs * (d_probs - along)).astype(bf16)
            d_queries = per_head(d_scores, keys) * HEAD ** (-0.5)
            d_keys = dot(d_scores, queries)
            d_values = dot(probs.astype(bf16), above)
            dqkv_ref[out, at : at + GROUP_WIDTH] = d_queries.astype(bf16)
            dqkv_ref[out, D + at : D + at + GROUP_WIDTH] = d_keys.astype(bf16)
            dqkv_ref[out, 2 * D + at : 2 * D + at + GROUP_WIDTH] = d_values.astype(bf16)


def border_kernel(tok_ref, g_ref, own_ref, own_g_ref, top_ref, g_top_ref, edge_ref, corner_ref, sem):
    copies = [
        pltpu.make_async_copy(tok_ref, own_ref, sem.at[0]),
        pltpu.make_async_copy(g_ref, own_g_ref, sem.at[1]),
    ]
    for copy in copies:
        copy.start()
    for copy in copies:
        copy.wait()
    edge = [own_ref[row * COLS : row * COLS + 16].astype(f32)[:BORDER] for row in range(ROWS)]
    cots = own_g_ref[...].astype(f32)
    side = [cots[row * PAIR_COLS : row * PAIR_COLS + BORDER] for row in range(PAIR_ROWS)]
    top_ref[...] = own_ref[:TOP]
    g_top_ref[...] = halves(cots[:PAIR_TOP]).astype(bf16)
    edge_ref[:EDGE] = jnp.concatenate(edge, axis=0).astype(bf16)
    edge_ref[EDGE:] = halves(jnp.concatenate(side, axis=0).astype(bf16))
    corner_ref[:TURN] = jnp.concatenate(edge[:4], axis=0).astype(bf16)
    corner_ref[TURN:] = halves(side[0]).astype(bf16)


def inner_kernel(tok_ref, *refs):
    held, got = refs[:HELD], refs[HELD : 2 * HELD]
    cells_ref, xs_ref, qkv_ref, mixed_ref, probs_ref, att_ref, sem = refs[2 * HELD :]
    copies = [pltpu.make_async_copy(a, b, sem.at[i]) for i, (a, b) in enumerate(zip(held, got))]
    for copy in copies:
        copy.start()
    gain_ref, pick_ref, wqkv_ref, wproj_ref = got[:4]
    normed = norm_parts(tok_ref[TOP:].astype(f32))[0]
    for copy in copies:
        copy.wait()
    cells_ref[...] = (normed * gain_ref[...]).astype(bf16)
    xs_ref[...] = dot(pick_ref[:INNER, :BAND_CELLS], cells_ref[:BAND_CELLS]).astype(bf16)
    qkv_ref[...] = dot(xs_ref[...], wqkv_ref[...]).astype(bf16)
    attend([False] * LOCAL, qkv_ref, mixed_ref, probs_ref)
    att_ref[...] = dot(mixed_ref[...], wproj_ref[...]).astype(bf16)


def outer_kernel(
    tok_ref, cells_ref, lat_ref, lon_ref, diag_ref, gain_ref, wqkv_ref, wproj_ref, pick_ref, shift_ref, cells_pick_ref,
    att0_ref,
    xs_ref, qkv_ref, mixed_ref, probs_ref, tok_out_ref, summed_ref, row_ref,
    att_ref,
):
    def normed(values):
        return norm_parts(values)[0] * gain_ref[...]

    lat, lon, diag = lat_ref[...], lon_ref[:EDGE].astype(f32), diag_ref[:TURN].astype(f32)
    first, second = band_sources(cells_ref[...], normed(lat.astype(f32)).astype(bf16), normed(lon), normed(diag))
    xs_ref[:PAD] = dot(pick_ref[INNER:], first).astype(bf16)
    xs_ref[PAD:] = dot(pick_ref[...], second).astype(bf16)
    qkv_ref[...] = dot(xs_ref[...], wqkv_ref[...]).astype(bf16)
    attend([False] + [True] * PER_BAND, qkv_ref, mixed_ref, probs_ref)
    att_ref[:INNER] = att0_ref[...]
    att_ref[INNER:] = dot(mixed_ref[...], wproj_ref[...]).astype(bf16)
    for band, source in enumerate(band_sources(tok_ref[TOP:], lat, lon, diag)):
        rows = pl.ds(band * BAND_CELLS, BAND_CELLS)
        tokens = dot(shift_ref[...], source)
        added = dot(cells_pick_ref[...], att_ref[pl.ds(band * BAND, BAND)])
        tok_out_ref[rows] = tokens.astype(bf16)
        summed_ref[rows] = (tokens + added).astype(bf16)
    row_ref[...] = summed_ref[TOKENS - COLS :]


def cotangent_kernel(
    g_ref, lat_ref, lon_ref, diag_ref, gain_ref, shift_ref, wmerge_ref, out_ref, weights_ref, sem
):
    copy = pltpu.make_async_copy(wmerge_ref, weights_ref, sem)
    copy.start()
    parts = []
    for half in range(2):
        lat = lat_ref[...].astype(f32)[half * PAIR_TOP : (half + 1) * PAIR_TOP]
        at = EDGE + half * PAIR_SIDE
        lon = lon_ref[at : at + PAIR_SIDE].astype(f32)[PAIR_CORNER:]
        diag = diag_ref[TURN:].astype(f32)[half * PAIR_CORNER : (half + 1) * PAIR_CORNER]
        own = g_ref[:, half * D : (half + 1) * D].astype(f32)[PAIR_TOP:]
        source = jnp.concatenate([own, lat, lon, diag], axis=0).astype(bf16)
        parts.append(dot(shift_ref[...], source).astype(bf16))
    cots = jnp.concatenate(parts, axis=1)
    copy.wait()
    for k in range(4):
        out_ref[k] = dot_nt(cots, weights_ref[k * D : (k + 1) * D]) * gain_ref[k]


def pair_kernel(
    summed_ref, row_ref, gain_ref, cot_ref, pair_ref, unpair_ref,
    dsum_ref, out_row_ref, normed_ref,
    members_ref,
):
    quarter = COLS
    for part in range(3):
        first = part * 4 * COLS - COLS
        if part:
            summed = summed_ref[first : first + 4 * COLS]
        else:
            summed = jnp.concatenate([row_ref[...], summed_ref[: 3 * COLS]], axis=0)
        paired = dot(pair_ref[...], summed)
        for k in range(4):
            members_ref[k, pl.ds(part * quarter, quarter)] = paired[k * quarter : (k + 1) * quarter]
    width = 4 * D
    total = sum(jnp.sum(members_ref[k], axis=-1, keepdims=True) for k in range(4))
    center = total / width
    for k in range(4):
        members_ref[k] = members_ref[k] - center
    spread = sum(jnp.sum(members_ref[k] * members_ref[k], axis=-1, keepdims=True) for k in range(4)) / width
    scale = lax.rsqrt(spread + EPS)
    for k in range(4):
        members_ref[k] = members_ref[k] * scale
        normed_ref[k] = (members_ref[k] * gain_ref[k]).astype(bf16)
    flat = sum(jnp.sum(cot_ref[k], axis=-1, keepdims=True) for k in range(4)) / width
    along = sum(jnp.sum(cot_ref[k] * members_ref[k], axis=-1, keepdims=True) for k in range(4)) / width
    for k in range(4):
        members_ref[k] = (cot_ref[k] - flat - members_ref[k] * along) * scale
    for part in range(3):
        rows = pl.ds(part * quarter, quarter)
        block = jnp.concatenate([members_ref[k, rows].astype(bf16) for k in range(4)], axis=0)
        dsum_ref[pl.ds(part * 4 * COLS, 4 * COLS)] = dot(unpair_ref[...], block).astype(bf16)
    out_row_ref[...] = dsum_ref[:COLS]


def merge_kernel(
    normed_ref, wmerge_ref, unshift_ref, cells_lon_ref, cells_diag_ref, main_ref, lat_ref, lon_ref, diag_ref
):
    total = dot(normed_ref[0], wmerge_ref[:D])
    for k in range(1, 4):
        total = total + dot(normed_ref[k], wmerge_ref[k * D : (k + 1) * D])
    pairs = dot(unshift_ref[...], total.astype(bf16))
    main_ref[...] = pairs[:PAIRS].astype(bf16)
    lat_ref[...] = halves(pairs[PAIRS - PAIR_TOP : PAIRS]).astype(bf16)
    lon_ref[:EDGE] = cells_lon_ref[...]
    lon_ref[EDGE:] = halves(pairs[PAIRS : PAIRS + PAIR_SIDE - PAIR_CORNER]).astype(bf16)
    diag_ref[:TURN] = cells_diag_ref[...]
    diag_ref[TURN:] = halves(pairs[PAIRS + PAIR_SIDE - PAIR_CORNER :]).astype(bf16)


def inner_back_kernel(
    dsum_ref, qkv0_ref, probs0_ref, qkv_ref, probs_ref, wproj_ref, pick_ref, xs0_ref, xs_ref, mixed0_ref, mixed_ref,
    up_ref, dqkv_ref, xst_ref, mixt_ref,
    dmix_ref,
):
    xst_ref[...] = jnp.concatenate([xs0_ref[...], xs_ref[...]], axis=0).T
    mixt_ref[...] = jnp.concatenate([mixed0_ref[...], mixed_ref[...]], axis=0).T
    up_ref[...] = dot(pick_ref[...], dsum_ref[COLS : COLS + BAND_CELLS]).astype(bf16)
    dmix_ref[...] = dot_nt(up_ref[...], wproj_ref[...]).astype(bf16)
    windows = [(qkv0_ref, probs0_ref, win) for win in range(LOCAL)] + [(qkv_ref, probs_ref, 0)]
    attend_back(windows, dmix_ref, dqkv_ref, 0)


def outer_back_kernel(
    dsum_ref, row_ref, xst_ref, mixt_ref, up0_ref, dqkv0_ref, qkv_ref, probs_ref, wproj_ref, pick_ref,
    dqkv_ref, keep_ref, send_ref,
    up_ref, dmix_ref,
):
    cells = jnp.concatenate([dsum_ref[COLS + BAND_CELLS :], row_ref[...]], axis=0)
    up_ref[:BAND] = up0_ref[...]
    up_ref[BAND:] = dot(pick_ref[...], cells).astype(bf16)
    dqkv_ref[:BAND] = dqkv0_ref[...]
    dmix_ref[...] = dot_nt(up_ref[BAND:], wproj_ref[...]).astype(bf16)
    attend_back([(qkv_ref, probs_ref, win) for win in range(1, REST)], dmix_ref, dqkv_ref, BAND)
    lat_at, lon_at = lax.axis_index("lat"), lax.axis_index("lon")
    even_core = lax.rem(lon_at, 2) == 0
    my_x = lax.rem(lax.div(lon_at, 2), 4)
    my_y = lax.div(lat_at, 8) * 2 + lax.div(lon_at, 8)
    x_steps = [lax.bitwise_xor(my_x, jnp.int32(i)) for i in range(4)]
    y_steps = [lax.bitwise_xor(my_y, jnp.int32(i)) for i in range(4)]
    for col in range(8):
        if col < 6:
            grad = dot(xst_ref[...], dqkv_ref[:, col * 256 : (col + 1) * 256])
        else:
            grad = dot(mixt_ref[...], up_ref[:, (col - 6) * 256 : (col - 5) * 256])
        even, odd = grad[:, :128], grad[:, 128:]
        kept = jnp.where(even_core, even, odd).astype(bf16)
        sent = jnp.where(even_core, odd, even).astype(bf16)
        low, x = divmod(col, 4)
        for lat in range(16):
            high, z = divmod(lat, 8)
            y = high * 2 + low
            rows = slice(lat * 32, (lat + 1) * 32)
            on_even = x_steps[x], lat * 2 + low
            on_odd = y_steps[y], z * 4 + x
            mine = [jnp.where(even_core, a, b) for a, b in zip(on_even, on_odd)]
            other = [jnp.where(even_core, b, a) for a, b in zip(on_even, on_odd)]
            keep_ref[mine[0], mine[1]] = kept[rows]
            send_ref[other[0], other[1]] = sent[rows]


def cells_back_kernel(
    dqkv_ref, wqkv_ref, cells_pick_ref, unshift_ref, tok_ref, dsum_ref, row_ref, gain_ref,
    main_ref, lat_ref, lon_ref, diag_ref,
    dx_ref,
):
    dx_ref[...] = dot_nt(dqkv_ref[...], wqkv_ref[...]).astype(bf16)
    for band in range(2):
        if band == 0:
            above = dsum_ref[COLS : COLS + BAND_CELLS]
        else:
            above = jnp.concatenate([dsum_ref[COLS + BAND_CELLS :], row_ref[...]], axis=0)
        cot = dot(cells_pick_ref[...], dx_ref[pl.ds(band * BAND, BAND)]) * gain_ref[...]
        normed, scale = norm_parts(tok_ref[pl.ds(band * BAND_CELLS, BAND_CELLS)].astype(f32))
        flat = jnp.mean(cot, axis=-1, keepdims=True)
        along = jnp.mean(cot * normed, axis=-1, keepdims=True)
        grads = (above.astype(f32) + (cot - flat - normed * along) * scale).astype(bf16)
        cells = dot(unshift_ref[...], grads).astype(bf16)
        if band == 0:
            main_ref[:BAND_CELLS] = cells[:BAND_CELLS]
        else:
            main_ref[BAND_CELLS:] = cells[: BAND_CELLS - TOP]
            lat_ref[...] = cells[BAND_CELLS - TOP : BAND_CELLS]
            diag_ref[...] = cells[BAND_CELLS + SIDE - TURN :]
        lon_ref[band * SIDE : (band + 1) * SIDE] = cells[BAND_CELLS:]


def fill_edge(field, side, rows, cols):
    width = field.shape[-1]
    field, side = field.astype(f32).reshape(rows, cols, width), side.astype(f32).reshape(rows, BORDER, width)
    first = field[:, :BORDER] + side
    return jnp.concatenate([first, field[:, BORDER:]], axis=1).reshape(rows * cols, width)


def own_cells_kernel(main_ref, lat_ref, lon_ref, diag_ref, m_main_ref, m_lat_ref, tokens_ref, merged_ref):
    corner = diag_ref[:TURN].astype(f32)[TURN - CORNER :]
    beside = lon_ref[:EDGE].astype(f32)[: EDGE - CORNER]
    tokens_ref[:TOP] = fill_edge(lat_ref[...], corner, SHIFT_LAT, COLS).astype(bf16)
    tokens_ref[TOP:] = fill_edge(main_ref[...], beside, ROWS - SHIFT_LAT, COLS).astype(bf16)
    side_rows = PAIR_SIDE - PAIR_CORNER
    for half in range(2):
        cols = pl.ds(half * D, D)
        lat = m_lat_ref[...].astype(f32)[half * PAIR_TOP : (half + 1) * PAIR_TOP]
        lon = lon_ref[EDGE:].astype(f32)[half * side_rows : (half + 1) * side_rows]
        diag = diag_ref[TURN:].astype(f32)[half * PAIR_CORNER : (half + 1) * PAIR_CORNER]
        own = m_main_ref[:, cols].astype(f32)[: PAIRS - PAIR_TOP]
        field, side = jnp.concatenate([lat, own], axis=0), jnp.concatenate([diag, lon], axis=0)
        merged_ref[:, cols] = fill_edge(field, side, PAIR_ROWS, PAIR_COLS).astype(bf16)


def add_kernel(a_ref, b_ref, *out_refs):
    for k, out_ref in enumerate(out_refs):
        out_ref[...] = (a_ref[k].astype(f32) + b_ref[k].astype(f32)).astype(bf16)


def join_kernel(a_ref, b_ref, c_ref, d_ref, out_ref):
    total = a_ref[...].astype(f32) + b_ref[...].astype(f32) + c_ref[...].astype(f32) + d_ref[...].astype(f32)
    out_ref[...] = total.astype(bf16)


def sum_kernel(parts_ref, out_ref):
    total = parts_ref[0].astype(f32)
    for i in range(1, parts_ref.shape[0]):
        total = total + parts_ref[i].astype(f32)
    out_ref[...] = total.astype(out_ref.dtype)


def call(kernel, outs, scratch=(), places=None, limit=20):
    spaces = {} if places is None else {
        "in_specs": [pl.BlockSpec(memory_space=(pltpu.VMEM, pl.ANY, pltpu.HBM)[p]) for p in places]
    }
    return pl.pallas_call(
        kernel,
        out_shape=[jax.ShapeDtypeStruct(s, t) for s, t in outs],
        scratch_shapes=[pltpu.VMEM(*s) if isinstance(s, tuple) else s for s in scratch],
        cost_estimate=pl.CostEstimate(flops=10**9, bytes_accessed=2 * 10**6, transcendentals=0),
        compiler_params=pltpu.CompilerParams(vmem_limit_bytes=limit * 1024 * 1024),
        **spaces,
    )


def saved(count):
    rows = count * PAD
    return [((rows, D), bf16), ((rows, 3 * D), bf16), ((rows, D), bf16), ((count, 2, PAD, GROUP * PAD), f32)]


def after(value, *others):
    return lax.optimization_barrier((value, *others))[0]


def chain(tok, gain, w_qkv, w_proj, gain_merge, w_merge, g_merged, fetch, up, down):
    tok, g_merged, top, g_top, edge, corner = call(
        border_kernel,
        [
            ((TOKENS, D), bf16), ((PAIRS, 2 * D), bf16),
            ((TOP, D), bf16), ((2 * PAIR_TOP, D), bf16),
            ((EDGE + 2 * PAIR_SIDE, D), bf16), ((TURN + 2 * PAIR_CORNER, D), bf16),
        ],
        [pltpu.SemaphoreType.DMA((2,))],
        [2, 2],
    )(tok, g_merged)
    beside = fetch(top, edge, corner)
    g_lat = up(g_top)
    pair, band = pair_selector(), band_selector()
    shift = shift_selector(WIN_LAT, COLS, SHIFT_LON)
    pair_shift = shift_selector(PAIR_ROWS, PAIR_COLS, SHIFT_LON // 2)
    held = [gain, jnp.asarray(band @ shift, bf16), w_qkv, w_proj, gain_merge]
    held += [jnp.asarray(c, bf16) for c in (shift, band.T, pair, pair.T, pair_shift)]
    got = call(
        inner_kernel,
        [(h.shape, h.dtype) for h in held] + [((TOKENS - TOP, D), bf16)] + saved(LOCAL) + [((INNER, D), bf16)],
        [pltpu.SemaphoreType.DMA((HELD,))],
        [0] + [1] * HELD,
    )(tok, *held)
    gain, pick, w_qkv, w_proj, gain_merge, shift, cells_pick, pair, unpair, pair_shift = got[:HELD]
    cells, xs0, qkv0, mixed0, probs0, att0 = got[HELD:]
    xs1, qkv1, mixed1, probs1, tok, summed, row = call(
        outer_kernel,
        saved(REST) + [((TOKENS, D), bf16), ((TOKENS, D), bf16), ((COLS, D), bf16)],
        [((WIDTH, D), bf16)],
    )(tok, cells, *beside, gain, w_qkv, w_proj, pick, shift, cells_pick, att0)
    behind = down(row)
    cots, w_merge = call(
        cotangent_kernel,
        [((4, PAIRS, D), f32), ((4 * D, 2 * D), bf16)],
        [pltpu.SemaphoreType.DMA],
        [0] * 6 + [1],
    )(after(g_merged, row), g_lat, *beside[1:], gain_merge, pair_shift, w_merge)
    d_summed, row, merge_normed = call(
        pair_kernel,
        [((TOKENS, D), bf16), ((COLS, D), bf16), ((4, PAIRS, D), bf16)],
        [((4, PAIRS, D), f32)],
    )(summed, behind, gain_merge, cots, pair, unpair)
    last = up(row)
    band = jnp.asarray(band_selector(), bf16)
    unshift = jnp.asarray(shift_selector(WIN_LAT, COLS, SHIFT_LON).T, bf16)
    pair_unshift = jnp.asarray(shift_selector(PAIR_ROWS, PAIR_COLS, SHIFT_LON // 2).T, bf16)
    up0, dqkv0, xst, mixt = call(
        inner_back_kernel,
        [((BAND, D), bf16), ((BAND, 3 * D), bf16), ((D, WIDTH), bf16), ((D, WIDTH), bf16)],
        [((BAND, D), bf16)],
    )(d_summed, qkv0, probs0, qkv1, probs1, w_proj, band, xs0, xs1, mixed0, mixed1)
    dqkv, keep, sent = call(
        outer_back_kernel,
        [((WIDTH, 3 * D), bf16), ((4, 32, 32, 128), bf16), ((4, 32, 32, 128), bf16)],
        [((WIDTH, D), bf16), ((BAND, D), bf16)],
    )(d_summed, last, xst, mixt, up0, dqkv0, qkv1, probs1, w_proj, band)
    main, to_lat, to_lon, to_diag = call(
        cells_back_kernel,
        [((TOKENS - TOP, D), bf16), ((TOP, D), bf16), ((EDGE, D), bf16), ((TURN, D), bf16)],
        [((WIDTH, D), bf16)],
    )(dqkv, w_qkv, cells_pick, unshift, tok, d_summed, last, gain)

    def merge(ready):
        m_main, m_lat, lon, diag = call(
            merge_kernel,
            [
                ((PAIRS, 2 * D), bf16), ((2 * PAIR_TOP, D), bf16),
                ((EDGE + 2 * (PAIR_SIDE - PAIR_CORNER), D), bf16), ((TURN + 2 * PAIR_CORNER, D), bf16),
            ],
        )(after(merge_normed, ready), w_merge, pair_unshift, to_lon, to_diag)
        return m_main, down(m_lat), to_lat, lon, diag

    def finish(lat, lon, diag, m_main, m_lat):
        grad_tokens, merged = call(own_cells_kernel, [((TOKENS, D), bf16), ((PAIRS, 2 * D), bf16)])(
            main, lat, lon, diag, m_main, m_lat
        )
        return merged, grad_tokens

    return merge, finish, keep, sent, to_lat


def solution(mesh):
    lats, lons = mesh.shape["lat"], mesh.shape["lon"]
    count = lats * lons

    def send(block, down, right):
        route = [
            (i, (i // lons + down) % lats * lons + (i % lons + right) % lons) for i in range(count)
        ]
        return lax.ppermute(block, ("lat", "lon"), route)

    def fetch(top, edge, corner):
        return send(top, -1, 0), send(edge, 0, -1), send(corner, -1, -1)

    def place(i):
        lat, lon = divmod(i, lons)
        return lat // 8, lat % 8, lon // 8, lon // 2 % 4, lon % 2

    def across(i, step):
        high, z, low, x, core = place(i)
        if core:
            high, low = divmod((high * 2 + low) ^ step, 2)
        else:
            x = x ^ step
        return (high * 8 + z) * lons + low * 8 + x * 2 + core

    rest = {}
    for i in range(count):
        high, z, low, x, core = place(i)
        rest.setdefault((core, high * 2 + low if core else x), []).append(i)
    rest = list(rest.values())

    def swap(block, step):
        return lax.ppermute(block, ("lat", "lon"), [(i, across(i, step)) for i in range(count)])

    def reduce_across(keep, sent, to_lat, merge):
        other = lax.ppermute(sent, ("lat", "lon"), [(i, i ^ 1) for i in range(count)])
        own, *others = call(add_kernel, [((32, 32, 128), bf16)] * 4)(keep, after(other, to_lat))
        got = [swap(block, step) for step, block in enumerate(others, 1)]
        m_main, m_lat, *pieces = merge(own)
        sums = call(join_kernel, [((32, 32, 128), bf16)])(after(own, m_main), *got)[0]
        return sums, m_main, m_lat, pieces

    def reduce_rest(sums):
        parts = lax.all_to_all(sums, ("lat", "lon"), 0, 0, axis_index_groups=rest, tiled=True)
        return call(sum_kernel, [((32, 128), f32)])(parts)[0]

    def body(tokens, gain_attn, w_qkv, w_proj, gain_merge, w_merge, g_merged):
        merge, finish, keep, sent, to_lat = chain(
            tokens.reshape(TOKENS, D), gain_attn.reshape(1, D), w_qkv, w_proj, gain_merge.reshape(4, 1, D),
            w_merge, g_merged.reshape(PAIRS, 2 * D), fetch,
            lambda row: send(row, -1, 0), lambda row: send(row, 1, 0),
        )
        sums, m_main, m_lat, (to_lat, to_lon, to_diag) = reduce_across(keep, sent, to_lat, merge)
        sums = after(sums, m_lat)
        grad_weights = reduce_rest(sums)
        beside = send(to_lat, 1, 0), send(to_lon, 0, 1), send(to_diag, 1, 1)
        merged, grad_tokens = finish(*(after(piece, sums) for piece in beside), m_main, m_lat)
        return (
            merged.reshape(ROWS // 2, COLS // 2, 2 * D),
            grad_tokens.reshape(ROWS, COLS, D),
            grad_weights,
        )

    return jax.shard_map(
        body,
        mesh=mesh,
        in_specs=(P("lat", "lon", None), P(), P(), P(), P(), P(), P("lat", "lon", None)),
        out_specs=(P("lat", "lon", None), P("lat", "lon", None), P("lat", "lon")),
        check_vma=False,
    )
```
